32 devices in a mesh: frames: 8 (over y, x, core), book: 4 (over z).
Axes of the slice: x: 2, y: 2, z: 4, core: 2. Of those that a mesh axis runs over, the one named last changes fastest.
Arguments:
- gate_pre: bfloat16 [2048, 6144], P('frames', 'book'), may hold values from -6 to 6
- up_pre: bfloat16 [2048, 6144], P('frames', 'book'), may hold values from -6 to 6
- down_weight: bfloat16 [6144, 4096], P('book'), may hold values from -0.109375 to 0.109375
- residual: bfloat16 [2048, 4096], P('frames', 'book'), may hold values from -6 to 6
- out_gain: bfloat16 [4096], replicated, may hold values from 0.25 to 1.75
- in_proj: bfloat16 [4, 4096, 1024], P('book', 'frames'), may hold values from -0.09375 to 0.09375
- embedding: bfloat16 [4, 1024, 1024], P('book', 'frames'), may hold values from -6 to 6
- token_ids: int32 [2048, 4], P('frames', 'book'), may hold values from 0 to 1023
- depth_gain: bfloat16 [4, 1024], P('book'), may hold values from 0.25 to 1.75
- qkv_weight: bfloat16 [4, 1024, 1536], P('book', 'frames'), may hold values from -2 to 2
Outputs:
- context: bfloat16 [2048, 4, 512], P(('frames', 'book'))
The draws below stay inside these ranges and needn't reach their ends.
All inputs are finite; a program needn't handle non-finite values.
Results may differ from the reference program's by a relative error of at most 0.019.
Values may be sent and summed in bfloat16 or wider, within the bound.
No kernel may reach another device: no remote copies, remote signals or barrier semaphores. Data moves between devices by JAX's collectives and lax.ppermute only.
A program may use at most 64 MiB of HBM per device.

```python
import math
import jax
import jax.numpy as jnp
from jax import lax

D = 4096
FFW = 6144
DD = 1024
H = 8
HD = 64
V = 1024
FR_DEV = 256
K = 4
FRAMES = 2048
N_FRAMES = 8


def draw_qkv_weight(key, part):
    first_key = jax.random.fold_in(jax.random.fold_in(key, 11), 0)
    width = H * HD
    drawn = jax.random.normal(first_key, (K, DD, 3 * width), jnp.float32) / math.sqrt(DD)
    return jnp.clip(drawn, -2.0, 2.0).astype(jnp.bfloat16)


def with_ends(array, rng, low, high):
    shape = array.shape
    index_at = [jax.random.randint(jax.random.fold_in(rng, axis), (), 0, shape[axis]) for axis in range(len(shape))]
    array = array.at[tuple(index_at)].set(low)
    longest = shape.index(max(shape))
    index_at[longest] = (index_at[longest] + 1) % shape[longest]
    return array.at[tuple(index_at)].set(high)


def with_spikes(result, key, source, target, blocks, factor):
    owner, partner = [(jnp.arange(result.shape[axis_at]) // (result.shape[axis_at] // blocks)).reshape([-1 if axis == axis_at else 1 for axis in range(result.ndim)]) for axis_at in (source, target)]
    chosen = jax.random.permutation(key, blocks)[partner]
    strong = (owner == chosen) | (owner == (partner + blocks // 2) % blocks)
    return jnp.where(strong, factor * result, result)


def level_of(rng, dims, cuts, least, high):
    def one(axis_at, blocks):
        steps = jax.random.uniform(jax.random.fold_in(jax.random.fold_in(rng, 6), axis_at), (blocks,), jnp.float32, least / len(cuts), high / len(cuts))
        return jnp.repeat(jnp.exp(steps), dims[axis_at] // blocks).reshape((-1,) + (1,) * (len(dims) - axis_at - 1))

    loudness = one(*cuts[0])
    for cut in cuts[1:]:
        loudness = loudness * one(*cut)
    return loudness


def centred(own_key, shape, deviation, reach, cuts=(), held_as=jnp.bfloat16):
    level = level_of(own_key, shape, cuts, -0.22, 0.18) if cuts else 1.0
    entries = jax.random.normal(own_key, shape, jnp.float32) * deviation * level
    return jnp.minimum(jnp.maximum(entries, -reach), reach).astype(held_as)


def bell_draw_with(rng, dims, scale, reach, cuts, heavy, held_as=jnp.bfloat16):
    values = scale * jax.random.normal(rng, dims, jnp.float32)
    if cuts:
        values = values * level_of(rng, dims, cuts, -0.22, 0.18)
    return jnp.clip(with_spikes(values, jax.random.fold_in(rng, 3), *heavy), -reach, reach).astype(held_as)


def setup_inputs(seed: int = 0) -> dict:
    splits = jax.random.split(jax.random.key(seed), 11)
    gate_pre = centred(splits[0], (FRAMES, FFW), 1.0, 6.0, ((0, 8), (1, 4)))
    up_pre = centred(splits[1], (FRAMES, FFW), 1.0, 6.0, ((0, 8), (1, 4)))
    down_weight = bell_draw_with(splits[2], (FFW, D), FFW ** -0.5, 0.109375, ((0, 4),), (0, 1, 4, 2.0))
    residual = centred(splits[3], (FRAMES, D), 1.0, 6.0, ((0, 8), (1, 4)))
    out_gain = jnp.clip(1.0 + 0.15 * jax.random.normal(splits[4], (D,), jnp.float32), 0.25, 1.75).astype(jnp.bfloat16)
    in_proj = centred(splits[5], (K, D, DD), D ** -0.5, 0.09375, ((0, 4), (1, 8)))
    embedding = centred(splits[6], (K, V, DD), 1.0, 6.0, ((0, 4), (1, 8)))
    token_ids = with_ends(jax.random.randint(splits[7], (FRAMES, K), 0, V), jax.random.fold_in(splits[7], 1), 0, V - 1).astype(jnp.int32)
    depth_gain = jnp.clip(1.0 + 0.15 * jax.random.normal(splits[8], (K, DD), jnp.float32), 0.25, 1.75).astype(jnp.bfloat16)
    qkv_weight = draw_qkv_weight(jax.random.fold_in(splits[10], 71), 0)
    return {"gate_pre": gate_pre, "up_pre": up_pre, "down_weight": down_weight, "residual": residual, "out_gain": out_gain, "in_proj": in_proj, "embedding": embedding, "token_ids": token_ids, "depth_gain": depth_gain, "qkv_weight": qkv_weight}


def rms_scale(values, gain):
    moment = lax.optimization_barrier(jnp.mean(values * values, axis=-1, keepdims=True))
    return values * lax.rsqrt(moment + 1e-05) * gain

def attend_frames(packed):
    frames_here = packed.shape[0]
    width = H * HD
    queries = packed[:, :, :width].reshape(frames_here, K, H, HD).astype(jnp.float32)
    keys_all = packed[:, :, width:2 * width].reshape(frames_here, K, H, HD).astype(jnp.float32)
    values_all = packed[:, :, 2 * width:].reshape(frames_here, K, H, HD).astype(jnp.float32)
    scores = jnp.einsum('nkhd,njhd->nhkj', queries, keys_all) * HD ** (-0.5)
    causal = jnp.arange(K)[:, None] >= jnp.arange(K)[None, :]
    scores = jnp.where(causal, scores, -1e+30)
    peak = lax.optimization_barrier(jnp.max(scores, axis=-1, keepdims=True))
    expo = jnp.exp(scores - peak)
    probability = lax.optimization_barrier((expo / lax.optimization_barrier(jnp.sum(expo, axis=-1, keepdims=True))).astype(jnp.bfloat16))
    context = jnp.einsum('nhkj,njhd->nkhd', probability.astype(jnp.float32), values_all)
    return context.reshape(frames_here, K, width).astype(jnp.bfloat16)

def reference(gate_pre, up_pre, down_weight, residual, out_gain, in_proj, embedding, token_ids, depth_gain, qkv_weight):
    hidden = (jax.nn.silu(gate_pre.astype(jnp.float32)) * up_pre.astype(jnp.float32)).astype(jnp.bfloat16)
    temporal = (jnp.dot(hidden, down_weight, preferred_element_type=jnp.float32) + residual.astype(jnp.float32)).astype(jnp.bfloat16)
    normed = rms_scale(temporal.astype(jnp.float32), out_gain.astype(jnp.float32)).astype(jnp.bfloat16)

    def per_book(book_index):
        projected = jnp.dot(normed, in_proj[book_index], preferred_element_type=jnp.float32)
        looked = jnp.take(embedding[book_index], token_ids[:, book_index], axis=0).astype(jnp.float32)
        depth_in = (projected + looked).astype(jnp.bfloat16)
        depth_normed = rms_scale(depth_in.astype(jnp.float32), depth_gain[book_index].astype(jnp.float32)).astype(jnp.bfloat16)
        return jnp.dot(depth_normed, qkv_weight[book_index], preferred_element_type=jnp.float32).astype(jnp.bfloat16)
    packed = lax.map(per_book, jnp.arange(K, dtype=jnp.int32))
    packed = jnp.transpose(packed, (1, 0, 2))
    blocks = packed.reshape(N_FRAMES, FR_DEV, K, packed.shape[2])
    context = lax.map(attend_frames, blocks)
    return context.reshape(FRAMES, K, H * HD)
```

```python
import jax
import jax.numpy as jnp
from jax import lax
from jax.sharding import PartitionSpec as P

H = 8
HD = 64
CHUNKS = 2


def attend_block(grouped):
    inner = grouped[0]
    frames_here = inner.shape[0]
    books = inner.shape[1]
    width = H * HD
    queries = inner[:, :, :width].reshape(frames_here, books, H, HD)
    keys_all = inner[:, :, width : 2 * width].reshape(frames_here, books, H, HD)
    values_all = inner[:, :, 2 * width :].reshape(frames_here, books, H, HD)
    scores = jnp.einsum(
        "nkhd,njhd->nhkj", queries, keys_all, preferred_element_type=jnp.float32
    ) * HD ** (-0.5)
    causal = lax.broadcasted_iota(jnp.int32, (books, books), 0) >= lax.broadcasted_iota(
        jnp.int32, (books, books), 1
    )
    scores = jnp.where(causal, scores, -1e30)
    peak = jnp.max(scores, axis=-1, keepdims=True)
    expo = jnp.exp(scores - peak)
    probability = (expo / jnp.sum(expo, axis=-1, keepdims=True)).astype(jnp.bfloat16)
    context = jnp.einsum(
        "nhkj,njhd->nkhd", probability, values_all, preferred_element_type=jnp.float32
    )
    return context.reshape(1, frames_here, books, width).astype(jnp.bfloat16)


def to_right(value, first, last):
    return lax.ppermute(value, "book", [(i, i + 1) for i in range(first, last)])


def to_left(value, first, last):
    return lax.ppermute(value, "book", [(i, i - 1) for i in range(first, last)])


def per_device(
    gate_pre,
    up_pre,
    down_weight,
    residual,
    out_gain,
    in_proj,
    embedding,
    token_ids,
    depth_gain,
    qkv_weight,
):
    f32, bf16 = jnp.float32, jnp.bfloat16
    frames_here = gate_pre.shape[0]
    books = lax.axis_size("book")
    here = lax.axis_index("book")
    width = residual.shape[1]
    rows = frames_here // CHUNKS

    proj_all = lax.all_gather(in_proj[0], "frames", axis=0, tiled=True)
    table = lax.all_gather(embedding[0], "frames", axis=0, tiled=True)
    qkv_all = lax.all_gather(qkv_weight[0], "frames", axis=0, tiled=True)

    def block_of(step):
        return lax.rem(here + step, books) * width

    hidden = (jax.nn.silu(gate_pre.astype(f32)) * up_pre.astype(f32)).astype(bf16)
    sums = {}
    for far in range(1, books):
        for step in (far, books - far):
            if step not in sums:
                block = lax.dynamic_slice_in_dim(down_weight, block_of(step), width, 1)
                sums[step] = jnp.dot(hidden, block, preferred_element_type=f32)
    block = lax.dynamic_slice_in_dim(down_weight, block_of(0), width, 1)
    sums[0] = jnp.dot(hidden, block, preferred_element_type=f32)

    pieces = [slice(c * rows, (c + 1) * rows) for c in range(CHUNKS)]
    right = [None] * CHUNKS
    left = [None] * CHUNKS
    for step in range(1, books):
        for c, piece in enumerate(pieces):
            going = sums[books - step][piece]
            if step > 1:
                going = going + right[c].astype(f32)
            right[c] = to_right(going.astype(bf16), 0, step)
            going = sums[step][piece]
            if step > 1:
                going = going + left[c].astype(f32)
            left[c] = to_left(going.astype(bf16), books - step, books)

    outs = []
    for c, piece in enumerate(pieces):
        own = sums[0][piece] + residual[piece].astype(f32)
        own = (own + right[c].astype(f32) + left[c].astype(f32)).astype(bf16)
        outs.append(own)

    from_left = [[own] for own in outs]
    from_right = [[own] for own in outs]
    for step in range(1, books):
        for c in range(CHUNKS):
            from_left[c].append(to_right(from_left[c][-1], step - 1, books - 1))
            from_right[c].append(to_left(from_right[c][-1], 1, books - step + 1))

    token_column = token_ids[:, 0]
    columns = lax.broadcasted_iota(jnp.int32, (1, table.shape[0]), 1)
    matches = (token_column[:, None] == columns).astype(bf16)
    looked = jnp.dot(matches, table, preferred_element_type=f32)

    gain = out_gain.astype(f32)
    packed = []
    for c, piece in enumerate(pieces):
        square = 0.0
        projected = 0.0
        for step in range(books):
            if step == 0:
                part = outs[c]
            else:
                part = from_right[c][step] + from_left[c][books - step]
            part = part.astype(f32)
            square = square + jnp.sum(part * part, axis=-1, keepdims=True)
            scaled = (part * lax.dynamic_slice_in_dim(gain, block_of(step), width, 0)).astype(bf16)
            block = lax.dynamic_slice_in_dim(proj_all, block_of(step), width, 0)
            projected = projected + jnp.dot(scaled, block, preferred_element_type=f32)
        projected = projected * lax.rsqrt(square / (books * width) + 1e-05)
        depth_in = (projected + looked[piece]).astype(bf16).astype(f32)
        moment = jnp.mean(depth_in * depth_in, axis=-1, keepdims=True)
        depth_normed = depth_in * lax.rsqrt(moment + 1e-05) * depth_gain[0].astype(f32)
        packed.append(
            jnp.dot(depth_normed.astype(bf16), qkv_all, preferred_element_type=f32).astype(bf16)
        )
    packed = jnp.concatenate(packed, axis=0)
    grouped = packed.reshape(books, frames_here // books, 1, packed.shape[1])
    context = attend_block(lax.all_to_all(grouped, "book", split_axis=0, concat_axis=2, tiled=True))
    return context.reshape(context.shape[1], context.shape[2], context.shape[3])


def solution(mesh):
    in_specs = (
        P("frames", "book"),
        P("frames", "book"),
        P("book", None),
        P("frames", "book"),
        P(),
        P("book", "frames", None),
        P("book", "frames", None),
        P("frames", "book"),
        P("book", None),
        P("book", "frames", None),
    )
    out_specs = P(("frames", "book"), None, None)
    return jax.shard_map(
        per_device, mesh=mesh, in_specs=in_specs, out_specs=out_specs, check_vma=False
    )
```

```python
import functools

import jax
import jax.numpy as jnp
from jax import lax
from jax.experimental import pallas as pl
from jax.experimental.pallas import tpu as pltpu
from jax.sharding import PartitionSpec as P

H = 8
HD = 64
f32, bf16 = jnp.float32, jnp.bfloat16


def tail_kernel(books, groups, place_ref, *refs):
    blocks = refs[:books]
    gain_ref, tokens_ref, depth_gain_ref, gathered = refs[books : books + 4]
    outs = refs[books + 4 : 2 * books + 4]
    proj, table, qkv, packed, sems = refs[2 * books + 4 :]
    place = place_ref[0]
    frames_here, width = blocks[0].shape
    depth = proj.shape[1]
    wide = qkv.shape[1]
    proj_rows = proj.shape[0] // groups
    table_rows = table.shape[0] // groups
    qkv_rows = qkv.shape[0] // groups
    per_book = groups // books
    half = qkv_rows // 2
    extra = wide - depth

    table_copies, proj_copies, qkv_copies = [], [], []

    def copy(source, target, into):
        number = len(table_copies) + len(proj_copies) + len(qkv_copies)
        made = pltpu.make_async_copy(source, target, sems.at[number])
        made.start()
        into.append(made)

    at_table = proj_rows
    at_qkv = proj_rows + table_rows
    at_extra = at_qkv + qkv_rows
    for g in range(groups):
        copy(
            gathered.at[g, pl.ds(at_table, table_rows)],
            table.at[pl.ds(g * table_rows, table_rows)],
            table_copies,
        )
    for m in range(books):
        for r in range(per_book):
            g = jnp.bitwise_xor(place, m) * per_book + r
            copy(
                gathered.at[g, pl.ds(0, proj_rows)],
                proj.at[pl.ds(pl.multiple_of(g * proj_rows, proj_rows), proj_rows)],
                proj_copies,
            )
    for g in range(groups):
        copy(
            gathered.at[g, pl.ds(at_qkv, qkv_rows)],
            qkv.at[pl.ds(g * qkv_rows, qkv_rows), pl.ds(0, depth)],
            qkv_copies,
        )
        for side in range(2):
            copy(
                gathered.at[g, pl.ds(at_extra, half), pl.ds(side * extra, extra)],
                qkv.at[pl.ds(g * qkv_rows + side * half, half), pl.ds(depth, extra)],
                qkv_copies,
            )

    columns = lax.broadcasted_iota(jnp.int32, (frames_here, table.shape[0]), 1)
    matches = (tokens_ref[...] == columns).astype(f32).astype(bf16)
    for made in table_copies:
        made.wait()
    looked = jnp.dot(matches, table[...], preferred_element_type=f32)

    square = jnp.zeros((frames_here, 1), f32)
    projected = jnp.zeros((frames_here, depth), f32)
    for m in range(books):
        start = pl.multiple_of(jnp.bitwise_xor(place, m) * width, width)
        part = blocks[m][...].astype(f32)
        square = square + jnp.sum(part * part, axis=-1, keepdims=True)
        scaled = (part * gain_ref[:, pl.ds(start, width)]).astype(bf16)
        for made in proj_copies[m * per_book : (m + 1) * per_book]:
            made.wait()
        projected = projected + jnp.dot(
            scaled, proj[pl.ds(start, width), :], preferred_element_type=f32
        )
    projected = projected * lax.rsqrt(square / (books * width) + 1e-05)
    depth_in = (projected + looked).astype(bf16).astype(f32)
    moment = jnp.mean(depth_in * depth_in, axis=-1, keepdims=True)
    depth_normed = (depth_in * lax.rsqrt(moment + 1e-05) * depth_gain_ref[...]).astype(bf16)
    for made in qkv_copies:
        made.wait()
    packed[...] = jnp.dot(depth_normed, qkv[...], preferred_element_type=f32).astype(bf16)
    rows = frames_here // books
    for m in range(books):
        start = pl.multiple_of(jnp.bitwise_xor(place, m) * rows, rows)
        outs[m][...] = packed[pl.ds(start, rows), :]


def tail(place, blocks, gain, tokens, depth_gain, gathered, sizes):
    books = len(blocks)
    groups = gathered.shape[0]
    features, codes, depth, wide = sizes
    frames_here = blocks[0].shape[0]
    vmem = pl.BlockSpec(memory_space=pltpu.VMEM)
    flops = 2 * frames_here * depth * (features + codes + wide)
    return pl.pallas_call(
        functools.partial(tail_kernel, books, groups),
        out_shape=[jax.ShapeDtypeStruct((frames_here // books, wide), bf16)] * books,
        in_specs=[pl.BlockSpec(memory_space=pltpu.SMEM)]
        + [vmem] * (books + 3)
        + [pl.BlockSpec(memory_space=pl.ANY)],
        out_specs=[vmem] * books,
        scratch_shapes=[
            pltpu.VMEM((features, depth), bf16),
            pltpu.VMEM((codes, depth), bf16),
            pltpu.VMEM((depth, wide), bf16),
            pltpu.VMEM((frames_here, wide), bf16),
            pltpu.SemaphoreType.DMA((5 * groups,)),
        ],
        compiler_params=pltpu.CompilerParams(vmem_limit_bytes=40 * 2**20),
        cost_estimate=pl.CostEstimate(
            flops=flops, bytes_accessed=gathered.size * 2, transcendentals=0
        ),
        name="project_lookup_qkv",
    )(place, *blocks, gain, tokens, depth_gain, gathered)


def attend_kernel(books, place_ref, *refs):
    arrived = refs[:books]
    out_ref, inner = refs[books:]
    place = place_ref[0]
    rows, wide = arrived[0].shape
    width = wide // 3
    for m in range(books):
        inner[jnp.bitwise_xor(place, m)] = arrived[m][...]
    head_of_row = lax.broadcasted_iota(jnp.int32, (width, width), 0) // HD
    head_of_column = lax.broadcasted_iota(jnp.int32, (width, width), 1) // HD
    same_head = (head_of_row == head_of_column).astype(f32).astype(bf16)
    keys_all = [inner[j, :, width : 2 * width].astype(f32) for j in range(books)]
    values_all = [inner[j, :, 2 * width :].astype(f32) for j in range(books)]
    contexts = []
    for k in range(books):
        query = inner[k, :, :width].astype(f32) * HD ** (-0.5)
        products = jnp.concatenate([query * keys_all[j] for j in range(k + 1)], axis=0)
        high = products.astype(bf16)
        low = (products - high.astype(f32)).astype(bf16)
        scores = jnp.dot(high, same_head, preferred_element_type=f32) + jnp.dot(
            low, same_head, preferred_element_type=f32
        )
        scores = [scores[j * rows : (j + 1) * rows] for j in range(k + 1)]
        peak = functools.reduce(jnp.maximum, scores)
        expo = [jnp.exp(score - peak) for score in scores]
        total = functools.reduce(jnp.add, expo)
        context = 0.0
        for j in range(k + 1):
            probability = (expo[j] / total).astype(bf16).astype(f32)
            context = context + probability * values_all[j]
        contexts.append(context)
    out_ref[...] = jnp.stack(contexts, axis=1).astype(bf16)


def attend(place, arrived):
    books = len(arrived)
    rows, wide = arrived[0].shape
    vmem = pl.BlockSpec(memory_space=pltpu.VMEM)
    return pl.pallas_call(
        functools.partial(attend_kernel, books),
        out_shape=jax.ShapeDtypeStruct((rows, books, wide // 3), bf16),
        in_specs=[pl.BlockSpec(memory_space=pltpu.SMEM)] + [vmem] * books,
        out_specs=vmem,
        scratch_shapes=[pltpu.VMEM((books, rows, wide), bf16)],
        compiler_params=pltpu.CompilerParams(vmem_limit_bytes=32 * 2**20),
        name="attend_books",
    )(place, *arrived)


def swap(value, distance):
    books = lax.axis_size("book")
    return lax.ppermute(value, "book", [(i, i ^ distance) for i in range(books)])


def per_device(
    gate_pre,
    up_pre,
    down_weight,
    residual,
    out_gain,
    in_proj,
    embedding,
    token_ids,
    depth_gain,
    qkv_weight,
):
    books = lax.axis_size("book")
    groups = lax.axis_size("frames")
    here = lax.axis_index("book").astype(jnp.int32)
    place = here[None]
    width = residual.shape[1]
    depth = in_proj.shape[2]
    wide = qkv_weight.shape[2]
    half = qkv_weight.shape[1] // 2

    beyond = qkv_weight[0, :, depth:]
    weights = jnp.concatenate(
        [
            in_proj[0],
            embedding[0],
            qkv_weight[0, :, :depth],
            jnp.concatenate([beyond[:half], beyond[half:]], axis=1),
        ],
        axis=0,
    )
    gathered = lax.all_gather(weights, "frames", axis=0)

    hidden = (jax.nn.silu(gate_pre.astype(f32)) * up_pre.astype(f32)).astype(bf16)

    def share(m):
        start = jnp.bitwise_xor(here, m) * width
        block = lax.dynamic_slice_in_dim(down_weight, start, width, 1)
        return jnp.dot(hidden, block, preferred_element_type=f32)

    sums = {books - 1: share(books - 1)}
    for m in range(books - 2, -1, -1):
        sums[m] = lax.optimization_barrier(share(m))
    sums[0] = sums[0] + residual.astype(f32)
    distance = 1
    while distance < books:
        for m in range(books - distance, 0, -2 * distance):
            came = swap(sums.pop(m).astype(bf16), distance)
            sums[m ^ distance] = sums[m ^ distance] + came.astype(f32)
        distance *= 2

    blocks = {0: sums[0].astype(bf16)}
    distance = books // 2
    while distance:
        for m in sorted(blocks):
            blocks[m ^ distance] = swap(blocks[m], distance)
        distance //= 2

    packed = tail(
        place,
        [blocks[m] for m in range(books)],
        out_gain.astype(f32)[None],
        token_ids,
        depth_gain.astype(f32),
        gathered,
        (books * width, groups * embedding.shape[1], depth, wide),
    )
    arrived = [packed[0]]
    far = {m: swap(packed[m], m) for m in range(books - 1, 0, -1)}
    arrived += [far[m] for m in range(1, books)]
    return attend(place, arrived)


def solution(mesh):
    in_specs = (
        P("frames", "book"),
        P("frames", "book"),
        P("book", None),
        P("frames", "book"),
        P(),
        P("book", "frames", None),
        P("book", "frames", None),
        P("frames", "book"),
        P("book", None),
        P("book", "frames", None),
    )
    out_specs = P(("frames", "book"), None, None)
    return jax.shard_map(
        per_device, mesh=mesh, in_specs=in_specs, out_specs=out_specs, check_vma=False
    )
```

```python
import functools

import jax
import jax.numpy as jnp
from jax import lax
from jax.experimental import pallas as pl
from jax.experimental.pallas import tpu as pltpu
from jax.sharding import PartitionSpec as P

H = 8
HD = 64
f32, bf16 = jnp.float32, jnp.bfloat16


def assemble_kernel(groups, sizes, place_ref, tokens_ref, *refs):
    parts = refs[:groups]
    looked_ref, qkv_ref, table, sems = refs[groups:]
    table_rows, qkv_rows = sizes
    half = qkv_rows // 2
    depth = table.shape[1]
    extra = qkv_ref.shape[1] - depth
    place = place_ref[0]
    table_copies, qkv_copies = [], []

    def copy(source, target, number, into):
        made = pltpu.make_async_copy(source, target, sems.at[number])
        made.start()
        into.append(made)

    for n in range(groups):
        g = jnp.bitwise_xor(place, n)
        start = pl.multiple_of(g * table_rows, table_rows)
        copy(
            parts[n].at[pl.ds(0, table_rows)], table.at[pl.ds(start, table_rows)], 4 * n, table_copies
        )
    for n in range(groups):
        g = jnp.bitwise_xor(place, n)
        start = pl.multiple_of(g * qkv_rows, qkv_rows)
        copy(
            parts[n].at[pl.ds(table_rows, qkv_rows)],
            qkv_ref.at[pl.ds(start, qkv_rows), pl.ds(0, depth)],
            4 * n + 1,
            qkv_copies,
        )
        for side in range(2):
            start = pl.multiple_of(g * qkv_rows + side * half, half)
            copy(
                parts[n].at[pl.ds(table_rows + qkv_rows, half), pl.ds(side * extra, extra)],
                qkv_ref.at[pl.ds(start, half), pl.ds(depth, extra)],
                4 * n + 2 + side,
                qkv_copies,
            )
    columns = lax.broadcasted_iota(jnp.int32, (tokens_ref.shape[0], table.shape[0]), 1)
    matches = (tokens_ref[...] == columns).astype(f32).astype(bf16)
    for made in table_copies:
        made.wait()
    looked_ref[...] = jnp.dot(matches, table[...], preferred_element_type=f32).astype(bf16)
    for made in qkv_copies:
        made.wait()


def assemble(place, tokens, parts, table_rows, qkv_rows, wide):
    groups = len(parts)
    frames_here = tokens.shape[0]
    depth = parts[0].shape[1]
    vmem = pl.BlockSpec(memory_space=pltpu.VMEM)
    return pl.pallas_call(
        functools.partial(assemble_kernel, groups, (table_rows, qkv_rows)),
        out_shape=[
            jax.ShapeDtypeStruct((frames_here, depth), bf16),
            jax.ShapeDtypeStruct((groups * qkv_rows, wide), bf16),
        ],
        in_specs=[pl.BlockSpec(memory_space=pltpu.SMEM), vmem]
        + [pl.BlockSpec(memory_space=pl.ANY)] * groups,
        out_specs=[vmem] * 2,
        scratch_shapes=[
            pltpu.VMEM((groups * table_rows, depth), bf16),
            pltpu.SemaphoreType.DMA((4 * groups,)),
        ],
        compiler_params=pltpu.CompilerParams(vmem_limit_bytes=24 * 2**20),
        cost_estimate=pl.CostEstimate(
            flops=2 * frames_here * groups * table_rows * depth,
            bytes_accessed=2 * groups * parts[0].size,
            transcendentals=0,
        ),
        name="lookup_and_qkv_rows",
    )(place, tokens, *parts)


def early_kernel(early, late, place_ref, gain_ref, *refs):
    count = len(early)
    blocks = dict(zip(early, refs[:count]))
    proj, projected_ref, square_ref, later, held, sems = refs[count:]
    place = place_ref[0]
    frames_here, width = refs[0].shape
    depth = proj.shape[1]

    def rows_of(m):
        return pl.ds(pl.multiple_of(jnp.bitwise_xor(place, m) * width, width), width)

    copies = []
    for number, m in enumerate(early):
        made = pltpu.make_async_copy(proj.at[rows_of(m)], held.at[number], sems.at[number])
        made.start()
        copies.append(made)
    for number, m in enumerate(late):
        made = pltpu.make_async_copy(
            proj.at[rows_of(m)], later.at[number], sems.at[count + number]
        )
        made.start()
        copies.append(made)
    square = jnp.zeros((frames_here, 1), f32)
    projected = jnp.zeros((frames_here, depth), f32)
    for number, m in enumerate(early):
        part = blocks[m][...].astype(f32)
        square = square + jnp.sum(part * part, axis=-1, keepdims=True)
        scaled = (part * gain_ref[:, rows_of(m)]).astype(bf16)
        copies[number].wait()
        projected = projected + jnp.dot(scaled, held[number], preferred_element_type=f32)
    projected_ref[...] = projected
    square_ref[...] = square
    for made in copies[count:]:
        made.wait()


def project_early(place, gain, blocks, early, late, proj):
    frames_here, width = blocks[0].shape
    depth = proj.shape[1]
    vmem = pl.BlockSpec(memory_space=pltpu.VMEM)
    return pl.pallas_call(
        functools.partial(early_kernel, early, late),
        out_shape=[
            jax.ShapeDtypeStruct((frames_here, depth), f32),
            jax.ShapeDtypeStruct((frames_here, 1), f32),
            jax.ShapeDtypeStruct((len(late), width, depth), bf16),
        ],
        in_specs=[pl.BlockSpec(memory_space=pltpu.SMEM), vmem]
        + [vmem] * len(early)
        + [pl.BlockSpec(memory_space=pltpu.HBM)],
        out_specs=[vmem] * 3,
        scratch_shapes=[
            pltpu.VMEM((len(early), width, depth), bf16),
            pltpu.SemaphoreType.DMA((len(early) + len(late),)),
        ],
        compiler_params=pltpu.CompilerParams(vmem_limit_bytes=42 * 2**20),
        cost_estimate=pl.CostEstimate(
            flops=2 * frames_here * depth * width * len(early),
            bytes_accessed=2 * proj.size,
            transcendentals=0,
        ),
        name="project_early_blocks",
    )(place, gain, *[blocks[m] for m in early], proj)


def late_kernel(books, late, place_ref, *refs):
    count = len(late)
    blocks = refs[:count]
    later, projected_ref, square_ref, looked_ref, gain_ref, depth_gain_ref, qkv_ref = refs[
        count : count + 7
    ]
    outs = refs[count + 7 : count + 7 + books]
    packed = refs[count + 7 + books]
    place = place_ref[0]
    frames_here, width = blocks[0].shape
    square = square_ref[...]
    projected = projected_ref[...]
    for number, m in enumerate(late):
        start = pl.multiple_of(jnp.bitwise_xor(place, m) * width, width)
        part = blocks[number][...].astype(f32)
        square = square + jnp.sum(part * part, axis=-1, keepdims=True)
        scaled = (part * gain_ref[:, pl.ds(start, width)]).astype(bf16)
        projected = projected + jnp.dot(scaled, later[number], preferred_element_type=f32)
    projected = projected * lax.rsqrt(square / (books * width) + 1e-05)
    depth_in = (projected + looked_ref[...].astype(f32)).astype(bf16).astype(f32)
    moment = jnp.mean(depth_in * depth_in, axis=-1, keepdims=True)
    depth_normed = (depth_in * lax.rsqrt(moment + 1e-05) * depth_gain_ref[...]).astype(bf16)
    packed[...] = jnp.dot(depth_normed, qkv_ref[...], preferred_element_type=f32).astype(bf16)
    rows = frames_here // books
    for m in range(books):
        start = pl.multiple_of(jnp.bitwise_xor(place, m) * rows, rows)
        outs[m][...] = packed[pl.ds(start, rows), :]


def project_late(place, blocks, late, later, projected, square, looked, gain, depth_gain, qkv):
    books = len(blocks)
    frames_here, width = blocks[0].shape
    depth, wide = qkv.shape
    vmem = pl.BlockSpec(memory_space=pltpu.VMEM)
    return pl.pallas_call(
        functools.partial(late_kernel, books, late),
        out_shape=[jax.ShapeDtypeStruct((frames_here // books, wide), bf16)] * books,
        in_specs=[pl.BlockSpec(memory_space=pltpu.SMEM)] + [vmem] * (len(late) + 7),
        out_specs=[vmem] * books,
        scratch_shapes=[pltpu.VMEM((frames_here, wide), bf16)],
        compiler_params=pltpu.CompilerParams(vmem_limit_bytes=32 * 2**20),
        cost_estimate=pl.CostEstimate(
            flops=2 * frames_here * depth * (width * len(late) + wide),
            bytes_accessed=2 * qkv.size,
            transcendentals=0,
        ),
        name="project_late_blocks_and_qkv",
    )(
        place,
        *[blocks[m] for m in late],
        later,
        projected,
        square,
        looked,
        gain,
        depth_gain,
        qkv,
    )


def attend_kernel(books, place_ref, *refs):
    arrived = refs[:books]
    out_ref, inner = refs[books:]
    place = place_ref[0]
    rows, wide = arrived[0].shape
    width = wide // 3
    for m in range(books):
        inner[jnp.bitwise_xor(place, m)] = arrived[m][...]
    head_of_row = lax.broadcasted_iota(jnp.int32, (width, width), 0) // HD
    head_of_column = lax.broadcasted_iota(jnp.int32, (width, width), 1) // HD
    same_head = (head_of_row == head_of_column).astype(f32).astype(bf16)
    keys_all = [inner[j, :, width : 2 * width].astype(f32) for j in range(books)]
    values_all = [inner[j, :, 2 * width :].astype(f32) for j in range(books)]
    contexts = []
    for k in range(books):
        query = inner[k, :, :width].astype(f32) * HD ** (-0.5)
        products = jnp.concatenate([query * keys_all[j] for j in range(k + 1)], axis=0)
        high = products.astype(bf16)
        low = (products - high.astype(f32)).astype(bf16)
        scores = jnp.dot(high, same_head, preferred_element_type=f32) + jnp.dot(
            low, same_head, preferred_element_type=f32
        )
        scores = [scores[j * rows : (j + 1) * rows] for j in range(k + 1)]
        peak = functools.reduce(jnp.maximum, scores)
        expo = [jnp.exp(score - peak) for score in scores]
        total = functools.reduce(jnp.add, expo)
        context = 0.0
        for j in range(k + 1):
            probability = (expo[j] / total).astype(bf16).astype(f32)
            context = context + probability * values_all[j]
        contexts.append(context)
    out_ref[...] = jnp.stack(contexts, axis=1).astype(bf16)


def attend(place, arrived):
    books = len(arrived)
    rows, wide = arrived[0].shape
    vmem = pl.BlockSpec(memory_space=pltpu.VMEM)
    return pl.pallas_call(
        functools.partial(attend_kernel, books),
        out_shape=jax.ShapeDtypeStruct((rows, books, wide // 3), bf16),
        in_specs=[pl.BlockSpec(memory_space=pltpu.SMEM)] + [vmem] * books,
        out_specs=vmem,
        scratch_shapes=[pltpu.VMEM((books, rows, wide), bf16)],
        compiler_params=pltpu.CompilerParams(vmem_limit_bytes=32 * 2**20),
        name="attend_books",
    )(place, *arrived)


def swap(value, axis, distance):
    return lax.ppermute(value, axis, [(i, i ^ distance) for i in range(lax.axis_size(axis))])


def after(value, *others):
    return lax.optimization_barrier((value, *others))[0]


def per_device(
    gate_pre,
    up_pre,
    down_weight,
    residual,
    out_gain,
    in_proj,
    embedding,
    token_ids,
    depth_gain,
    qkv_weight,
):
    books = lax.axis_size("book")
    groups = lax.axis_size("frames")
    here = lax.axis_index("book").astype(jnp.int32)
    place = here[None]
    width = residual.shape[1]
    depth = in_proj.shape[2]
    wide = qkv_weight.shape[2]
    table_rows = embedding.shape[1]
    qkv_rows = qkv_weight.shape[1]
    gain = out_gain.astype(f32)[None]

    proj = lax.all_gather(in_proj[0], "frames", axis=0, tiled=True)

    hidden = (jax.nn.silu(gate_pre.astype(f32)) * up_pre.astype(f32)).astype(bf16)

    def share(m, *others):
        start = jnp.bitwise_xor(here, m) * width
        block = lax.dynamic_slice_in_dim(down_weight, start, width, 1)
        factor = after(hidden, *others) if others else hidden
        return jnp.dot(factor, block, preferred_element_type=f32)

    sums = {books - 1: share(books - 1)}
    first = sums[books - 1].astype(bf16)

    table_mine, qkv_mine = after((embedding[0], qkv_weight[0]), first)
    beyond = qkv_mine[:, depth:]
    rows = jnp.concatenate(
        [
            table_mine,
            qkv_mine[:, :depth],
            jnp.concatenate([beyond[: qkv_rows // 2], beyond[qkv_rows // 2 :]], axis=1),
        ],
        axis=0,
    )
    parts = {0: rows}
    for n in range(2, groups, 2):
        parts[n] = swap(rows, "frames", n)

    sums[books - 2] = lax.optimization_barrier(share(books - 2, rows))
    distance = 1
    while distance < books:
        came = None
        for m in range(books - distance, 0, -2 * distance):
            going = sums.pop(m).astype(bf16)
            if came is not None:
                going = after(going, came)
            came = swap(going, "book", distance)
            if m == books - 1:
                for n in range(books - 3, -1, -1):
                    sums[n] = lax.optimization_barrier(share(n, came))
                sums[0] = sums[0] + residual.astype(f32)
            sums[m ^ distance] = sums[m ^ distance] + came.astype(f32)
        distance *= 2

    blocks = {0: sums[0].astype(bf16)}
    distance = books // 2
    while distance:
        for m in sorted(blocks):
            going = blocks[m] if m == 0 else after(blocks[m], blocks[distance])
            blocks[m ^ distance] = swap(going, "book", distance)
        distance //= 2

    for n in range(0, groups, 2):
        parts[n + 1] = swap(after(parts[n], blocks[0]), "frames", 1)
    looked, qkv = assemble(
        lax.axis_index("frames").astype(jnp.int32)[None],
        token_ids,
        [parts[n] for n in range(groups)],
        table_rows,
        qkv_rows,
        wide,
    )

    early = [m for m in range(books) if m % 2 == 0 or m == 1]
    late = [m for m in range(books) if m not in early]
    projected, square, later = project_early(place, gain, blocks, early, late, proj)
    packed = project_late(
        place,
        blocks,
        late,
        later,
        projected,
        square,
        looked,
        gain,
        depth_gain.astype(f32),
        qkv,
    )
    far = {m: swap(packed[m], "book", m) for m in range(books - 1, 0, -1)}
    return attend(place, [packed[0]] + [far[m] for m in range(1, books)])


def solution(mesh):
    in_specs = (
        P("frames", "book"),
        P("frames", "book"),
        P("book", None),
        P("frames", "book"),
        P(),
        P("book", "frames", None),
        P("book", "frames", None),
        P("frames", "book"),
        P("book", None),
        P("book", "frames", None),
    )
    out_specs = P(("frames", "book"), None, None)
    return jax.shard_map(
        per_device, mesh=mesh, in_specs=in_specs, out_specs=out_specs, check_vma=False
    )
```

```python
import functools

import jax
import jax.numpy as jnp
from jax import lax
from jax.experimental import pallas as pl
from jax.experimental.pallas import tpu as pltpu
from jax.sharding import PartitionSpec as P

H = 8
HD = 64
f32, bf16 = jnp.float32, jnp.bfloat16


def pack_kernel(proj_ref, table_ref, qkv_ref, packed_ref, sems):
    proj_rows, depth = proj_ref.shape
    table_rows = table_ref.shape[0]
    qkv_rows, wide = qkv_ref.shape
    half, extra = qkv_rows // 2, wide - depth
    at_qkv = proj_rows + table_rows
    at_extra = at_qkv + qkv_rows
    moves = [
        (proj_ref, packed_ref.at[pl.ds(0, proj_rows)]),
        (table_ref, packed_ref.at[pl.ds(proj_rows, table_rows)]),
        (qkv_ref.at[:, pl.ds(0, depth)], packed_ref.at[pl.ds(at_qkv, qkv_rows)]),
    ]
    for side in range(2):
        moves.append(
            (
                qkv_ref.at[pl.ds(side * half, half), pl.ds(depth, extra)],
                packed_ref.at[pl.ds(at_extra, half), pl.ds(side * extra, extra)],
            )
        )
    copies = [
        pltpu.make_async_copy(source, target, sems.at[number])
        for number, (source, target) in enumerate(moves)
    ]
    for made in copies:
        made.start()
    for made in copies:
        made.wait()


def pack(proj, table, qkv):
    depth = proj.shape[1]
    rows = proj.shape[0] + table.shape[0] + qkv.shape[0] + qkv.shape[0] // 2
    return pl.pallas_call(
        pack_kernel,
        out_shape=jax.ShapeDtypeStruct((rows, depth), bf16),
        in_specs=[pl.BlockSpec(memory_space=pl.ANY)] * 3,
        out_specs=pl.BlockSpec(memory_space=pltpu.VMEM),
        scratch_shapes=[pltpu.SemaphoreType.DMA((5,))],
        compiler_params=pltpu.CompilerParams(vmem_limit_bytes=4 * 2**20),
        name="pack_weight_rows",
    )(proj, table, qkv)


def assemble_kernel(groups, sizes, place_ref, tokens_ref, *refs):
    parts = refs[:groups]
    looked_ref, qkv_ref, table, sems = refs[groups:]
    table_rows, qkv_rows, firsts = sizes
    half = qkv_rows // 2
    depth = table.shape[1]
    extra = qkv_ref.shape[1] - depth
    place = place_ref[1]
    table_copies, qkv_copies = [], []

    def copy(source, target, number, into):
        made = pltpu.make_async_copy(source, target, sems.at[number])
        made.start()
        into.append(made)

    for n in range(groups):
        g = jnp.bitwise_xor(place, n)
        start = pl.multiple_of(g * table_rows, table_rows)
        copy(
            parts[n].at[pl.ds(firsts[n], table_rows)],
            table.at[pl.ds(start, table_rows)],
            4 * n,
            table_copies,
        )
    for n in range(groups):
        g = jnp.bitwise_xor(place, n)
        at_qkv = firsts[n] + table_rows
        start = pl.multiple_of(g * qkv_rows, qkv_rows)
        copy(
            parts[n].at[pl.ds(at_qkv, qkv_rows)],
            qkv_ref.at[pl.ds(start, qkv_rows), pl.ds(0, depth)],
            4 * n + 1,
            qkv_copies,
        )
        for side in range(2):
            start = pl.multiple_of(g * qkv_rows + side * half, half)
            copy(
                parts[n].at[pl.ds(at_qkv + qkv_rows, half), pl.ds(side * extra, extra)],
                qkv_ref.at[pl.ds(start, half), pl.ds(depth, extra)],
                4 * n + 2 + side,
                qkv_copies,
            )
    columns = lax.broadcasted_iota(jnp.int32, (tokens_ref.shape[0], table.shape[0]), 1)
    matches = (tokens_ref[...] == columns).astype(f32).astype(bf16)
    for made in table_copies:
        made.wait()
    looked_ref[...] = jnp.dot(matches, table[...], preferred_element_type=f32).astype(bf16)
    for made in qkv_copies:
        made.wait()


def assemble(place, tokens, parts, firsts, table_rows, qkv_rows, wide):
    groups = len(parts)
    frames_here = tokens.shape[0]
    depth = parts[0].shape[1]
    vmem = pl.BlockSpec(memory_space=pltpu.VMEM)
    return pl.pallas_call(
        functools.partial(assemble_kernel, groups, (table_rows, qkv_rows, firsts)),
        out_shape=[
            jax.ShapeDtypeStruct((frames_here, depth), bf16),
            jax.ShapeDtypeStruct((groups * qkv_rows, wide), bf16),
        ],
        in_specs=[pl.BlockSpec(memory_space=pltpu.SMEM)] + [vmem] * (1 + groups),
        out_specs=[vmem] * 2,
        scratch_shapes=[
            pltpu.VMEM((groups * table_rows, depth), bf16),
            pltpu.SemaphoreType.DMA((4 * groups,)),
        ],
        compiler_params=pltpu.CompilerParams(vmem_limit_bytes=24 * 2**20),
        name="lookup_and_qkv_rows",
    )(place, tokens, *parts)


def is_late(m):
    return (m % 2 == 1) & (m != 1)


def add_products(late, books, pieces, where, refs, held, projected_ref):
    here, group = where
    rows_each = held.shape[2] * books // (1 + max(n for n, _, _ in pieces))
    per_book = held.shape[2] // rows_each
    for (n, row, count), ref in zip(pieces, refs):
        owner = jnp.bitwise_xor(group, n)
        book = owner // per_book
        start = (owner % per_book) * rows_each + row

        @pl.when(is_late(jnp.bitwise_xor(here, book)) == late)
        def _():
            columns = pl.ds(pl.multiple_of(start, 128), count)
            projected_ref[...] += jnp.dot(
                held[book, :, columns], ref[:count, :], preferred_element_type=f32
            )


def hold_blocks(blocks, here, gain_ref, held):
    square = 0.0
    for m, ref in blocks.items():
        book = jnp.bitwise_xor(here, m)
        part = ref[...].astype(f32)
        square = square + jnp.sum(part * part, axis=-1, keepdims=True)
        width = part.shape[1]
        columns = pl.ds(pl.multiple_of(book * width, width), width)
        held[book] = (part * gain_ref[:, columns]).astype(bf16)
    return square


def early_kernel(books, early, pieces, place_ref, gain_ref, *refs):
    blocks = dict(zip(early, refs))
    proj = refs[len(early) : len(early) + len(pieces)]
    projected_ref, square_ref, held = refs[len(early) + len(pieces) :]
    where = place_ref[0], place_ref[1]
    square_ref[...] = hold_blocks(blocks, where[0], gain_ref, held)
    projected_ref[...] = jnp.zeros_like(projected_ref)
    add_products(False, books, pieces, where, proj, held, projected_ref)


def project_early(place, gain, blocks, early, pieces, proj):
    books = len(blocks)
    frames_here, width = blocks[0].shape
    depth = proj[0].shape[1]
    vmem = pl.BlockSpec(memory_space=pltpu.VMEM)
    return pl.pallas_call(
        functools.partial(early_kernel, books, early, pieces),
        out_shape=[
            jax.ShapeDtypeStruct((frames_here, depth), f32),
            jax.ShapeDtypeStruct((frames_here, 1), f32),
        ],
        in_specs=[pl.BlockSpec(memory_space=pltpu.SMEM)]
        + [vmem] * (1 + len(early) + len(pieces)),
        out_specs=[vmem] * 2,
        scratch_shapes=[pltpu.VMEM((books, frames_here, width), bf16)],
        compiler_params=pltpu.CompilerParams(vmem_limit_bytes=24 * 2**20),
        name="project_early_blocks",
    )(place, gain, *[blocks[m] for m in early], *proj)


def late_kernel(books, late, pieces, place_ref, gain_ref, *refs):
    blocks = dict(zip(late, refs))
    refs = refs[len(late) :]
    proj = refs[: len(pieces)]
    early_ref, square_ref, looked_ref, depth_gain_ref, qkv_ref = refs[
        len(pieces) : len(pieces) + 5
    ]
    refs = refs[len(pieces) + 5 :]
    outs = refs[:books]
    held, projected_ref, packed = refs[books:]
    where = place_ref[0], place_ref[1]
    frames_here, width = held.shape[1:]
    square = square_ref[...] + hold_blocks(blocks, where[0], gain_ref, held)
    projected_ref[...] = early_ref[...]
    add_products(True, books, pieces, where, proj, held, projected_ref)
    projected = projected_ref[...] * lax.rsqrt(square / (books * width) + 1e-05)
    depth_in = (projected + looked_ref[...].astype(f32)).astype(bf16).astype(f32)
    moment = jnp.mean(depth_in * depth_in, axis=-1, keepdims=True)
    depth_normed = (depth_in * lax.rsqrt(moment + 1e-05) * depth_gain_ref[...]).astype(bf16)
    packed[...] = jnp.dot(depth_normed, qkv_ref[...], preferred_element_type=f32).astype(bf16)
    rows = frames_here // books
    for m in range(books):
        start = pl.multiple_of(jnp.bitwise_xor(where[0], m) * rows, rows)
        outs[m][...] = packed[pl.ds(start, rows), :]


def project_late(
    place, gain, blocks, late, pieces, proj, projected, square, looked, depth_gain, qkv
):
    books = len(blocks)
    frames_here, width = blocks[0].shape
    depth, wide = qkv.shape
    vmem = pl.BlockSpec(memory_space=pltpu.VMEM)
    return pl.pallas_call(
        functools.partial(late_kernel, books, late, pieces),
        out_shape=[jax.ShapeDtypeStruct((frames_here // books, wide), bf16)] * books,
        in_specs=[pl.BlockSpec(memory_space=pltpu.SMEM)]
        + [vmem] * (1 + len(late) + len(pieces) + 5),
        out_specs=[vmem] * books,
        scratch_shapes=[
            pltpu.VMEM((books, frames_here, width), bf16),
            pltpu.VMEM((frames_here, depth), f32),
            pltpu.VMEM((frames_here, wide), bf16),
        ],
        compiler_params=pltpu.CompilerParams(vmem_limit_bytes=28 * 2**20),
        name="project_late_blocks_and_qkv",
    )(
        place,
        gain,
        *[blocks[m] for m in late],
        *proj,
        projected,
        square,
        looked,
        depth_gain,
        qkv,
    )


def attend_kernel(books, place_ref, *refs):
    arrived = refs[:books]
    out_ref, inner = refs[books:]
    place = place_ref[0]
    rows, wide = arrived[0].shape
    width = wide // 3
    for m in range(books):
        inner[jnp.bitwise_xor(place, m)] = arrived[m][...]
    head_of_row = lax.broadcasted_iota(jnp.int32, (width, width), 0) // HD
    head_of_column = lax.broadcasted_iota(jnp.int32, (width, width), 1) // HD
    same_head = (head_of_row == head_of_column).astype(f32).astype(bf16)
    keys_all = [inner[j, :, width : 2 * width].astype(f32) for j in range(books)]
    values_all = [inner[j, :, 2 * width :].astype(f32) for j in range(books)]
    contexts = []
    for k in range(books):
        query = inner[k, :, :width].astype(f32) * HD ** (-0.5)
        products = jnp.concatenate([query * keys_all[j] for j in range(k + 1)], axis=0)
        high = products.astype(bf16)
        low = (products - high.astype(f32)).astype(bf16)
        scores = jnp.dot(high, same_head, preferred_element_type=f32) + jnp.dot(
            low, same_head, preferred_element_type=f32
        )
        scores = [scores[j * rows : (j + 1) * rows] for j in range(k + 1)]
        peak = functools.reduce(jnp.maximum, scores)
        expo = [jnp.exp(score - peak) for score in scores]
        total = functools.reduce(jnp.add, expo)
        context = 0.0
        for j in range(k + 1):
            probability = (expo[j] / total).astype(bf16).astype(f32)
            context = context + probability * values_all[j]
        contexts.append(context)
    out_ref[...] = jnp.stack(contexts, axis=1).astype(bf16)


def attend(place, arrived):
    books = len(arrived)
    rows, wide = arrived[0].shape
    vmem = pl.BlockSpec(memory_space=pltpu.VMEM)
    return pl.pallas_call(
        functools.partial(attend_kernel, books),
        out_shape=jax.ShapeDtypeStruct((rows, books, wide // 3), bf16),
        in_specs=[pl.BlockSpec(memory_space=pltpu.SMEM)] + [vmem] * books,
        out_specs=vmem,
        scratch_shapes=[pltpu.VMEM((books, rows, wide), bf16)],
        compiler_params=pltpu.CompilerParams(vmem_limit_bytes=16 * 2**20),
        name="attend_books",
    )(place, *arrived)


def swap(value, axis, distance):
    return lax.ppermute(value, axis, [(i, i ^ distance) for i in range(lax.axis_size(axis))])


def after(value, *others):
    return lax.optimization_barrier((value, *others))[0]


def bits_of(number):
    return [1 << place for place in range(number.bit_length()) if number >> place & 1]


def per_device(
    gate_pre,
    up_pre,
    down_weight,
    residual,
    out_gain,
    in_proj,
    embedding,
    token_ids,
    depth_gain,
    qkv_weight,
):
    books = lax.axis_size("book")
    groups = lax.axis_size("frames")
    here = lax.axis_index("book").astype(jnp.int32)
    place = jnp.stack([here, lax.axis_index("frames").astype(jnp.int32)])
    width = residual.shape[1]
    depth = in_proj.shape[2]
    wide = qkv_weight.shape[2]
    proj_rows = in_proj.shape[1]
    table_rows = embedding.shape[1]
    qkv_rows = qkv_weight.shape[1]
    gain = out_gain.astype(f32)[None]

    hidden = (jax.nn.silu(gate_pre.astype(f32)) * up_pre.astype(f32)).astype(bf16)

    def share(m, *others):
        start = jnp.bitwise_xor(here, m) * width
        block = lax.dynamic_slice_in_dim(down_weight, start, width, 1)
        factor = after(hidden, *others) if others else hidden
        return jnp.dot(factor, block, preferred_element_type=f32)

    sums = {books - 1: share(books - 1)}
    first = sums[books - 1].astype(bf16)

    rows = pack(*after((in_proj[0], embedding[0], qkv_weight[0]), first))
    parts = {0: [(0, rows)]}
    near = [n for n in range(2, groups, 2) if len(bits_of(n)) == 1]
    for n in near:
        parts[n] = [(0, swap(rows, "frames", n))]

    sums[books - 2] = lax.optimization_barrier(share(books - 2, rows))
    distance = 1
    while distance < books:
        came = None
        for m in range(books - distance, 0, -2 * distance):
            going = sums.pop(m).astype(bf16)
            if came is not None:
                going = after(going, came, sums[m + distance])
            came = swap(going, "book", distance)
            if m == books - 1:
                for n in range(books - 3, -1, -1):
                    sums[n] = lax.optimization_barrier(share(n, came))
                sums[0] = sums[0] + residual.astype(f32)
            sums[m ^ distance] = sums[m ^ distance] + came.astype(f32)
        distance *= 2

    blocks = {0: sums[0].astype(bf16)}
    distance = books // 2
    while distance:
        for m in sorted(blocks):
            going = blocks[m] if m == 0 else after(blocks[m], blocks[distance])
            blocks[m ^ distance] = swap(going, "book", distance)
        distance //= 2

    arrived = after([parts[n][0][1] for n in near], blocks[0])
    for n, value in zip(near, arrived):
        parts[n] = [(0, value)]
    cut = rows.shape[0] // 2 // 128 * 128
    for n in range(2, groups, 2):
        sides = bits_of(n)
        if n in near:
            continue
        if len(sides) == 2 and 0 < cut < proj_rows:
            upper = swap(parts[n ^ sides[0]][0][1][:cut], "frames", sides[0])
            lower = swap(parts[n ^ sides[1]][0][1][cut:], "frames", sides[1])
            parts[n] = [(0, upper), (cut, lower)]
        else:
            parts[n] = [(0, swap(rows, "frames", n))]
    for n in range(0, groups, 2):
        parts[n + 1] = [(first, swap(value, "frames", 1)) for first, value in parts[n]]
    looked, qkv = assemble(
        place,
        token_ids,
        [parts[n][-1][1] for n in range(groups)],
        [proj_rows - parts[n][-1][0] for n in range(groups)],
        table_rows,
        qkv_rows,
        wide,
    )

    pieces, proj = [], []
    for n in range(groups):
        for first, value in parts[n]:
            pieces.append((n, first, min(value.shape[0], proj_rows - first)))
            proj.append(value)
    early = [m for m in range(books) if not is_late(m)]
    late = [m for m in range(books) if is_late(m)]
    projected, square = project_early(place, gain, blocks, early, pieces, proj)
    packed = project_late(
        place,
        gain,
        blocks,
        late,
        pieces,
        proj,
        projected,
        square,
        looked,
        depth_gain.astype(f32),
        qkv,
    )
    far = {m: swap(packed[m], "book", m) for m in range(books - 1, 0, -1)}
    return attend(place, [packed[0]] + [far[m] for m in range(1, books)])


def solution(mesh):
    in_specs = (
        P("frames", "book"),
        P("frames", "book"),
        P("book", None),
        P("frames", "book"),
        P(),
        P("book", "frames", None),
        P("book", "frames", None),
        P("frames", "book"),
        P("book", None),
        P("book", "frames", None),
    )
    out_specs = P(("frames", "book"), None, None)
    return jax.shard_map(
        per_device, mesh=mesh, in_specs=in_specs, out_specs=out_specs, check_vma=False
    )
```

```python
import functools

import jax
import jax.numpy as jnp
from jax import lax
from jax.experimental import pallas as pl
from jax.experimental.pallas import tpu as pltpu
from jax.sharding import PartitionSpec as P

H = 8
HD = 64
f32, bf16 = jnp.float32, jnp.bfloat16


def pack_kernel(proj_ref, table_ref, qkv_ref, packed_ref, sems):
    proj_rows, depth = proj_ref.shape
    table_rows = table_ref.shape[0]
    qkv_rows, wide = qkv_ref.shape
    half, extra = qkv_rows // 2, wide - depth
    at_qkv = proj_rows + table_rows
    at_extra = at_qkv + qkv_rows
    moves = [
        (proj_ref, packed_ref.at[pl.ds(0, proj_rows)]),
        (table_ref, packed_ref.at[pl.ds(proj_rows, table_rows)]),
        (qkv_ref.at[:, pl.ds(0, depth)], packed_ref.at[pl.ds(at_qkv, qkv_rows)]),
    ]
    for side in range(2):
        moves.append(
            (
                qkv_ref.at[pl.ds(side * half, half), pl.ds(depth, extra)],
                packed_ref.at[pl.ds(at_extra, half), pl.ds(side * extra, extra)],
            )
        )
    copies = [
        pltpu.make_async_copy(source, target, sems.at[number])
        for number, (source, target) in enumerate(moves)
    ]
    for made in copies:
        made.start()
    for made in copies:
        made.wait()


def pack(proj, table, qkv):
    depth = proj.shape[1]
    rows = proj.shape[0] + table.shape[0] + qkv.shape[0] + qkv.shape[0] // 2
    return pl.pallas_call(
        pack_kernel,
        out_shape=jax.ShapeDtypeStruct((rows, depth), bf16),
        in_specs=[pl.BlockSpec(memory_space=pl.ANY)] * 3,
        out_specs=pl.BlockSpec(memory_space=pltpu.VMEM),
        scratch_shapes=[pltpu.SemaphoreType.DMA((5,))],
        compiler_params=pltpu.CompilerParams(vmem_limit_bytes=4 * 2**20),
        name="pack_weight_rows",
    )(proj, table, qkv)


def is_late(m):
    return (m % 2 == 1) & (m != 1)


def hold_blocks(blocks, here, gain_ref, held):
    square = 0.0
    for m, ref in blocks.items():
        book = jnp.bitwise_xor(here, m)
        part = ref[...].astype(f32)
        square = square + jnp.sum(part * part, axis=-1, keepdims=True)
        width = part.shape[1]
        columns = pl.ds(pl.multiple_of(book * width, width), width)
        held[book] = (part * gain_ref[:, columns]).astype(bf16)
    return square


def early_kernel(books, early, pieces, sizes, place_ref, tokens_ref, gain_ref, *refs):
    blocks = dict(zip(early, refs))
    parts = refs[len(early) : len(early) + len(pieces)]
    outs = refs[len(early) + len(pieces) :]
    projected_ref, square_ref, later_ref, looked_ref, qkv_ref, held, table, sems = outs
    proj_rows, table_rows, qkv_rows = sizes
    here, group = place_ref[0], place_ref[1]
    width = held.shape[2]
    per_book = width // proj_rows
    half = qkv_rows // 2
    depth = table.shape[1]
    extra = qkv_ref.shape[1] - depth

    moves = []
    for (n, first), ref in zip(pieces, parts):
        if first + ref.shape[0] <= proj_rows:
            continue
        g = jnp.bitwise_xor(group, n)
        at_table = proj_rows - first
        at_qkv = at_table + table_rows
        at_extra = at_qkv + qkv_rows
        start = pl.multiple_of(g * table_rows, table_rows)
        moves.append(
            (0, ref.at[pl.ds(at_table, table_rows)], table.at[pl.ds(start, table_rows)])
        )
        start = pl.multiple_of(g * qkv_rows, qkv_rows)
        moves.append(
            (
                1,
                ref.at[pl.ds(at_qkv, qkv_rows)],
                qkv_ref.at[pl.ds(start, qkv_rows), pl.ds(0, depth)],
            )
        )
        for side in range(2):
            start = pl.multiple_of(g * qkv_rows + side * half, half)
            moves.append(
                (
                    1,
                    ref.at[pl.ds(at_extra, half), pl.ds(side * extra, extra)],
                    qkv_ref.at[pl.ds(start, half), pl.ds(depth, extra)],
                )
            )
    copies = [
        (kind, pltpu.make_async_copy(source, target, sems.at[number]))
        for number, (kind, source, target) in enumerate(moves)
    ]
    for _, made in copies:
        made.start()

    square_ref[...] = hold_blocks(blocks, here, gain_ref, held)
    projected_ref[...] = jnp.zeros_like(projected_ref)
    for (n, first), ref in zip(pieces, parts):
        count = min(ref.shape[0], proj_rows - first)
        owner = jnp.bitwise_xor(group, n)
        book = owner // per_book
        start = pl.multiple_of((owner % per_book) * proj_rows + first, 128)
        late = is_late(jnp.bitwise_xor(here, book))

        @pl.when(jnp.logical_not(late))
        def _():
            projected_ref[...] += jnp.dot(
                held[book, :, pl.ds(start, count)], ref[:count, :], preferred_element_type=f32
            )

        @pl.when(late)
        def _():
            slot = jnp.bitwise_xor(here, book) // 2 - 1
            later_ref[slot, pl.ds(start, count), :] = ref[:count, :]

    columns = lax.broadcasted_iota(jnp.int32, (tokens_ref.shape[0], table.shape[0]), 1)
    matches = (tokens_ref[...] == columns).astype(f32).astype(bf16)
    for kind, made in copies:
        if kind == 0:
            made.wait()
    looked_ref[...] = jnp.dot(matches, table[...], preferred_element_type=f32).astype(bf16)
    for kind, made in copies:
        if kind == 1:
            made.wait()


def project_early(place, tokens, gain, blocks, early, pieces, parts, sizes, wide):
    books = len(blocks)
    frames_here, width = blocks[0].shape
    depth = parts[0].shape[1]
    proj_rows, table_rows, qkv_rows = sizes
    groups = books * width // proj_rows
    vmem = pl.BlockSpec(memory_space=pltpu.VMEM)
    return pl.pallas_call(
        functools.partial(early_kernel, books, early, pieces, sizes),
        out_shape=[
            jax.ShapeDtypeStruct((frames_here, depth), f32),
            jax.ShapeDtypeStruct((frames_here, 1), f32),
            jax.ShapeDtypeStruct((books - len(early), width, depth), bf16),
            jax.ShapeDtypeStruct((frames_here, depth), bf16),
            jax.ShapeDtypeStruct((groups * qkv_rows, wide), bf16),
        ],
        in_specs=[pl.BlockSpec(memory_space=pltpu.SMEM)]
        + [vmem] * (2 + len(early) + len(parts)),
        out_specs=[vmem] * 5,
        scratch_shapes=[
            pltpu.VMEM((books, frames_here, width), bf16),
            pltpu.VMEM((groups * table_rows, depth), bf16),
            pltpu.SemaphoreType.DMA((4 * groups,)),
        ],
        compiler_params=pltpu.CompilerParams(vmem_limit_bytes=36 * 2**20),
        cost_estimate=pl.CostEstimate(flops=0, bytes_accessed=0, transcendentals=0),
        name="early_products_and_lookup",
    )(place, tokens, gain, *[blocks[m] for m in early], *parts)


def late_kernel(books, late, place_ref, gain_ref, *refs):
    blocks = dict(zip(late, refs))
    later_ref, early_ref, square_ref, looked_ref, depth_gain_ref, qkv_ref = refs[
        len(late) : len(late) + 6
    ]
    refs = refs[len(late) + 6 :]
    outs = refs[:books]
    held, packed = refs[books:]
    here = place_ref[0]
    frames_here, width = held.shape[1:]
    square = square_ref[...] + hold_blocks(blocks, here, gain_ref, held)
    projected = early_ref[...]
    for slot, m in enumerate(late):
        projected = projected + jnp.dot(
            held[jnp.bitwise_xor(here, m)], later_ref[slot], preferred_element_type=f32
        )
    projected = projected * lax.rsqrt(square / (books * width) + 1e-05)
    depth_in = (projected + looked_ref[...].astype(f32)).astype(bf16).astype(f32)
    moment = jnp.mean(depth_in * depth_in, axis=-1, keepdims=True)
    depth_normed = (depth_in * lax.rsqrt(moment + 1e-05) * depth_gain_ref[...]).astype(bf16)
    packed[...] = jnp.dot(depth_normed, qkv_ref[...], preferred_element_type=f32).astype(bf16)
    rows = frames_here // books
    for m in range(books):
        start = pl.multiple_of(jnp.bitwise_xor(here, m) * rows, rows)
        outs[m][...] = packed[pl.ds(start, rows), :]


def project_late(place, gain, blocks, late, later, projected, square, looked, depth_gain, qkv):
    books = len(blocks)
    frames_here, width = blocks[0].shape
    wide = qkv.shape[1]
    vmem = pl.BlockSpec(memory_space=pltpu.VMEM)
    return pl.pallas_call(
        functools.partial(late_kernel, books, late),
        out_shape=[jax.ShapeDtypeStruct((frames_here // books, wide), bf16)] * books,
        in_specs=[pl.BlockSpec(memory_space=pltpu.SMEM)] + [vmem] * (len(late) + 7),
        out_specs=[vmem] * books,
        scratch_shapes=[
            pltpu.VMEM((books, frames_here, width), bf16),
            pltpu.VMEM((frames_here, wide), bf16),
        ],
        compiler_params=pltpu.CompilerParams(vmem_limit_bytes=24 * 2**20),
        name="late_products_and_qkv",
    )(
        place,
        gain,
        *[blocks[m] for m in late],
        later,
        projected,
        square,
        looked,
        depth_gain,
        qkv,
    )


def attend_kernel(books, place_ref, *refs):
    arrived = refs[:books]
    out_ref, inner = refs[books:]
    place = place_ref[0]
    rows, wide = arrived[0].shape
    width = wide // 3
    for m in range(books):
        inner[jnp.bitwise_xor(place, m)] = arrived[m][...]
    head_of_row = lax.broadcasted_iota(jnp.int32, (width, width), 0) // HD
    head_of_column = lax.broadcasted_iota(jnp.int32, (width, width), 1) // HD
    same_head = (head_of_row == head_of_column).astype(f32).astype(bf16)
    keys_all = [inner[j, :, width : 2 * width].astype(f32) for j in range(books)]
    values_all = [inner[j, :, 2 * width :].astype(f32) for j in range(books)]
    contexts = []
    for k in range(books):
        query = inner[k, :, :width].astype(f32) * HD ** (-0.5)
        products = jnp.concatenate([query * keys_all[j] for j in range(k + 1)], axis=0)
        high = products.astype(bf16)
        low = (products - high.astype(f32)).astype(bf16)
        scores = jnp.dot(high, same_head, preferred_element_type=f32) + jnp.dot(
            low, same_head, preferred_element_type=f32
        )
        scores = [scores[j * rows : (j + 1) * rows] for j in range(k + 1)]
        peak = functools.reduce(jnp.maximum, scores)
        expo = [jnp.exp(score - peak) for score in scores]
        total = functools.reduce(jnp.add, expo)
        context = 0.0
        for j in range(k + 1):
            probability = (expo[j] / total).astype(bf16).astype(f32)
            context = context + probability * values_all[j]
        contexts.append(context)
    out_ref[...] = jnp.stack(contexts, axis=1).astype(bf16)


def attend(place, arrived):
    books = len(arrived)
    rows, wide = arrived[0].shape
    vmem = pl.BlockSpec(memory_space=pltpu.VMEM)
    return pl.pallas_call(
        functools.partial(attend_kernel, books),
        out_shape=jax.ShapeDtypeStruct((rows, books, wide // 3), bf16),
        in_specs=[pl.BlockSpec(memory_space=pltpu.SMEM)] + [vmem] * books,
        out_specs=vmem,
        scratch_shapes=[pltpu.VMEM((books, rows, wide), bf16)],
        compiler_params=pltpu.CompilerParams(vmem_limit_bytes=16 * 2**20),
        name="attend_books",
    )(place, *arrived)


def swap(value, axis, distance):
    return lax.ppermute(value, axis, [(i, i ^ distance) for i in range(lax.axis_size(axis))])


def after(value, *others):
    return lax.optimization_barrier((value, *others))[0]


def bits_of(number):
    return [1 << place for place in range(number.bit_length()) if number >> place & 1]


def per_device(
    gate_pre,
    up_pre,
    down_weight,
    residual,
    out_gain,
    in_proj,
    embedding,
    token_ids,
    depth_gain,
    qkv_weight,
):
    books = lax.axis_size("book")
    groups = lax.axis_size("frames")
    here = lax.axis_index("book").astype(jnp.int32)
    place = jnp.stack([here, lax.axis_index("frames").astype(jnp.int32)])
    width = residual.shape[1]
    depth = in_proj.shape[2]
    wide = qkv_weight.shape[2]
    proj_rows = in_proj.shape[1]
    table_rows = embedding.shape[1]
    qkv_rows = qkv_weight.shape[1]
    gain = out_gain.astype(f32)[None]

    hidden = (jax.nn.silu(gate_pre.astype(f32)) * up_pre.astype(f32)).astype(bf16)

    def share(m, *others):
        start = jnp.bitwise_xor(here, m) * width
        block = lax.dynamic_slice_in_dim(down_weight, start, width, 1)
        factor = after(hidden, *others) if others else hidden
        return jnp.dot(factor, block, preferred_element_type=f32)

    sums = {books - 1: share(books - 1)}
    first = sums[books - 1].astype(bf16)

    rows = pack(*after((in_proj[0], embedding[0], qkv_weight[0]), first))
    parts = {0: [(0, rows)]}
    near = [n for n in range(2, groups, 2) if len(bits_of(n)) == 1]
    for n in near:
        parts[n] = [(0, swap(rows, "frames", n))]

    parts[1] = [(0, swap(rows, "frames", 1))]
    sums[books - 2] = lax.optimization_barrier(share(books - 2, rows))
    for m in range(books - 3, 0, -1):
        sums[m] = lax.optimization_barrier(share(m, parts[1][0][1]))
    distance = 1
    while distance < books:
        came = None
        for m in range(books - distance, 0, -2 * distance):
            going = sums.pop(m).astype(bf16)
            if came is not None:
                going = after(going, came, sums[m + distance])
            came = swap(going, "book", distance)
            sums[m ^ distance] = sums[m ^ distance] + came.astype(f32)
            if m == books - 1:
                sums[0] = lax.optimization_barrier(share(0, came))
                sums[0] = sums[0] + residual.astype(f32)
        distance *= 2

    blocks = {0: sums[0].astype(bf16)}

    arrived = after([parts[n][0][1] for n in near], blocks[0])
    for n, value in zip(near, arrived):
        parts[n] = [(0, value)]
    cut = rows.shape[0] // 2 // 128 * 128
    for n in range(2, groups, 2):
        sides = bits_of(n)
        if n in near:
            continue
        if len(sides) == 2 and 0 < cut < proj_rows:
            upper = swap(parts[n ^ sides[0]][0][1][:cut], "frames", sides[0])
            lower = swap(parts[n ^ sides[1]][0][1][cut:], "frames", sides[1])
            parts[n] = [(0, upper), (cut, lower)]
        else:
            parts[n] = [(0, swap(rows, "frames", n))]
    for n in range(2, groups, 2):
        parts[n + 1] = [(first, swap(value, "frames", 1)) for first, value in parts[n]]

    near_there = [parts[n + 1][0][1] for n in near]
    distance = books // 2
    while distance:
        for m in sorted(blocks):
            going = blocks[m]
            if m:
                going = after(going, blocks[distance])
            elif distance == 1:
                going = after(going, *near_there)
            blocks[m ^ distance] = swap(going, "book", distance)
        distance //= 2

    pieces = [(n, first) for n in range(groups) for first, _ in parts[n]]
    early = [m for m in range(books) if not is_late(m)]
    late = [m for m in range(books) if is_late(m)]
    projected, square, later, looked, qkv = project_early(
        place,
        token_ids,
        gain,
        blocks,
        early,
        pieces,
        [value for n in range(groups) for _, value in parts[n]],
        (proj_rows, table_rows, qkv_rows),
        wide,
    )
    packed = project_late(
        place,
        gain,
        blocks,
        late,
        later,
        projected,
        square,
        looked,
        depth_gain.astype(f32),
        qkv,
    )
    far = {m: swap(packed[m], "book", m) for m in range(books - 1, 0, -1)}
    return attend(place, [packed[0]] + [far[m] for m in range(1, books)])


def solution(mesh):
    in_specs = (
        P("frames", "book"),
        P("frames", "book"),
        P("book", None),
        P("frames", "book"),
        P(),
        P("book", "frames", None),
        P("book", "frames", None),
        P("frames", "book"),
        P("book", None),
        P("book", "frames", None),
    )
    out_specs = P(("frames", "book"), None, None)
    return jax.shard_map(
        per_device, mesh=mesh, in_specs=in_specs, out_specs=out_specs, check_vma=False
    )
```

```python
import functools

import jax
import jax.numpy as jnp
from jax import lax
from jax.experimental import pallas as pl
from jax.experimental.pallas import tpu as pltpu
from jax.sharding import PartitionSpec as P

H = 8
HD = 64
f32, bf16 = jnp.float32, jnp.bfloat16


def first_kernel(place_ref, gate_ref, up_ref, down_ref, hidden_ref, first_ref, held, sems):
    steps, each, width = held.shape
    books = down_ref.shape[1] // width
    start = pl.multiple_of(jnp.bitwise_xor(place_ref[0], books - 1) * width, width)
    copies = []
    for step in range(steps):
        copies.append(
            pltpu.make_async_copy(
                down_ref.at[pl.ds(step * each, each), pl.ds(start, width)],
                held.at[step],
                sems.at[step],
            )
        )
        copies[-1].start()
    total = 0.0
    for step in range(steps):
        columns = pl.ds(step * each, each)
        gate = gate_ref[:, columns].astype(f32)
        hidden = gate / (1.0 + jnp.exp(-gate)) * up_ref[:, columns].astype(f32)
        hidden = hidden.astype(bf16)
        hidden_ref[:, columns] = hidden
        copies[step].wait()
        total = total + jnp.dot(hidden, held[step], preferred_element_type=f32)
    first_ref[...] = total.astype(bf16)


def first_products(place, gate, up, down, width):
    frames_here, hidden_width = gate.shape
    steps = max(hidden_width // 512, 1)
    vmem = pl.BlockSpec(memory_space=pltpu.VMEM)
    return pl.pallas_call(
        first_kernel,
        out_shape=[
            jax.ShapeDtypeStruct((frames_here, hidden_width), bf16),
            jax.ShapeDtypeStruct((frames_here, width), bf16),
        ],
        in_specs=[pl.BlockSpec(memory_space=pltpu.SMEM)]
        + [vmem] * 2
        + [pl.BlockSpec(memory_space=pl.ANY)],
        out_specs=[vmem] * 2,
        scratch_shapes=[
            pltpu.VMEM((steps, hidden_width // steps, width), bf16),
            pltpu.SemaphoreType.DMA((steps,)),
        ],
        compiler_params=pltpu.CompilerParams(vmem_limit_bytes=56 * 2**20),
        name="hidden_and_first_products",
    )(place, gate, up, down)


def pack_kernel(proj_ref, table_ref, qkv_ref, packed_ref, sems):
    proj_rows, depth = proj_ref.shape
    table_rows = table_ref.shape[0]
    qkv_rows, wide = qkv_ref.shape
    half, extra = qkv_rows // 2, wide - depth
    at_qkv = proj_rows + table_rows
    at_extra = at_qkv + qkv_rows
    moves = [
        (proj_ref, packed_ref.at[pl.ds(0, proj_rows)]),
        (table_ref, packed_ref.at[pl.ds(proj_rows, table_rows)]),
        (qkv_ref.at[:, pl.ds(0, depth)], packed_ref.at[pl.ds(at_qkv, qkv_rows)]),
    ]
    for side in range(2):
        moves.append(
            (
                qkv_ref.at[pl.ds(side * half, half), pl.ds(depth, extra)],
                packed_ref.at[pl.ds(at_extra, half), pl.ds(side * extra, extra)],
            )
        )
    copies = [
        pltpu.make_async_copy(source, target, sems.at[number])
        for number, (source, target) in enumerate(moves)
    ]
    for made in copies:
        made.start()
    for made in copies:
        made.wait()


def pack(proj, table, qkv):
    depth = proj.shape[1]
    rows = proj.shape[0] + table.shape[0] + qkv.shape[0] + qkv.shape[0] // 2
    return pl.pallas_call(
        pack_kernel,
        out_shape=jax.ShapeDtypeStruct((rows, depth), bf16),
        in_specs=[pl.BlockSpec(memory_space=pl.ANY)] * 3,
        out_specs=pl.BlockSpec(memory_space=pltpu.VMEM),
        scratch_shapes=[pltpu.SemaphoreType.DMA((5,))],
        compiler_params=pltpu.CompilerParams(vmem_limit_bytes=56 * 2**20),
        name="pack_weight_rows",
    )(proj, table, qkv)


def is_late(m):
    return (m % 2 == 1) & (m != 1)


def hold_blocks(blocks, here, gain_ref, held):
    square = 0.0
    for m, ref in blocks.items():
        book = jnp.bitwise_xor(here, m)
        part = ref[...].astype(f32)
        square = square + jnp.sum(part * part, axis=-1, keepdims=True)
        width = part.shape[1]
        columns = pl.ds(pl.multiple_of(book * width, width), width)
        held[book] = (part * gain_ref[:, columns].astype(f32)).astype(bf16)
    return square


def early_kernel(books, early, pieces, sizes, place_ref, tokens_ref, gain_ref, *refs):
    blocks = dict(zip(early, refs))
    parts = refs[len(early) : len(early) + len(pieces)]
    projected_ref, square_ref, looked_ref, held, proj, table, sems = refs[
        len(early) + len(pieces) :
    ]
    proj_rows, table_rows, _ = sizes
    here, group = place_ref[0], place_ref[1]
    per_book = held.shape[2] // proj_rows

    table_copies, proj_copies = [], []
    for number, ((n, first), ref) in enumerate(zip(pieces, parts)):
        if first + ref.shape[0] > proj_rows:
            g = jnp.bitwise_xor(group, n)
            start = pl.multiple_of(g * table_rows, table_rows)
            made = pltpu.make_async_copy(
                ref.at[pl.ds(proj_rows - first, table_rows)],
                table.at[pl.ds(start, table_rows)],
                sems.at[number],
            )
            made.start()
            table_copies.append(made)
    for number, ((n, first), ref) in enumerate(zip(pieces, parts)):
        count = min(ref.shape[0], proj_rows - first)
        made = pltpu.make_async_copy(
            ref.at[pl.ds(0, count)],
            proj.at[pl.ds(n * proj_rows + first, count)],
            sems.at[len(pieces) + number],
        )
        made.start()
        proj_copies.append(made)

    square_ref[...] = hold_blocks(blocks, here, gain_ref, held)
    codes = lax.broadcasted_iota(jnp.int32, (table.shape[0], tokens_ref.shape[1]), 0)
    matches = (tokens_ref[...] == codes).astype(f32).astype(bf16)
    for made in table_copies:
        made.wait()
    looked = lax.dot_general(
        matches, table[...], (((0,), (0,)), ((), ())), preferred_element_type=f32
    )
    looked_ref[...] = looked.astype(bf16)
    projected_ref[...] = jnp.zeros_like(projected_ref)
    for (n, first), made, ref in zip(pieces, proj_copies, parts):
        count = min(ref.shape[0], proj_rows - first)
        owner = jnp.bitwise_xor(group, n)
        book = owner // per_book
        start = pl.multiple_of((owner % per_book) * proj_rows + first, 128)
        made.wait()

        @pl.when(jnp.logical_not(is_late(jnp.bitwise_xor(here, book))))
        def _():
            projected_ref[...] += jnp.dot(
                held[book, :, pl.ds(start, count)],
                proj[pl.ds(n * proj_rows + first, count), :],
                preferred_element_type=f32,
            )


def project_early(place, tokens, gain, blocks, early, pieces, parts, sizes):
    books = len(blocks)
    frames_here, width = blocks[0].shape
    depth = parts[0].shape[1]
    proj_rows, table_rows, _ = sizes
    groups = books * width // proj_rows
    vmem = pl.BlockSpec(memory_space=pltpu.VMEM)
    return pl.pallas_call(
        functools.partial(early_kernel, books, early, pieces, sizes),
        out_shape=[
            jax.ShapeDtypeStruct((frames_here, depth), f32),
            jax.ShapeDtypeStruct((frames_here, 1), f32),
            jax.ShapeDtypeStruct((frames_here, depth), bf16),
        ],
        in_specs=[pl.BlockSpec(memory_space=pltpu.SMEM)]
        + [vmem] * (2 + len(early))
        + [pl.BlockSpec(memory_space=pl.ANY)] * len(parts),
        out_specs=[vmem] * 3,
        scratch_shapes=[
            pltpu.VMEM((books, frames_here, width), bf16),
            pltpu.VMEM((books * width, depth), bf16),
            pltpu.VMEM((groups * table_rows, depth), bf16),
            pltpu.SemaphoreType.DMA((2 * len(pieces),)),
        ],
        compiler_params=pltpu.CompilerParams(vmem_limit_bytes=50 * 2**20),
        cost_estimate=pl.CostEstimate(flops=0, bytes_accessed=0, transcendentals=0),
        name="early_products_and_lookup",
    )(place, tokens, gain, *[blocks[m] for m in early], *parts)


def late_kernel(books, late, pieces, sizes, place_ref, gain_ref, *refs):
    blocks = dict(zip(late, refs))
    early_ref, square_ref, looked_ref, depth_gain_ref = refs[len(late) : len(late) + 4]
    refs = refs[len(late) + 4 :]
    parts = refs[: len(pieces)]
    outs = refs[len(pieces) : len(pieces) + books]
    held, proj, qkv, packed, sems = refs[len(pieces) + books :]
    proj_rows, table_rows, qkv_rows = sizes
    here, group = place_ref[0], place_ref[1]
    frames_here, width = held.shape[1:]
    per_book = width // proj_rows
    half = qkv_rows // 2
    depth = proj.shape[2]
    extra = qkv.shape[1] - depth

    proj_copies = []
    for number, ((n, first), ref) in enumerate(zip(pieces, parts)):
        count = min(ref.shape[0], proj_rows - first)
        owner = jnp.bitwise_xor(group, n)
        m = jnp.bitwise_xor(here, owner // per_book)
        start = pl.multiple_of((owner % per_book) * proj_rows + first, 128)
        slot = jnp.maximum(m // 2 - 1, 0)
        made = pltpu.make_async_copy(
            ref.at[pl.ds(0, count)], proj.at[slot, pl.ds(start, count)], sems.at[number]
        )
        pl.when(is_late(m))(made.start)
        proj_copies.append((is_late(m), made))
    qkv_copies = []

    def copy(source, target):
        made = pltpu.make_async_copy(source, target, sems.at[len(pieces) + len(qkv_copies)])
        made.start()
        qkv_copies.append(made)

    for (n, first), ref in zip(pieces, parts):
        if first + ref.shape[0] > proj_rows:
            g = jnp.bitwise_xor(group, n)
            at_qkv = proj_rows - first + table_rows
            start = pl.multiple_of(g * qkv_rows, qkv_rows)
            copy(
                ref.at[pl.ds(at_qkv, qkv_rows)], qkv.at[pl.ds(start, qkv_rows), pl.ds(0, depth)]
            )
            for side in range(2):
                start = pl.multiple_of(g * qkv_rows + side * half, half)
                copy(
                    ref.at[pl.ds(at_qkv + qkv_rows, half), pl.ds(side * extra, extra)],
                    qkv.at[pl.ds(start, half), pl.ds(depth, extra)],
                )

    square = square_ref[...] + hold_blocks(blocks, here, gain_ref, held)
    projected = early_ref[...]
    for late_here, made in proj_copies:
        pl.when(late_here)(made.wait)
    for slot, m in enumerate(late):
        projected = projected + jnp.dot(
            held[jnp.bitwise_xor(here, m)], proj[slot], preferred_element_type=f32
        )
    projected = projected * lax.rsqrt(square / (books * width) + 1e-05)
    depth_in = (projected + looked_ref[...].astype(f32)).astype(bf16).astype(f32)
    moment = jnp.mean(depth_in * depth_in, axis=-1, keepdims=True)
    depth_normed = depth_in * lax.rsqrt(moment + 1e-05) * depth_gain_ref[...].astype(f32)
    for made in qkv_copies:
        made.wait()
    packed[...] = jnp.dot(
        depth_normed.astype(bf16), qkv[...], preferred_element_type=f32
    ).astype(bf16)
    rows = frames_here // books
    for m in range(books):
        start = pl.multiple_of(jnp.bitwise_xor(here, m) * rows, rows)
        outs[m][...] = packed[pl.ds(start, rows), :]


def project_late(
    place, gain, blocks, late, projected, square, looked, depth_gain, pieces, parts, sizes, wide
):
    books = len(blocks)
    frames_here, width = blocks[0].shape
    depth = projected.shape[1]
    proj_rows, _, qkv_rows = sizes
    groups = books * width // proj_rows
    vmem = pl.BlockSpec(memory_space=pltpu.VMEM)
    return pl.pallas_call(
        functools.partial(late_kernel, books, late, pieces, sizes),
        out_shape=[jax.ShapeDtypeStruct((frames_here // books, wide), bf16)] * books,
        in_specs=[pl.BlockSpec(memory_space=pltpu.SMEM)]
        + [vmem] * (len(late) + 5)
        + [pl.BlockSpec(memory_space=pl.ANY)] * len(parts),
        out_specs=[vmem] * books,
        scratch_shapes=[
            pltpu.VMEM((books, frames_here, width), bf16),
            pltpu.VMEM((len(late), width, depth), bf16),
            pltpu.VMEM((groups * qkv_rows, wide), bf16),
            pltpu.VMEM((frames_here, wide), bf16),
            pltpu.SemaphoreType.DMA((len(pieces) + 3 * groups,)),
        ],
        compiler_params=pltpu.CompilerParams(vmem_limit_bytes=50 * 2**20),
        name="late_products_and_qkv",
    )(
        place,
        gain,
        *[blocks[m] for m in late],
        projected,
        square,
        looked,
        depth_gain,
        *parts,
    )


def attend_kernel(books, place_ref, *refs):
    arrived = refs[:books]
    out_ref, inner = refs[books:]
    place = place_ref[0]
    rows, wide = arrived[0].shape
    width = wide // 3
    for m in range(books):
        inner[jnp.bitwise_xor(place, m)] = arrived[m][...]
    head_of_row = lax.broadcasted_iota(jnp.int32, (width, width), 0) // HD
    head_of_column = lax.broadcasted_iota(jnp.int32, (width, width), 1) // HD
    same_head = (head_of_row == head_of_column).astype(f32).astype(bf16)
    keys_all = [inner[j, :, width : 2 * width].astype(f32) for j in range(books)]
    values_all = [inner[j, :, 2 * width :].astype(f32) for j in range(books)]
    contexts = []
    for k in range(books):
        query = inner[k, :, :width].astype(f32) * HD ** (-0.5)
        products = jnp.concatenate([query * keys_all[j] for j in range(k + 1)], axis=0)
        high = products.astype(bf16)
        low = (products - high.astype(f32)).astype(bf16)
        scores = jnp.dot(high, same_head, preferred_element_type=f32) + jnp.dot(
            low, same_head, preferred_element_type=f32
        )
        scores = [scores[j * rows : (j + 1) * rows] for j in range(k + 1)]
        peak = functools.reduce(jnp.maximum, scores)
        expo = [jnp.exp(score - peak) for score in scores]
        total = functools.reduce(jnp.add, expo)
        context = 0.0
        for j in range(k + 1):
            probability = (expo[j] / total).astype(bf16).astype(f32)
            context = context + probability * values_all[j]
        contexts.append(context)
    out_ref[...] = jnp.stack(contexts, axis=1).astype(bf16)


def attend(place, arrived):
    books = len(arrived)
    rows, wide = arrived[0].shape
    vmem = pl.BlockSpec(memory_space=pltpu.VMEM)
    return pl.pallas_call(
        functools.partial(attend_kernel, books),
        out_shape=jax.ShapeDtypeStruct((rows, books, wide // 3), bf16),
        in_specs=[pl.BlockSpec(memory_space=pltpu.SMEM)] + [vmem] * books,
        out_specs=vmem,
        scratch_shapes=[pltpu.VMEM((books, rows, wide), bf16)],
        compiler_params=pltpu.CompilerParams(vmem_limit_bytes=16 * 2**20),
        name="attend_books",
    )(place, *arrived)


def swap(value, axis, distance):
    return lax.ppermute(value, axis, [(i, i ^ distance) for i in range(lax.axis_size(axis))])


def after(value, *others):
    return lax.optimization_barrier((value, *others))[0]


def bits_of(number):
    return [1 << place for place in range(number.bit_length()) if number >> place & 1]


def per_device(
    gate_pre,
    up_pre,
    down_weight,
    residual,
    out_gain,
    in_proj,
    embedding,
    token_ids,
    depth_gain,
    qkv_weight,
):
    books = lax.axis_size("book")
    groups = lax.axis_size("frames")
    here = lax.axis_index("book").astype(jnp.int32)
    place = jnp.stack([here, lax.axis_index("frames").astype(jnp.int32)])
    width = residual.shape[1]
    proj_rows = in_proj.shape[1]
    gain = out_gain[None]

    hidden, first = first_products(place, gate_pre, up_pre, down_weight, width)

    def share(m, *others):
        start = jnp.bitwise_xor(here, m) * width
        block = lax.dynamic_slice_in_dim(down_weight, start, width, 1)
        factor = after(hidden, *others) if others else hidden
        return jnp.dot(factor, block, preferred_element_type=f32)

    rows = pack(*after((in_proj[0], embedding[0], qkv_weight[0]), first))
    parts = {0: [(0, rows)]}
    near = [n for n in range(2, groups, 2) if len(bits_of(n)) == 1]
    for n in near:
        parts[n] = [(0, swap(rows, "frames", n))]

    sums = {books - 1: first}
    parts[1] = [(0, swap(rows, "frames", 1))]
    sums[books - 2] = lax.optimization_barrier(share(books - 2, rows))
    for n in range(books - 3, 0, -1):
        sums[n] = lax.optimization_barrier(share(n, parts[1][0][1]))
    distance = 1
    while distance < books:
        came = None
        for m in range(books - distance, 0, -2 * distance):
            going = sums.pop(m).astype(bf16)
            if came is not None:
                going = after(going, came, sums[m + distance])
            came = swap(going, "book", distance)
            sums[m ^ distance] = sums[m ^ distance] + came.astype(f32)
            if m == books - 1:
                sums[0] = lax.optimization_barrier(share(0, came))
                sums[0] = sums[0] + residual.astype(f32)
        distance *= 2

    blocks = {0: sums[0].astype(bf16)}

    arrived = after([parts[n][0][1] for n in near], blocks[0])
    for n, value in zip(near, arrived):
        parts[n] = [(0, value)]
    cut = rows.shape[0] // 2 // 128 * 128
    for n in range(2, groups, 2):
        sides = bits_of(n)
        if n in near:
            continue
        if len(sides) == 2 and 0 < cut < proj_rows:
            upper = swap(parts[n ^ sides[0]][0][1][:cut], "frames", sides[0])
            lower = swap(parts[n ^ sides[1]][0][1][cut:], "frames", sides[1])
            parts[n] = [(0, upper), (cut, lower)]
        else:
            parts[n] = [(0, swap(rows, "frames", n))]
    for n in range(2, groups, 2):
        parts[n + 1] = [(first, swap(value, "frames", 1)) for first, value in parts[n]]

    near_there = [parts[n + 1][0][1] for n in near]
    distance = books // 2
    while distance:
        for m in sorted(blocks):
            going = blocks[m]
            if m:
                going = after(going, blocks[distance])
            elif distance == 1:
                going = after(going, *near_there)
            blocks[m ^ distance] = swap(going, "book", distance)
        distance //= 2

    pieces = [(n, first) for n in range(groups) for first, _ in parts[n]]
    arrived = [value for n in range(groups) for _, value in parts[n]]
    sizes = proj_rows, embedding.shape[1], qkv_weight.shape[1]
    early = [m for m in range(books) if not is_late(m)]
    late = [m for m in range(books) if is_late(m)]
    projected, square, looked = project_early(
        place, token_ids.reshape(1, -1), gain, blocks, early, pieces, arrived, sizes
    )
    packed = project_late(
        place,
        gain,
        blocks,
        late,
        projected,
        square,
        looked,
        depth_gain,
        pieces,
        arrived,
        sizes,
        qkv_weight.shape[2],
    )
    far = {m: swap(packed[m], "book", m) for m in range(books - 1, 0, -1)}
    return attend(place, [packed[0]] + [far[m] for m in range(1, books)])


def solution(mesh):
    in_specs = (
        P("frames", "book"),
        P("frames", "book"),
        P("book", None),
        P("frames", "book"),
        P(),
        P("book", "frames", None),
        P("book", "frames", None),
        P("frames", "book"),
        P("book", None),
        P("book", "frames", None),
    )
    out_specs = P(("frames", "book"), None, None)
    return jax.shard_map(
        per_device, mesh=mesh, in_specs=in_specs, out_specs=out_specs, check_vma=False
    )
```

```python
import functools

import jax
import jax.numpy as jnp
from jax import lax
from jax.experimental import pallas as pl
from jax.experimental.pallas import tpu as pltpu
from jax.sharding import PartitionSpec as P

H = 8
HD = 64
f32, bf16 = jnp.float32, jnp.bfloat16


def first_kernel(gate_ref, up_ref, down_ref, hidden_ref, first_ref, gates, ups, held, sems):
    steps, each, width = held.shape
    books = down_ref.shape[1] // width
    start = pl.multiple_of(jnp.bitwise_xor(lax.axis_index("book"), books - 1) * width, width)
    copies = []
    for step in range(steps):
        rows = pl.ds(step * each, each)
        moves = [
            (gate_ref.at[:, rows], gates.at[step]),
            (up_ref.at[:, rows], ups.at[step]),
            (down_ref.at[rows, pl.ds(start, width)], held.at[step]),
        ]
        for kind, (source, target) in enumerate(moves):
            copies.append(pltpu.make_async_copy(source, target, sems.at[3 * step + kind]))
            copies[-1].start()
    total = 0.0
    for step in range(steps):
        copies[3 * step].wait()
        copies[3 * step + 1].wait()
        gate = gates[step].astype(f32)
        hidden = gate / (1.0 + jnp.exp(-gate)) * ups[step].astype(f32)
        hidden = hidden.astype(bf16)
        hidden_ref[:, pl.ds(step * each, each)] = hidden
        copies[3 * step + 2].wait()
        total = total + jnp.dot(hidden, held[step], preferred_element_type=f32)
    first_ref[...] = total.astype(bf16)


def first_products(gate, up, down, width):
    frames_here, hidden_width = gate.shape
    steps = max(hidden_width // 512, 1)
    vmem = pl.BlockSpec(memory_space=pltpu.VMEM)
    return pl.pallas_call(
        first_kernel,
        out_shape=[
            jax.ShapeDtypeStruct((frames_here, hidden_width), bf16),
            jax.ShapeDtypeStruct((frames_here, width), bf16),
        ],
        in_specs=[pl.BlockSpec(memory_space=pl.ANY)] * 3,
        out_specs=[vmem] * 2,
        scratch_shapes=[
            pltpu.VMEM((steps, frames_here, hidden_width // steps), bf16),
            pltpu.VMEM((steps, frames_here, hidden_width // steps), bf16),
            pltpu.VMEM((steps, hidden_width // steps, width), bf16),
            pltpu.SemaphoreType.DMA((3 * steps,)),
        ],
        compiler_params=pltpu.CompilerParams(vmem_limit_bytes=53 * 2**20),
        name="hidden_and_first_products",
    )(gate, up, down)


def pack_kernel(proj_ref, table_ref, qkv_ref, packed_ref, sems):
    proj_rows, depth = proj_ref.shape
    table_rows = table_ref.shape[0]
    qkv_rows, wide = qkv_ref.shape
    half, extra = qkv_rows // 2, wide - depth
    at_qkv = proj_rows + table_rows
    at_extra = at_qkv + qkv_rows
    moves = [
        (proj_ref, packed_ref.at[pl.ds(0, proj_rows)]),
        (table_ref, packed_ref.at[pl.ds(proj_rows, table_rows)]),
        (qkv_ref.at[:, pl.ds(0, depth)], packed_ref.at[pl.ds(at_qkv, qkv_rows)]),
    ]
    for side in range(2):
        moves.append(
            (
                qkv_ref.at[pl.ds(side * half, half), pl.ds(depth, extra)],
                packed_ref.at[pl.ds(at_extra, half), pl.ds(side * extra, extra)],
            )
        )
    copies = [
        pltpu.make_async_copy(source, target, sems.at[number])
        for number, (source, target) in enumerate(moves)
    ]
    for made in copies:
        made.start()
    for made in copies:
        made.wait()


def pack(proj, table, qkv):
    depth = proj.shape[1]
    rows = proj.shape[0] + table.shape[0] + qkv.shape[0] + qkv.shape[0] // 2
    return pl.pallas_call(
        pack_kernel,
        out_shape=jax.ShapeDtypeStruct((rows, depth), bf16),
        in_specs=[pl.BlockSpec(memory_space=pl.ANY)] * 3,
        out_specs=pl.BlockSpec(memory_space=pltpu.VMEM),
        scratch_shapes=[pltpu.SemaphoreType.DMA((5,))],
        compiler_params=pltpu.CompilerParams(vmem_limit_bytes=4 * 2**20),
        name="pack_weight_rows",
    )(proj, table, qkv)


def is_late(m):
    return (m % 2 == 1) & (m != 1)


def hold_blocks(blocks, here, gain_ref, held):
    square = 0.0
    for m, ref in blocks.items():
        book = jnp.bitwise_xor(here, m)
        part = ref[...].astype(f32)
        square = square + jnp.sum(part * part, axis=-1, keepdims=True)
        width = part.shape[1]
        columns = pl.ds(pl.multiple_of(book * width, width), width)
        held[book] = (part * gain_ref[:, columns].astype(f32)).astype(bf16)
    return square


def early_kernel(books, early, pieces, sizes, tokens_ref, gain_ref, *refs):
    blocks = dict(zip(early, refs))
    parts = refs[len(early) : len(early) + len(pieces)]
    projected_ref, square_ref, looked_ref, held, proj, table, sems = refs[
        len(early) + len(pieces) :
    ]
    proj_rows, table_rows, _ = sizes
    here, group = lax.axis_index("book"), lax.axis_index("frames")
    per_book = held.shape[2] // proj_rows

    table_copies, proj_copies = [], []
    for number, ((n, first), ref) in enumerate(zip(pieces, parts)):
        if first + ref.shape[0] > proj_rows:
            g = jnp.bitwise_xor(group, n)
            start = pl.multiple_of(g * table_rows, table_rows)
            made = pltpu.make_async_copy(
                ref.at[pl.ds(proj_rows - first, table_rows)],
                table.at[pl.ds(start, table_rows)],
                sems.at[number],
            )
            made.start()
            table_copies.append(made)
    for number, ((n, first), ref) in enumerate(zip(pieces, parts)):
        count = min(ref.shape[0], proj_rows - first)
        made = pltpu.make_async_copy(
            ref.at[pl.ds(0, count)],
            proj.at[pl.ds(n * proj_rows + first, count)],
            sems.at[len(pieces) + number],
        )
        made.start()
        proj_copies.append(made)

    square_ref[...] = hold_blocks(blocks, here, gain_ref, held)
    codes = lax.broadcasted_iota(jnp.int32, (table.shape[0], tokens_ref.shape[1]), 0)
    matches = (tokens_ref[...] == codes).astype(f32).astype(bf16)
    for made in table_copies:
        made.wait()
    looked = lax.dot_general(
        matches, table[...], (((0,), (0,)), ((), ())), preferred_element_type=f32
    )
    looked_ref[...] = looked.astype(bf16)
    projected_ref[...] = jnp.zeros_like(projected_ref)
    for (n, first), made, ref in zip(pieces, proj_copies, parts):
        count = min(ref.shape[0], proj_rows - first)
        owner = jnp.bitwise_xor(group, n)
        book = owner // per_book
        start = pl.multiple_of((owner % per_book) * proj_rows + first, 128)
        made.wait()

        @pl.when(jnp.logical_not(is_late(jnp.bitwise_xor(here, book))))
        def _():
            projected_ref[...] += jnp.dot(
                held[book, :, pl.ds(start, count)],
                proj[pl.ds(n * proj_rows + first, count), :],
                preferred_element_type=f32,
            )


def project_early(tokens, gain, blocks, early, pieces, parts, sizes):
    books = len(blocks)
    frames_here, width = blocks[0].shape
    depth = parts[0].shape[1]
    proj_rows, table_rows, _ = sizes
    groups = books * width // proj_rows
    vmem = pl.BlockSpec(memory_space=pltpu.VMEM)
    return pl.pallas_call(
        functools.partial(early_kernel, books, early, pieces, sizes),
        out_shape=[
            jax.ShapeDtypeStruct((frames_here, depth), f32),
            jax.ShapeDtypeStruct((frames_here, 1), f32),
            jax.ShapeDtypeStruct((frames_here, depth), bf16),
        ],
        in_specs=[vmem] * (2 + len(early))
        + [pl.BlockSpec(memory_space=pl.ANY)] * len(parts),
        out_specs=[vmem] * 3,
        scratch_shapes=[
            pltpu.VMEM((books, frames_here, width), bf16),
            pltpu.VMEM((books * width, depth), bf16),
            pltpu.VMEM((groups * table_rows, depth), bf16),
            pltpu.SemaphoreType.DMA((2 * len(pieces),)),
        ],
        compiler_params=pltpu.CompilerParams(vmem_limit_bytes=50 * 2**20),
        cost_estimate=pl.CostEstimate(flops=0, bytes_accessed=0, transcendentals=0),
        name="early_products_and_lookup",
    )(tokens, gain, *[blocks[m] for m in early], *parts)


def late_kernel(books, late, pieces, sizes, gain_ref, *refs):
    blocks = dict(zip(late, refs))
    early_ref, square_ref, looked_ref, depth_gain_ref = refs[len(late) : len(late) + 4]
    refs = refs[len(late) + 4 :]
    parts = refs[: len(pieces)]
    outs = refs[len(pieces) : len(pieces) + books]
    held, proj, qkv, packed, sems = refs[len(pieces) + books :]
    proj_rows, table_rows, qkv_rows = sizes
    here, group = lax.axis_index("book"), lax.axis_index("frames")
    frames_here, width = held.shape[1:]
    per_book = width // proj_rows
    half = qkv_rows // 2
    depth = proj.shape[2]
    extra = qkv.shape[1] - depth

    proj_copies = []
    for number, ((n, first), ref) in enumerate(zip(pieces, parts)):
        count = min(ref.shape[0], proj_rows - first)
        owner = jnp.bitwise_xor(group, n)
        m = jnp.bitwise_xor(here, owner // per_book)
        start = pl.multiple_of((owner % per_book) * proj_rows + first, 128)
        slot = jnp.maximum(m // 2 - 1, 0)
        made = pltpu.make_async_copy(
            ref.at[pl.ds(0, count)], proj.at[slot, pl.ds(start, count)], sems.at[number]
        )
        pl.when(is_late(m))(made.start)
        proj_copies.append((is_late(m), made))
    qkv_copies = []

    def copy(source, target):
        made = pltpu.make_async_copy(source, target, sems.at[len(pieces) + len(qkv_copies)])
        made.start()
        qkv_copies.append(made)

    for (n, first), ref in zip(pieces, parts):
        if first + ref.shape[0] > proj_rows:
            g = jnp.bitwise_xor(group, n)
            at_qkv = proj_rows - first + table_rows
            start = pl.multiple_of(g * qkv_rows, qkv_rows)
            copy(
                ref.at[pl.ds(at_qkv, qkv_rows)], qkv.at[pl.ds(start, qkv_rows), pl.ds(0, depth)]
            )
            for side in range(2):
                start = pl.multiple_of(g * qkv_rows + side * half, half)
                copy(
                    ref.at[pl.ds(at_qkv + qkv_rows, half), pl.ds(side * extra, extra)],
                    qkv.at[pl.ds(start, half), pl.ds(depth, extra)],
                )

    square = square_ref[...] + hold_blocks(blocks, here, gain_ref, held)
    projected = early_ref[...]
    for late_here, made in proj_copies:
        pl.when(late_here)(made.wait)
    for slot, m in enumerate(late):
        projected = projected + jnp.dot(
            held[jnp.bitwise_xor(here, m)], proj[slot], preferred_element_type=f32
        )
    projected = projected * lax.rsqrt(square / (books * width) + 1e-05)
    depth_in = (projected + looked_ref[...].astype(f32)).astype(bf16).astype(f32)
    moment = jnp.mean(depth_in * depth_in, axis=-1, keepdims=True)
    depth_normed = depth_in * lax.rsqrt(moment + 1e-05) * depth_gain_ref[...].astype(f32)
    for made in qkv_copies:
        made.wait()
    packed[...] = jnp.dot(
        depth_normed.astype(bf16), qkv[...], preferred_element_type=f32
    ).astype(bf16)
    rows = frames_here // books
    for m in range(books):
        start = pl.multiple_of(jnp.bitwise_xor(here, m) * rows, rows)
        outs[m][...] = packed[pl.ds(start, rows), :]


def project_late(
    gain, blocks, late, projected, square, looked, depth_gain, pieces, parts, sizes, wide
):
    books = len(blocks)
    frames_here, width = blocks[0].shape
    depth = projected.shape[1]
    proj_rows, _, qkv_rows = sizes
    groups = books * width // proj_rows
    vmem = pl.BlockSpec(memory_space=pltpu.VMEM)
    return pl.pallas_call(
        functools.partial(late_kernel, books, late, pieces, sizes),
        out_shape=[jax.ShapeDtypeStruct((frames_here // books, wide), bf16)] * books,
        in_specs=[vmem] * (len(late) + 5)
        + [pl.BlockSpec(memory_space=pl.ANY)] * len(parts),
        out_specs=[vmem] * books,
        scratch_shapes=[
            pltpu.VMEM((books, frames_here, width), bf16),
            pltpu.VMEM((len(late), width, depth), bf16),
            pltpu.VMEM((groups * qkv_rows, wide), bf16),
            pltpu.VMEM((frames_here, wide), bf16),
            pltpu.SemaphoreType.DMA((len(pieces) + 3 * groups,)),
        ],
        compiler_params=pltpu.CompilerParams(vmem_limit_bytes=50 * 2**20),
        name="late_products_and_qkv",
    )(
        gain,
        *[blocks[m] for m in late],
        projected,
        square,
        looked,
        depth_gain,
        *parts,
    )


def attend_kernel(books, *refs):
    arrived = refs[:books]
    out_ref, inner = refs[books:]
    place = lax.axis_index("book")
    rows, wide = arrived[0].shape
    width = wide // 3
    for m in range(books):
        inner[jnp.bitwise_xor(place, m)] = arrived[m][...]
    head_of_row = lax.broadcasted_iota(jnp.int32, (width, width), 0) // HD
    head_of_column = lax.broadcasted_iota(jnp.int32, (width, width), 1) // HD
    same_head = (head_of_row == head_of_column).astype(f32).astype(bf16)
    keys_all = [inner[j, :, width : 2 * width].astype(f32) for j in range(books)]
    values_all = [inner[j, :, 2 * width :].astype(f32) for j in range(books)]
    contexts = []
    for k in range(books):
        query = inner[k, :, :width].astype(f32) * HD ** (-0.5)
        products = jnp.concatenate([query * keys_all[j] for j in range(k + 1)], axis=0)
        high = products.astype(bf16)
        low = (products - high.astype(f32)).astype(bf16)
        scores = jnp.dot(high, same_head, preferred_element_type=f32) + jnp.dot(
            low, same_head, preferred_element_type=f32
        )
        scores = [scores[j * rows : (j + 1) * rows] for j in range(k + 1)]
        peak = functools.reduce(jnp.maximum, scores)
        expo = [jnp.exp(score - peak) for score in scores]
        total = functools.reduce(jnp.add, expo)
        context = 0.0
        for j in range(k + 1):
            probability = (expo[j] / total).astype(bf16).astype(f32)
            context = context + probability * values_all[j]
        contexts.append(context)
    out_ref[...] = jnp.stack(contexts, axis=1).astype(bf16)


def attend(arrived):
    books = len(arrived)
    rows, wide = arrived[0].shape
    vmem = pl.BlockSpec(memory_space=pltpu.VMEM)
    return pl.pallas_call(
        functools.partial(attend_kernel, books),
        out_shape=jax.ShapeDtypeStruct((rows, books, wide // 3), bf16),
        in_specs=[vmem] * books,
        out_specs=vmem,
        scratch_shapes=[pltpu.VMEM((books, rows, wide), bf16)],
        compiler_params=pltpu.CompilerParams(vmem_limit_bytes=16 * 2**20),
        name="attend_books",
    )(*arrived)


def swap(value, axis, distance):
    return lax.ppermute(value, axis, [(i, i ^ distance) for i in range(lax.axis_size(axis))])


def after(value, *others):
    return lax.optimization_barrier((value, *others))[0]


def bits_of(number):
    return [1 << place for place in range(number.bit_length()) if number >> place & 1]


def per_device(
    gate_pre,
    up_pre,
    down_weight,
    residual,
    out_gain,
    in_proj,
    embedding,
    token_ids,
    depth_gain,
    qkv_weight,
):
    books = lax.axis_size("book")
    groups = lax.axis_size("frames")
    here = lax.axis_index("book").astype(jnp.int32)
    width = residual.shape[1]
    proj_rows = in_proj.shape[1]
    gain = out_gain[None]

    hidden, first = first_products(gate_pre, up_pre, down_weight, width)

    def share(m, *others):
        start = jnp.bitwise_xor(here, m) * width
        block = lax.dynamic_slice_in_dim(down_weight, start, width, 1)
        factor = after(hidden, *others) if others else hidden
        return jnp.dot(factor, block, preferred_element_type=f32)

    rows = pack(*after((in_proj[0], embedding[0], qkv_weight[0]), first))
    parts = {0: [(0, rows)]}
    near = [n for n in range(2, groups, 2) if len(bits_of(n)) == 1]
    for n in near:
        parts[n] = [(0, swap(rows, "frames", n))]

    sums = {books - 1: first}
    parts[1] = [(0, swap(rows, "frames", 1))]
    sums[books - 2] = lax.optimization_barrier(share(books - 2, rows))
    for n in range(books - 3, 0, -1):
        sums[n] = lax.optimization_barrier(share(n, parts[1][0][1]))
    distance = 1
    while distance < books:
        came = None
        for m in range(books - distance, 0, -2 * distance):
            going = sums.pop(m).astype(bf16)
            if came is not None:
                going = after(going, came, sums[m + distance])
            came = swap(going, "book", distance)
            if m == books - 1:
                came = after(came, *[sums[n] for n in range(1, books - 1)])
            sums[m ^ distance] = sums[m ^ distance] + came.astype(f32)
            if m == books - 1:
                sums[0] = lax.optimization_barrier(share(0, came))
                sums[0] = sums[0] + residual.astype(f32)
        distance *= 2

    blocks = {0: sums[0].astype(bf16)}

    arrived = after([parts[n][0][1] for n in near], blocks[0])
    for n, value in zip(near, arrived):
        parts[n] = [(0, value)]
    cut = rows.shape[0] // 2 // 128 * 128
    for n in range(2, groups, 2):
        sides = bits_of(n)
        if n in near:
            continue
        if len(sides) == 2 and 0 < cut < proj_rows:
            upper = swap(parts[n ^ sides[0]][0][1][:cut], "frames", sides[0])
            lower = swap(parts[n ^ sides[1]][0][1][cut:], "frames", sides[1])
            parts[n] = [(0, upper), (cut, lower)]
        else:
            parts[n] = [(0, swap(rows, "frames", n))]
    for n in range(2, groups, 2):
        parts[n + 1] = [(first, swap(value, "frames", 1)) for first, value in parts[n]]

    near_there = [parts[n + 1][0][1] for n in near]
    distance = books // 2
    while distance:
        for m in sorted(blocks):
            going = blocks[m]
            if m:
                going = after(going, blocks[distance])
            elif distance == 1:
                going = after(going, *near_there)
            blocks[m ^ distance] = swap(going, "book", distance)
        distance //= 2

    pieces = [(n, first) for n in range(groups) for first, _ in parts[n]]
    arrived = [value for n in range(groups) for _, value in parts[n]]
    sizes = proj_rows, embedding.shape[1], qkv_weight.shape[1]
    early = [m for m in range(books) if not is_late(m)]
    late = [m for m in range(books) if is_late(m)]
    projected, square, looked = project_early(
        token_ids.reshape(1, -1), gain, blocks, early, pieces, arrived, sizes
    )
    packed = project_late(
        gain,
        blocks,
        late,
        projected,
        square,
        looked,
        depth_gain,
        pieces,
        arrived,
        sizes,
        qkv_weight.shape[2],
    )
    far = {m: swap(packed[m], "book", m) for m in range(books - 1, 0, -1)}
    return attend([packed[0]] + [far[m] for m in range(1, books)])


def solution(mesh):
    in_specs = (
        P("frames", "book"),
        P("frames", "book"),
        P("book", None),
        P("frames", "book"),
        P(),
        P("book", "frames", None),
        P("book", "frames", None),
        P("frames", "book"),
        P("book", None),
        P("book", "frames", None),
    )
    out_specs = P(("frames", "book"), None, None)
    return jax.shard_map(
        per_device, mesh=mesh, in_specs=in_specs, out_specs=out_specs, check_vma=False
    )
```

```python
import functools

import jax
import jax.numpy as jnp
from jax import lax
from jax.experimental import pallas as pl
from jax.experimental.pallas import tpu as pltpu
from jax.sharding import PartitionSpec as P

H = 8
HD = 64
f32, bf16 = jnp.float32, jnp.bfloat16


def first_kernel(gate_ref, up_ref, down_ref, hidden_ref, first_ref, gates, ups, held, sems):
    steps, each, width = held.shape
    books = down_ref.shape[1] // width
    start = pl.multiple_of(jnp.bitwise_xor(lax.axis_index("book"), books - 1) * width, width)
    copies = []
    for step in range(steps):
        rows = pl.ds(step * each, each)
        moves = [
            (gate_ref.at[:, rows], gates.at[step]),
            (up_ref.at[:, rows], ups.at[step]),
            (down_ref.at[rows, pl.ds(start, width)], held.at[step]),
        ]
        for kind, (source, target) in enumerate(moves):
            copies.append(pltpu.make_async_copy(source, target, sems.at[3 * step + kind]))
            copies[-1].start()
    total = 0.0
    for step in range(steps):
        copies[3 * step].wait()
        copies[3 * step + 1].wait()
        gate = gates[step].astype(f32)
        hidden = gate / (1.0 + jnp.exp(-gate)) * ups[step].astype(f32)
        hidden = hidden.astype(bf16)
        hidden_ref[:, pl.ds(step * each, each)] = hidden
        copies[3 * step + 2].wait()
        total = total + jnp.dot(hidden, held[step], preferred_element_type=f32)
    first_ref[...] = total.astype(bf16)


def first_products(gate, up, down, width):
    frames_here, hidden_width = gate.shape
    steps = max(hidden_width // 512, 1)
    vmem = pl.BlockSpec(memory_space=pltpu.VMEM)
    return pl.pallas_call(
        first_kernel,
        out_shape=[
            jax.ShapeDtypeStruct((frames_here, hidden_width), bf16),
            jax.ShapeDtypeStruct((frames_here, width), bf16),
        ],
        in_specs=[pl.BlockSpec(memory_space=pl.ANY)] * 3,
        out_specs=[vmem] * 2,
        scratch_shapes=[
            pltpu.VMEM((steps, frames_here, hidden_width // steps), bf16),
            pltpu.VMEM((steps, frames_here, hidden_width // steps), bf16),
            pltpu.VMEM((steps, hidden_width // steps, width), bf16),
            pltpu.SemaphoreType.DMA((3 * steps,)),
        ],
        compiler_params=pltpu.CompilerParams(vmem_limit_bytes=53 * 2**20),
        cost_estimate=pl.CostEstimate(flops=0, bytes_accessed=0, transcendentals=0),
        name="hidden_and_first_products",
    )(gate, up, down)


def pack_kernel(proj_ref, table_ref, qkv_ref, packed_ref, sems):
    proj_rows, depth = proj_ref.shape
    table_rows = table_ref.shape[0]
    qkv_rows, wide = qkv_ref.shape
    half, extra = qkv_rows // 2, wide - depth
    at_qkv = proj_rows + table_rows
    at_extra = at_qkv + qkv_rows
    moves = [
        (proj_ref, packed_ref.at[pl.ds(0, proj_rows)]),
        (table_ref, packed_ref.at[pl.ds(proj_rows, table_rows)]),
        (qkv_ref.at[:, pl.ds(0, depth)], packed_ref.at[pl.ds(at_qkv, qkv_rows)]),
    ]
    for side in range(2):
        moves.append(
            (
                qkv_ref.at[pl.ds(side * half, half), pl.ds(depth, extra)],
                packed_ref.at[pl.ds(at_extra, half), pl.ds(side * extra, extra)],
            )
        )
    copies = [
        pltpu.make_async_copy(source, target, sems.at[number])
        for number, (source, target) in enumerate(moves)
    ]
    for made in copies:
        made.start()
    for made in copies:
        made.wait()


def pack(proj, table, qkv):
    depth = proj.shape[1]
    rows = proj.shape[0] + table.shape[0] + qkv.shape[0] + qkv.shape[0] // 2
    return pl.pallas_call(
        pack_kernel,
        out_shape=jax.ShapeDtypeStruct((rows, depth), bf16),
        in_specs=[pl.BlockSpec(memory_space=pl.ANY)] * 3,
        out_specs=pl.BlockSpec(memory_space=pltpu.VMEM),
        scratch_shapes=[pltpu.SemaphoreType.DMA((5,))],
        compiler_params=pltpu.CompilerParams(vmem_limit_bytes=4 * 2**20),
        name="pack_weight_rows",
    )(proj, table, qkv)


def cut_kernel(cut, upper_from, lower_from, upper_ref, lower_ref, sems):
    upper = pltpu.make_async_copy(upper_from.at[pl.ds(0, cut)], upper_ref, sems.at[0])
    lower = pltpu.make_async_copy(
        lower_from.at[pl.ds(cut, lower_ref.shape[0])], lower_ref, sems.at[1]
    )
    upper.start()
    lower.start()
    upper.wait()
    lower.wait()


def cut_rows(upper_from, lower_from, cut):
    rows, depth = upper_from.shape
    return pl.pallas_call(
        functools.partial(cut_kernel, cut),
        out_shape=[
            jax.ShapeDtypeStruct((cut, depth), bf16),
            jax.ShapeDtypeStruct((rows - cut, depth), bf16),
        ],
        in_specs=[pl.BlockSpec(memory_space=pl.ANY)] * 2,
        out_specs=[pl.BlockSpec(memory_space=pl.ANY)] * 2,
        scratch_shapes=[pltpu.SemaphoreType.DMA((2,))],
        name="cut_rows",
    )(upper_from, lower_from)


def is_late(m):
    return (m % 2 == 1) & (m != 1)


def hold_blocks(blocks, here, gain_ref, held, square_ref):
    for m, pieces in blocks.items():
        book = jnp.bitwise_xor(here, m)
        width = held.shape[2]
        columns = pl.ds(pl.multiple_of(book * width, width), width)
        gain = gain_ref[:, columns].astype(f32)
        row = 0
        for ref in pieces:
            rows = pl.ds(row, ref.shape[0])
            row += ref.shape[0]
            part = ref[...].astype(f32)
            square_ref[rows, :] += jnp.sum(part * part, axis=-1, keepdims=True)
            held[book, rows, :] = (part * gain).astype(bf16)


def with_refs(counts, refs):
    blocks, at = {}, 0
    for m, count in counts:
        blocks[m] = refs[at : at + count]
        at += count
    return blocks, refs[at:]


def early_kernel(books, counts, pieces, sizes, tokens_ref, gain_ref, *refs):
    blocks, refs = with_refs(counts, refs)
    parts = refs[: len(pieces)]
    projected_ref, square_ref, looked_ref, held, proj, table, sems = refs[len(pieces) :]
    proj_rows, table_rows, _ = sizes
    here, group = lax.axis_index("book"), lax.axis_index("frames")
    per_book = held.shape[2] // proj_rows

    table_copies, proj_copies = [], []
    for number, ((n, first), ref) in enumerate(zip(pieces, parts)):
        if first + ref.shape[0] > proj_rows:
            g = jnp.bitwise_xor(group, n)
            start = pl.multiple_of(g * table_rows, table_rows)
            made = pltpu.make_async_copy(
                ref.at[pl.ds(proj_rows - first, table_rows)],
                table.at[pl.ds(start, table_rows)],
                sems.at[number],
            )
            made.start()
            table_copies.append(made)
    for number, ((n, first), ref) in enumerate(zip(pieces, parts)):
        count = min(ref.shape[0], proj_rows - first)
        made = pltpu.make_async_copy(
            ref.at[pl.ds(0, count)],
            proj.at[pl.ds(n * proj_rows + first, count)],
            sems.at[len(pieces) + number],
        )
        made.start()
        proj_copies.append(made)

    square_ref[...] = jnp.zeros_like(square_ref)
    hold_blocks(blocks, here, gain_ref, held, square_ref)
    codes = lax.broadcasted_iota(jnp.int32, (table.shape[0], tokens_ref.shape[1]), 0)
    matches = (tokens_ref[...] == codes).astype(f32).astype(bf16)
    for made in table_copies:
        made.wait()
    looked = lax.dot_general(
        matches, table[...], (((0,), (0,)), ((), ())), preferred_element_type=f32
    )
    looked_ref[...] = looked.astype(bf16)
    projected_ref[...] = jnp.zeros_like(projected_ref)
    for (n, first), made, ref in zip(pieces, proj_copies, parts):
        count = min(ref.shape[0], proj_rows - first)
        owner = jnp.bitwise_xor(group, n)
        book = owner // per_book
        start = pl.multiple_of((owner % per_book) * proj_rows + first, 128)
        made.wait()

        @pl.when(jnp.logical_not(is_late(jnp.bitwise_xor(here, book))))
        def _():
            projected_ref[...] += jnp.dot(
                held[book, :, pl.ds(start, count)],
                proj[pl.ds(n * proj_rows + first, count), :],
                preferred_element_type=f32,
            )


def project_early(tokens, gain, blocks, early, pieces, parts, sizes):
    books = len(blocks)
    frames_here, width = blocks[0][0].shape
    counts = [(m, len(blocks[m])) for m in early]
    given = [piece for m in early for piece in blocks[m]]
    depth = parts[0].shape[1]
    proj_rows, table_rows, _ = sizes
    groups = books * width // proj_rows
    vmem = pl.BlockSpec(memory_space=pltpu.VMEM)
    return pl.pallas_call(
        functools.partial(early_kernel, books, counts, pieces, sizes),
        out_shape=[
            jax.ShapeDtypeStruct((frames_here, depth), f32),
            jax.ShapeDtypeStruct((frames_here, 1), f32),
            jax.ShapeDtypeStruct((frames_here, depth), bf16),
        ],
        in_specs=[vmem] * (2 + len(given))
        + [pl.BlockSpec(memory_space=pl.ANY)] * len(parts),
        out_specs=[vmem] * 3,
        scratch_shapes=[
            pltpu.VMEM((books, frames_here, width), bf16),
            pltpu.VMEM((books * width, depth), bf16),
            pltpu.VMEM((groups * table_rows, depth), bf16),
            pltpu.SemaphoreType.DMA((2 * len(pieces),)),
        ],
        compiler_params=pltpu.CompilerParams(vmem_limit_bytes=50 * 2**20),
        cost_estimate=pl.CostEstimate(flops=0, bytes_accessed=0, transcendentals=0),
        name="early_products_and_lookup",
    )(tokens, gain, *given, *parts)


def late_kernel(books, counts, pieces, sizes, gain_ref, *refs):
    blocks, refs = with_refs(counts, refs)
    early_ref, square_ref, looked_ref, depth_gain_ref = refs[:4]
    parts = refs[4 : len(pieces) + 4]
    refs = refs[len(pieces) + 4 :]
    outs = refs[:books]
    held, proj, qkv, packed, squares, sems = refs[books:]
    proj_rows, table_rows, qkv_rows = sizes
    here, group = lax.axis_index("book"), lax.axis_index("frames")
    frames_here, width = held.shape[1:]
    per_book = width // proj_rows
    half = qkv_rows // 2
    depth = proj.shape[2]
    extra = qkv.shape[1] - depth

    proj_copies = []
    for number, ((n, first), ref) in enumerate(zip(pieces, parts)):
        count = min(ref.shape[0], proj_rows - first)
        owner = jnp.bitwise_xor(group, n)
        m = jnp.bitwise_xor(here, owner // per_book)
        start = pl.multiple_of((owner % per_book) * proj_rows + first, 128)
        slot = jnp.maximum(m // 2 - 1, 0)
        made = pltpu.make_async_copy(
            ref.at[pl.ds(0, count)], proj.at[slot, pl.ds(start, count)], sems.at[number]
        )
        pl.when(is_late(m))(made.start)
        proj_copies.append((is_late(m), made))
    qkv_copies = []

    def copy(source, target):
        made = pltpu.make_async_copy(source, target, sems.at[len(pieces) + len(qkv_copies)])
        made.start()
        qkv_copies.append(made)

    for (n, first), ref in zip(pieces, parts):
        if first + ref.shape[0] > proj_rows:
            g = jnp.bitwise_xor(group, n)
            at_qkv = proj_rows - first + table_rows
            start = pl.multiple_of(g * qkv_rows, qkv_rows)
            copy(
                ref.at[pl.ds(at_qkv, qkv_rows)], qkv.at[pl.ds(start, qkv_rows), pl.ds(0, depth)]
            )
            for side in range(2):
                start = pl.multiple_of(g * qkv_rows + side * half, half)
                copy(
                    ref.at[pl.ds(at_qkv + qkv_rows, half), pl.ds(side * extra, extra)],
                    qkv.at[pl.ds(start, half), pl.ds(depth, extra)],
                )

    squares[...] = square_ref[...]
    hold_blocks(blocks, here, gain_ref, held, squares)
    square = squares[...]
    projected = early_ref[...]
    for late_here, made in proj_copies:
        pl.when(late_here)(made.wait)
    for slot, (m, _) in enumerate(counts):
        projected = projected + jnp.dot(
            held[jnp.bitwise_xor(here, m)], proj[slot], preferred_element_type=f32
        )
    projected = projected * lax.rsqrt(square / (books * width) + 1e-05)
    depth_in = (projected + looked_ref[...].astype(f32)).astype(bf16).astype(f32)
    moment = jnp.mean(depth_in * depth_in, axis=-1, keepdims=True)
    depth_normed = depth_in * lax.rsqrt(moment + 1e-05) * depth_gain_ref[...].astype(f32)
    for made in qkv_copies:
        made.wait()
    packed[...] = jnp.dot(
        depth_normed.astype(bf16), qkv[...], preferred_element_type=f32
    ).astype(bf16)
    rows = frames_here // books
    for m in range(books):
        start = pl.multiple_of(jnp.bitwise_xor(here, m) * rows, rows)
        outs[m][...] = packed[pl.ds(start, rows), :]


def project_late(
    gain, blocks, late, projected, square, looked, depth_gain, pieces, parts, sizes, wide
):
    books = len(blocks)
    frames_here, width = blocks[0][0].shape
    counts = [(m, len(blocks[m])) for m in late]
    given = [piece for m in late for piece in blocks[m]]
    depth = projected.shape[1]
    proj_rows, _, qkv_rows = sizes
    groups = books * width // proj_rows
    vmem = pl.BlockSpec(memory_space=pltpu.VMEM)
    return pl.pallas_call(
        functools.partial(late_kernel, books, counts, pieces, sizes),
        out_shape=[jax.ShapeDtypeStruct((frames_here // books, wide), bf16)] * books,
        in_specs=[vmem] * (len(given) + 5)
        + [pl.BlockSpec(memory_space=pl.ANY)] * len(parts),
        out_specs=[vmem] * books,
        scratch_shapes=[
            pltpu.VMEM((books, frames_here, width), bf16),
            pltpu.VMEM((len(late), width, depth), bf16),
            pltpu.VMEM((groups * qkv_rows, wide), bf16),
            pltpu.VMEM((frames_here, wide), bf16),
            pltpu.VMEM((frames_here, 1), f32),
            pltpu.SemaphoreType.DMA((len(pieces) + 3 * groups,)),
        ],
        compiler_params=pltpu.CompilerParams(vmem_limit_bytes=50 * 2**20),
        name="late_products_and_qkv",
    )(
        gain,
        *given,
        projected,
        square,
        looked,
        depth_gain,
        *parts,
    )


def attend_kernel(books, *refs):
    arrived = refs[:books]
    out_ref, inner = refs[books:]
    place = lax.axis_index("book")
    rows, wide = arrived[0].shape
    width = wide // 3
    for m in range(books):
        inner[jnp.bitwise_xor(place, m)] = arrived[m][...]
    head_of_row = lax.broadcasted_iota(jnp.int32, (width, width), 0) // HD
    head_of_column = lax.broadcasted_iota(jnp.int32, (width, width), 1) // HD
    same_head = (head_of_row == head_of_column).astype(f32).astype(bf16)
    keys_all = [inner[j, :, width : 2 * width].astype(f32) for j in range(books)]
    values_all = [inner[j, :, 2 * width :].astype(f32) for j in range(books)]
    contexts = []
    for k in range(books):
        query = inner[k, :, :width].astype(f32) * HD ** (-0.5)
        products = jnp.concatenate([query * keys_all[j] for j in range(k + 1)], axis=0)
        high = products.astype(bf16)
        low = (products - high.astype(f32)).astype(bf16)
        scores = jnp.dot(high, same_head, preferred_element_type=f32) + jnp.dot(
            low, same_head, preferred_element_type=f32
        )
        scores = [scores[j * rows : (j + 1) * rows] for j in range(k + 1)]
        peak = functools.reduce(jnp.maximum, scores)
        expo = [jnp.exp(score - peak) for score in scores]
        total = functools.reduce(jnp.add, expo)
        context = 0.0
        for j in range(k + 1):
            probability = (expo[j] / total).astype(bf16).astype(f32)
            context = context + probability * values_all[j]
        contexts.append(context)
    out_ref[...] = jnp.stack(contexts, axis=1).astype(bf16)


def attend(arrived):
    books = len(arrived)
    rows, wide = arrived[0].shape
    vmem = pl.BlockSpec(memory_space=pltpu.VMEM)
    return pl.pallas_call(
        functools.partial(attend_kernel, books),
        out_shape=jax.ShapeDtypeStruct((rows, books, wide // 3), bf16),
        in_specs=[vmem] * books,
        out_specs=vmem,
        scratch_shapes=[pltpu.VMEM((books, rows, wide), bf16)],
        compiler_params=pltpu.CompilerParams(vmem_limit_bytes=16 * 2**20),
        name="attend_books",
    )(*arrived)


def swap(value, axis, distance):
    return lax.ppermute(value, axis, [(i, i ^ distance) for i in range(lax.axis_size(axis))])


def after(value, *others):
    return lax.optimization_barrier((value, *others))[0]


def halves(value):
    rows = value.shape[0] * 3 // 8 // 16 * 16
    return [value[:rows], value[rows:]]


def bits_of(number):
    return [1 << place for place in range(number.bit_length()) if number >> place & 1]


def per_device(
    gate_pre,
    up_pre,
    down_weight,
    residual,
    out_gain,
    in_proj,
    embedding,
    token_ids,
    depth_gain,
    qkv_weight,
):
    books = lax.axis_size("book")
    groups = lax.axis_size("frames")
    here = lax.axis_index("book").astype(jnp.int32)
    width = residual.shape[1]
    proj_rows = in_proj.shape[1]
    gain = out_gain[None]

    rows = pack(in_proj[0], embedding[0], qkv_weight[0])
    parts = {0: [(0, rows)]}
    near = [n for n in range(2, groups, 2) if len(bits_of(n)) == 1]
    for n in near:
        parts[n] = [(0, swap(rows, "frames", n))]
    parts[1] = [(0, swap(rows, "frames", 1))]

    hidden, first = first_products(after(gate_pre, rows), up_pre, down_weight, width)

    def share(m, *others):
        start = jnp.bitwise_xor(here, m) * width
        block = lax.dynamic_slice_in_dim(down_weight, start, width, 1)
        factor = after(hidden, *others) if others else hidden
        return jnp.dot(factor, block, preferred_element_type=f32)

    sums = {books - 1: first, books - 2: lax.optimization_barrier(share(books - 2))}
    for n in range(books - 3, 0, -1):
        sums[n] = lax.optimization_barrier(share(n, parts[1][0][1]))
    sums = {m: halves(value) for m, value in sums.items()}
    distance = 1
    while distance < books:
        came = None
        for m in range(books - distance, 0, -2 * distance):
            going = [half.astype(bf16) for half in sums.pop(m)]
            if came is None:
                came = [swap(half, "book", distance) for half in going]
                midway = [came[0], going[1]] + sums.get(0, [])
            else:
                whole = after(jnp.concatenate(going, axis=0), came[0], sums[m + distance][0])
                came = halves(swap(whole, "book", distance))
            if m == books - 1:
                first_came = came[0]
                came[0] = after(came[0], *[sums[n][0] for n in range(1, books - 1)])
            sums[m ^ distance] = [
                kept + half.astype(f32) for kept, half in zip(sums[m ^ distance], came)
            ]
            if m == books - 1:
                sums[0] = halves(
                    lax.optimization_barrier(share(0, first_came)) + residual.astype(f32)
                )
        distance *= 2
    own = jnp.concatenate([half.astype(bf16) for half in sums[0]], axis=0)

    arrived = after([parts[n][0][1] for n in near], *midway)
    for n, value in zip(near, arrived):
        parts[n] = [(0, value)]
    cut = rows.shape[0] // 2 // 128 * 128
    for n in range(2, groups, 2):
        sides = bits_of(n)
        if n in near:
            continue
        if len(sides) == 2 and 0 < cut < proj_rows:
            upper, lower = cut_rows(parts[n ^ sides[0]][0][1], parts[n ^ sides[1]][0][1], cut)
            upper = swap(upper, "frames", sides[0])
            lower = swap(lower, "frames", sides[1])
            parts[n] = [(0, upper), (cut, lower)]
        else:
            parts[n] = [(0, swap(rows, "frames", n))]
    for n in near:
        parts[n + 1] = [(0, swap(parts[n][0][1], "frames", 1))]

    near_there = [parts[n + 1][0][1] for n in near]
    blocks = {0: [own]}
    distance = books // 2
    while distance:
        for m in sorted(blocks):
            going = blocks[m]
            if m == 0:
                going = [after(own, *near_there)] if distance == 1 else halves(own)
            blocks[m ^ distance] = [swap(piece, "book", distance) for piece in going]
        distance //= 2

    through = blocks[1] + blocks[books // 2] + blocks[books - 1][:1]
    for n in range(2, groups, 2):
        if n not in near:
            parts[n + 1] = [
                (first, swap(after(value, *through), "frames", 1))
                for first, value in parts[n]
            ]

    pieces = [(n, first) for n in range(groups) for first, _ in parts[n]]
    arrived = [value for n in range(groups) for _, value in parts[n]]
    sizes = proj_rows, embedding.shape[1], qkv_weight.shape[1]
    early = [m for m in range(books) if not is_late(m)]
    late = [m for m in range(books) if is_late(m)]
    projected, square, looked = project_early(
        token_ids.reshape(1, -1), gain, blocks, early, pieces, arrived, sizes
    )
    packed = project_late(
        gain,
        blocks,
        late,
        projected,
        square,
        looked,
        depth_gain,
        pieces,
        arrived,
        sizes,
        qkv_weight.shape[2],
    )
    far = {m: swap(packed[m], "book", m) for m in range(books - 1, 0, -1)}
    return attend([packed[0]] + [far[m] for m in range(1, books)])


def solution(mesh):
    in_specs = (
        P("frames", "book"),
        P("frames", "book"),
        P("book", None),
        P("frames", "book"),
        P(),
        P("book", "frames", None),
        P("book", "frames", None),
        P("frames", "book"),
        P("book", None),
        P("book", "frames", None),
    )
    out_specs = P(("frames", "book"), None, None)
    return jax.shard_map(
        per_device, mesh=mesh, in_specs=in_specs, out_specs=out_specs, check_vma=False
    )
```

```python
import functools

import jax
import jax.numpy as jnp
from jax import lax
from jax.experimental import pallas as pl
from jax.experimental.pallas import tpu as pltpu
from jax.sharding import PartitionSpec as P

H = 8
HD = 64
f32, bf16 = jnp.float32, jnp.bfloat16


def first_kernel(gate_ref, up_ref, down_ref, hidden_ref, first_ref, gates, ups, held, sems):
    steps, each, width = held.shape
    books = down_ref.shape[1] // width
    start = pl.multiple_of(jnp.bitwise_xor(lax.axis_index("book"), books - 1) * width, width)
    copies = []
    for step in range(steps):
        rows = pl.ds(step * each, each)
        moves = [
            (gate_ref.at[:, rows], gates.at[step]),
            (up_ref.at[:, rows], ups.at[step]),
            (down_ref.at[rows, pl.ds(start, width)], held.at[step]),
        ]
        for kind, (source, target) in enumerate(moves):
            copies.append(pltpu.make_async_copy(source, target, sems.at[3 * step + kind]))
            copies[-1].start()
    total = 0.0
    for step in range(steps):
        copies[3 * step].wait()
        copies[3 * step + 1].wait()
        gate = gates[step].astype(f32)
        hidden = gate / (1.0 + jnp.exp(-gate)) * ups[step].astype(f32)
        hidden = hidden.astype(bf16)
        hidden_ref[:, pl.ds(step * each, each)] = hidden
        copies[3 * step + 2].wait()
        total = total + jnp.dot(hidden, held[step], preferred_element_type=f32)
    first_ref[...] = total.astype(bf16)


def first_products(gate, up, down, width):
    frames_here, hidden_width = gate.shape
    steps = max(hidden_width // 512, 1)
    vmem = pl.BlockSpec(memory_space=pltpu.VMEM)
    return pl.pallas_call(
        first_kernel,
        out_shape=[
            jax.ShapeDtypeStruct((frames_here, hidden_width), bf16),
            jax.ShapeDtypeStruct((frames_here, width), bf16),
        ],
        in_specs=[pl.BlockSpec(memory_space=pl.ANY)] * 3,
        out_specs=[vmem] * 2,
        scratch_shapes=[
            pltpu.VMEM((steps, frames_here, hidden_width // steps), bf16),
            pltpu.VMEM((steps, frames_here, hidden_width // steps), bf16),
            pltpu.VMEM((steps, hidden_width // steps, width), bf16),
            pltpu.SemaphoreType.DMA((3 * steps,)),
        ],
        compiler_params=pltpu.CompilerParams(vmem_limit_bytes=53 * 2**20),
        name="hidden_and_first_products",
    )(gate, up, down)


def share_kernel(partner, hidden_ref, down_ref, out_ref, held, sems):
    steps, each, width = held.shape
    start = pl.multiple_of(jnp.bitwise_xor(lax.axis_index("book"), partner) * width, width)
    copies = []
    for step in range(steps):
        rows = pl.ds(step * each, each)
        copies.append(
            pltpu.make_async_copy(
                down_ref.at[rows, pl.ds(start, width)], held.at[step], sems.at[step]
            )
        )
        copies[-1].start()
    total = 0.0
    for step in range(steps):
        copies[step].wait()
        total = total + jnp.dot(
            hidden_ref[:, pl.ds(step * each, each)], held[step], preferred_element_type=f32
        )
    out_ref[...] = total


def share_products(hidden, down, width, partner):
    frames_here, hidden_width = hidden.shape
    steps = max(hidden_width // 512, 1)
    vmem = pl.BlockSpec(memory_space=pltpu.VMEM)
    return pl.pallas_call(
        functools.partial(share_kernel, partner),
        out_shape=jax.ShapeDtypeStruct((frames_here, width), f32),
        in_specs=[vmem, pl.BlockSpec(memory_space=pl.ANY)],
        out_specs=vmem,
        scratch_shapes=[
            pltpu.VMEM((steps, hidden_width // steps, width), bf16),
            pltpu.SemaphoreType.DMA((steps,)),
        ],
        compiler_params=pltpu.CompilerParams(vmem_limit_bytes=53 * 2**20),
        name="share_products",
    )(hidden, down)


def pack_kernel(proj_ref, table_ref, qkv_ref, packed_ref, sems):
    proj_rows, depth = proj_ref.shape
    table_rows = table_ref.shape[0]
    qkv_rows, wide = qkv_ref.shape
    half, extra = qkv_rows // 2, wide - depth
    at_qkv = proj_rows + table_rows
    at_extra = at_qkv + qkv_rows
    moves = [
        (proj_ref, packed_ref.at[pl.ds(0, proj_rows)]),
        (table_ref, packed_ref.at[pl.ds(proj_rows, table_rows)]),
        (qkv_ref.at[:, pl.ds(0, depth)], packed_ref.at[pl.ds(at_qkv, qkv_rows)]),
    ]
    for side in range(2):
        moves.append(
            (
                qkv_ref.at[pl.ds(side * half, half), pl.ds(depth, extra)],
                packed_ref.at[pl.ds(at_extra, half), pl.ds(side * extra, extra)],
            )
        )
    copies = [
        pltpu.make_async_copy(source, target, sems.at[number])
        for number, (source, target) in enumerate(moves)
    ]
    for made in copies:
        made.start()
    for made in copies:
        made.wait()


def pack(proj, table, qkv):
    depth = proj.shape[1]
    rows = proj.shape[0] + table.shape[0] + qkv.shape[0] + qkv.shape[0] // 2
    return pl.pallas_call(
        pack_kernel,
        out_shape=jax.ShapeDtypeStruct((rows, depth), bf16),
        in_specs=[pl.BlockSpec(memory_space=pl.ANY)] * 3,
        out_specs=pl.BlockSpec(memory_space=pltpu.VMEM),
        scratch_shapes=[pltpu.SemaphoreType.DMA((5,))],
        compiler_params=pltpu.CompilerParams(vmem_limit_bytes=4 * 2**20),
        name="pack_weight_rows",
    )(proj, table, qkv)


def cut_kernel(cut, upper_from, lower_from, upper_ref, lower_ref, sems):
    upper = pltpu.make_async_copy(upper_from.at[pl.ds(0, cut)], upper_ref, sems.at[0])
    lower = pltpu.make_async_copy(
        lower_from.at[pl.ds(cut, lower_ref.shape[0])], lower_ref, sems.at[1]
    )
    upper.start()
    lower.start()
    upper.wait()
    lower.wait()


def cut_rows(upper_from, lower_from, cut):
    rows, depth = upper_from.shape
    return pl.pallas_call(
        functools.partial(cut_kernel, cut),
        out_shape=[
            jax.ShapeDtypeStruct((cut, depth), bf16),
            jax.ShapeDtypeStruct((rows - cut, depth), bf16),
        ],
        in_specs=[pl.BlockSpec(memory_space=pl.ANY)] * 2,
        out_specs=[pl.BlockSpec(memory_space=pltpu.VMEM)] * 2,
        scratch_shapes=[pltpu.SemaphoreType.DMA((2,))],
        name="cut_rows",
    )(upper_from, lower_from)


def is_late(m):
    return (m % 2 == 1) & (m != 1)


def hold_blocks(blocks, here, gain_ref, held):
    square = 0.0
    for m, ref in blocks.items():
        book = jnp.bitwise_xor(here, m)
        part = ref[...].astype(f32)
        square = square + jnp.sum(part * part, axis=-1, keepdims=True)
        width = part.shape[1]
        columns = pl.ds(pl.multiple_of(book * width, width), width)
        held[book] = (part * gain_ref[:, columns].astype(f32)).astype(bf16)
    return square


def early_kernel(books, early, pieces, sizes, tokens_ref, gain_ref, *refs):
    blocks = dict(zip(early, refs))
    parts = refs[len(early) : len(early) + len(pieces)]
    projected_ref, square_ref, looked_ref, held, proj, table, sems = refs[
        len(early) + len(pieces) :
    ]
    proj_rows, table_rows, _ = sizes
    here, group = lax.axis_index("book"), lax.axis_index("frames")
    per_book = held.shape[2] // proj_rows

    table_copies, proj_copies = [], []
    for number, ((n, first), ref) in enumerate(zip(pieces, parts)):
        if first + ref.shape[0] > proj_rows:
            g = jnp.bitwise_xor(group, n)
            start = pl.multiple_of(g * table_rows, table_rows)
            made = pltpu.make_async_copy(
                ref.at[pl.ds(proj_rows - first, table_rows)],
                table.at[pl.ds(start, table_rows)],
                sems.at[number],
            )
            made.start()
            table_copies.append(made)
    for number, ((n, first), ref) in enumerate(zip(pieces, parts)):
        count = min(ref.shape[0], proj_rows - first)
        made = pltpu.make_async_copy(
            ref.at[pl.ds(0, count)],
            proj.at[pl.ds(n * proj_rows + first, count)],
            sems.at[len(pieces) + number],
        )
        made.start()
        proj_copies.append(made)

    square_ref[...] = hold_blocks(blocks, here, gain_ref, held)
    codes = lax.broadcasted_iota(jnp.int32, (table.shape[0], tokens_ref.shape[1]), 0)
    matches = (tokens_ref[...] == codes).astype(f32).astype(bf16)
    for made in table_copies:
        made.wait()
    looked = lax.dot_general(
        matches, table[...], (((0,), (0,)), ((), ())), preferred_element_type=f32
    )
    looked_ref[...] = looked.astype(bf16)
    projected_ref[...] = jnp.zeros_like(projected_ref)
    for (n, first), made, ref in zip(pieces, proj_copies, parts):
        count = min(ref.shape[0], proj_rows - first)
        owner = jnp.bitwise_xor(group, n)
        book = owner // per_book
        start = pl.multiple_of((owner % per_book) * proj_rows + first, 128)
        made.wait()

        @pl.when(jnp.logical_not(is_late(jnp.bitwise_xor(here, book))))
        def _():
            projected_ref[...] += jnp.dot(
                held[book, :, pl.ds(start, count)],
                proj[pl.ds(n * proj_rows + first, count), :],
                preferred_element_type=f32,
            )


def project_early(tokens, gain, blocks, early, pieces, parts, sizes):
    books = len(blocks)
    frames_here, width = blocks[0].shape
    depth = parts[0].shape[1]
    proj_rows, table_rows, _ = sizes
    groups = books * width // proj_rows
    vmem = pl.BlockSpec(memory_space=pltpu.VMEM)
    return pl.pallas_call(
        functools.partial(early_kernel, books, early, pieces, sizes),
        out_shape=[
            jax.ShapeDtypeStruct((frames_here, depth), f32),
            jax.ShapeDtypeStruct((frames_here, 1), f32),
            jax.ShapeDtypeStruct((frames_here, depth), bf16),
        ],
        in_specs=[vmem] * (2 + len(early))
        + [pl.BlockSpec(memory_space=pl.ANY)] * len(parts),
        out_specs=[vmem] * 3,
        scratch_shapes=[
            pltpu.VMEM((books, frames_here, width), bf16),
            pltpu.VMEM((books * width, depth), bf16),
            pltpu.VMEM((groups * table_rows, depth), bf16),
            pltpu.SemaphoreType.DMA((2 * len(pieces),)),
        ],
        compiler_params=pltpu.CompilerParams(vmem_limit_bytes=50 * 2**20),
        name="early_products_and_lookup",
    )(tokens, gain, *[blocks[m] for m in early], *parts)


def late_kernel(books, late, pieces, sizes, gain_ref, *refs):
    blocks = dict(zip(late, refs))
    early_ref, square_ref, looked_ref, depth_gain_ref = refs[len(late) : len(late) + 4]
    refs = refs[len(late) + 4 :]
    parts = refs[: len(pieces)]
    outs = refs[len(pieces) : len(pieces) + books]
    held, proj, qkv, packed, sems = refs[len(pieces) + books :]
    proj_rows, table_rows, qkv_rows = sizes
    here, group = lax.axis_index("book"), lax.axis_index("frames")
    frames_here, width = held.shape[1:]
    per_book = width // proj_rows
    half = qkv_rows // 2
    depth = proj.shape[2]
    extra = qkv.shape[1] - depth

    proj_copies = []
    for number, ((n, first), ref) in enumerate(zip(pieces, parts)):
        count = min(ref.shape[0], proj_rows - first)
        owner = jnp.bitwise_xor(group, n)
        m = jnp.bitwise_xor(here, owner // per_book)
        start = pl.multiple_of((owner % per_book) * proj_rows + first, 128)
        slot = jnp.maximum(m // 2 - 1, 0)
        made = pltpu.make_async_copy(
            ref.at[pl.ds(0, count)], proj.at[slot, pl.ds(start, count)], sems.at[number]
        )
        pl.when(is_late(m))(made.start)
        proj_copies.append((is_late(m), made))
    qkv_copies = []

    def copy(source, target):
        made = pltpu.make_async_copy(source, target, sems.at[len(pieces) + len(qkv_copies)])
        made.start()
        qkv_copies.append(made)

    for (n, first), ref in zip(pieces, parts):
        if first + ref.shape[0] > proj_rows:
            g = jnp.bitwise_xor(group, n)
            at_qkv = proj_rows - first + table_rows
            start = pl.multiple_of(g * qkv_rows, qkv_rows)
            copy(
                ref.at[pl.ds(at_qkv, qkv_rows)], qkv.at[pl.ds(start, qkv_rows), pl.ds(0, depth)]
            )
            for side in range(2):
                start = pl.multiple_of(g * qkv_rows + side * half, half)
                copy(
                    ref.at[pl.ds(at_qkv + qkv_rows, half), pl.ds(side * extra, extra)],
                    qkv.at[pl.ds(start, half), pl.ds(depth, extra)],
                )

    square = square_ref[...] + hold_blocks(blocks, here, gain_ref, held)
    projected = early_ref[...]
    for late_here, made in proj_copies:
        pl.when(late_here)(made.wait)
    for slot, m in enumerate(late):
        projected = projected + jnp.dot(
            held[jnp.bitwise_xor(here, m)], proj[slot], preferred_element_type=f32
        )
    projected = projected * lax.rsqrt(square / (books * width) + 1e-05)
    depth_in = (projected + looked_ref[...].astype(f32)).astype(bf16).astype(f32)
    moment = jnp.mean(depth_in * depth_in, axis=-1, keepdims=True)
    depth_normed = depth_in * lax.rsqrt(moment + 1e-05) * depth_gain_ref[...].astype(f32)
    for made in qkv_copies:
        made.wait()
    packed[...] = jnp.dot(
        depth_normed.astype(bf16), qkv[...], preferred_element_type=f32
    ).astype(bf16)
    rows = frames_here // books
    for m in range(books):
        start = pl.multiple_of(jnp.bitwise_xor(here, m) * rows, rows)
        outs[m][...] = packed[pl.ds(start, rows), :]


def project_late(
    gain, blocks, late, projected, square, looked, depth_gain, pieces, parts, sizes, wide
):
    books = len(blocks)
    frames_here, width = blocks[0].shape
    depth = projected.shape[1]
    proj_rows, _, qkv_rows = sizes
    groups = books * width // proj_rows
    vmem = pl.BlockSpec(memory_space=pltpu.VMEM)
    return pl.pallas_call(
        functools.partial(late_kernel, books, late, pieces, sizes),
        out_shape=[jax.ShapeDtypeStruct((frames_here // books, wide), bf16)] * books,
        in_specs=[vmem] * (len(late) + 5)
        + [pl.BlockSpec(memory_space=pl.ANY)] * len(parts),
        out_specs=[vmem] * books,
        scratch_shapes=[
            pltpu.VMEM((books, frames_here, width), bf16),
            pltpu.VMEM((len(late), width, depth), bf16),
            pltpu.VMEM((groups * qkv_rows, wide), bf16),
            pltpu.VMEM((frames_here, wide), bf16),
            pltpu.SemaphoreType.DMA((len(pieces) + 3 * groups,)),
        ],
        compiler_params=pltpu.CompilerParams(vmem_limit_bytes=50 * 2**20),
        name="late_products_and_qkv",
    )(
        gain,
        *[blocks[m] for m in late],
        projected,
        square,
        looked,
        depth_gain,
        *parts,
    )


def attend_kernel(books, *refs):
    arrived = refs[:books]
    out_ref, inner = refs[books:]
    place = lax.axis_index("book")
    rows, wide = arrived[0].shape
    width = wide // 3
    for m in range(books):
        inner[jnp.bitwise_xor(place, m)] = arrived[m][...]
    head_of_row = lax.broadcasted_iota(jnp.int32, (width, width), 0) // HD
    head_of_column = lax.broadcasted_iota(jnp.int32, (width, width), 1) // HD
    same_head = (head_of_row == head_of_column).astype(f32).astype(bf16)
    keys_all = [inner[j, :, width : 2 * width].astype(f32) for j in range(books)]
    values_all = [inner[j, :, 2 * width :].astype(f32) for j in range(books)]
    contexts = []
    for k in range(books):
        query = inner[k, :, :width].astype(f32) * HD ** (-0.5)
        products = jnp.concatenate([query * keys_all[j] for j in range(k + 1)], axis=0)
        high = products.astype(bf16)
        low = (products - high.astype(f32)).astype(bf16)
        scores = jnp.dot(high, same_head, preferred_element_type=f32) + jnp.dot(
            low, same_head, preferred_element_type=f32
        )
        scores = [scores[j * rows : (j + 1) * rows] for j in range(k + 1)]
        peak = functools.reduce(jnp.maximum, scores)
        expo = [jnp.exp(score - peak) for score in scores]
        total = functools.reduce(jnp.add, expo)
        context = 0.0
        for j in range(k + 1):
            probability = (expo[j] / total).astype(bf16).astype(f32)
            context = context + probability * values_all[j]
        contexts.append(context)
    out_ref[...] = jnp.stack(contexts, axis=1).astype(bf16)


def attend(arrived):
    books = len(arrived)
    rows, wide = arrived[0].shape
    vmem = pl.BlockSpec(memory_space=pltpu.VMEM)
    return pl.pallas_call(
        functools.partial(attend_kernel, books),
        out_shape=jax.ShapeDtypeStruct((rows, books, wide // 3), bf16),
        in_specs=[vmem] * books,
        out_specs=vmem,
        scratch_shapes=[pltpu.VMEM((books, rows, wide), bf16)],
        compiler_params=pltpu.CompilerParams(vmem_limit_bytes=16 * 2**20),
        name="attend_books",
    )(*arrived)


def swap(value, axis, distance):
    return lax.ppermute(value, axis, [(i, i ^ distance) for i in range(lax.axis_size(axis))])


def after(value, *others):
    return lax.optimization_barrier((value, *others))[0]


def bits_of(number):
    return [1 << place for place in range(number.bit_length()) if number >> place & 1]


def per_device(
    gate_pre,
    up_pre,
    down_weight,
    residual,
    out_gain,
    in_proj,
    embedding,
    token_ids,
    depth_gain,
    qkv_weight,
):
    books = lax.axis_size("book")
    groups = lax.axis_size("frames")
    here = lax.axis_index("book").astype(jnp.int32)
    width = residual.shape[1]
    proj_rows = in_proj.shape[1]
    gain = out_gain[None]

    hidden, first = first_products(gate_pre, up_pre, down_weight, width)

    def share(m, *others):
        factor = after(hidden, *others) if others else hidden
        return share_products(factor, down_weight, width, m)

    rows = pack(*after((in_proj[0], embedding[0], qkv_weight[0]), first))
    parts = {0: [(0, rows)]}
    near = [n for n in range(2, groups, 2) if len(bits_of(n)) == 1]
    for n in near:
        parts[n] = [(0, swap(rows, "frames", n))]

    sums = {books - 1: first}
    parts[1] = [(0, swap(rows, "frames", 1))]
    sums[books - 2] = lax.optimization_barrier(share(books - 2, rows))
    for n in range(books - 3, 0, -1):
        sums[n] = lax.optimization_barrier(share(n, rows))
    distance = 1
    while distance < books:
        came = None
        for m in range(books - distance, 0, -2 * distance):
            going = sums.pop(m).astype(bf16)
            if came is not None:
                going = after(going, came, sums[m + distance])
            came = swap(going, "book", distance)
            if m == books - 1:
                came = after(came, *[sums[n] for n in range(1, books - 1)])
            sums[m ^ distance] = sums[m ^ distance] + came.astype(f32)
            if m == books - 1:
                sums[0] = lax.optimization_barrier(share(0, came, parts[1][0][1]))
                sums[0] = sums[0] + residual.astype(f32)
        distance *= 2

    blocks = {0: sums[0].astype(bf16)}

    arrived = after([parts[n][0][1] for n in near], blocks[0])
    for n, value in zip(near, arrived):
        parts[n] = [(0, value)]
    cut = rows.shape[0] // 2 // 128 * 128
    for n in range(2, groups, 2):
        sides = bits_of(n)
        if n in near:
            continue
        if len(sides) == 2 and 0 < cut < proj_rows:
            upper, lower = cut_rows(parts[n ^ sides[0]][0][1], parts[n ^ sides[1]][0][1], cut)
            upper = swap(upper, "frames", sides[0])
            lower = swap(lower, "frames", sides[1])
            parts[n] = [(0, upper), (cut, lower)]
        else:
            parts[n] = [(0, swap(rows, "frames", n))]
    for n in range(2, groups, 2):
        parts[n + 1] = [(first, swap(value, "frames", 1)) for first, value in parts[n]]

    near_there = [parts[n + 1][0][1] for n in near]
    distance = books // 2
    while distance:
        for m in sorted(blocks):
            going = blocks[m]
            if m:
                going = after(going, blocks[distance])
            elif distance == 1:
                going = after(going, *near_there)
            blocks[m ^ distance] = swap(going, "book", distance)
        distance //= 2

    pieces = [(n, first) for n in range(groups) for first, _ in parts[n]]
    arrived = [value for n in range(groups) for _, value in parts[n]]
    sizes = proj_rows, embedding.shape[1], qkv_weight.shape[1]
    early = [m for m in range(books) if not is_late(m)]
    late = [m for m in range(books) if is_late(m)]
    projected, square, looked = project_early(
        token_ids.reshape(1, -1), gain, blocks, early, pieces, arrived, sizes
    )
    packed = project_late(
        gain,
        blocks,
        late,
        projected,
        square,
        looked,
        depth_gain,
        pieces,
        arrived,
        sizes,
        qkv_weight.shape[2],
    )
    far = {m: swap(packed[m], "book", m) for m in range(books - 1, 0, -1)}
    return attend([packed[0]] + [far[m] for m in range(1, books)])


def solution(mesh):
    in_specs = (
        P("frames", "book"),
        P("frames", "book"),
        P("book", None),
        P("frames", "book"),
        P(),
        P("book", "frames", None),
        P("book", "frames", None),
        P("frames", "book"),
        P("book", None),
        P("book", "frames", None),
    )
    out_specs = P(("frames", "book"), None, None)
    return jax.shard_map(
        per_device, mesh=mesh, in_specs=in_specs, out_specs=out_specs, check_vma=False
    )
```

```python
import functools

import jax
import jax.numpy as jnp
from jax import lax
from jax.experimental import pallas as pl
from jax.experimental.pallas import tpu as pltpu
from jax.sharding import PartitionSpec as P

H = 8
HD = 64
f32, bf16 = jnp.float32, jnp.bfloat16


def split_frames(frames):
    first = frames * 11 // 16 // 16 * 16
    return [first, frames - first]


def first_kernel(gate_ref, up_ref, down_ref, hidden_ref, one_ref, two_ref, gates, ups, held, sems):
    steps, each, width = held.shape
    books = down_ref.shape[1] // width
    start = pl.multiple_of(jnp.bitwise_xor(lax.axis_index("book"), books - 1) * width, width)
    copies = []
    for step in range(steps):
        rows = pl.ds(step * each, each)
        moves = [
            (gate_ref.at[:, rows], gates.at[step]),
            (up_ref.at[:, rows], ups.at[step]),
            (down_ref.at[rows, pl.ds(start, width)], held.at[step]),
        ]
        for kind, (source, target) in enumerate(moves):
            copies.append(pltpu.make_async_copy(source, target, sems.at[3 * step + kind]))
            copies[-1].start()
    total = 0.0
    for step in range(steps):
        copies[3 * step].wait()
        copies[3 * step + 1].wait()
        gate = gates[step].astype(f32)
        hidden = gate / (1.0 + jnp.exp(-gate)) * ups[step].astype(f32)
        hidden = hidden.astype(bf16)
        hidden_ref[:, pl.ds(step * each, each)] = hidden
        copies[3 * step + 2].wait()
        total = total + jnp.dot(hidden, held[step], preferred_element_type=f32)
    one_ref[...] = total[: one_ref.shape[0]].astype(bf16)
    two_ref[...] = total[one_ref.shape[0] :].astype(bf16)


def first_products(gate, up, down, width):
    frames_here, hidden_width = gate.shape
    steps = max(hidden_width // 512, 1)
    vmem = pl.BlockSpec(memory_space=pltpu.VMEM)
    return pl.pallas_call(
        first_kernel,
        out_shape=[
            jax.ShapeDtypeStruct((frames_here, hidden_width), bf16),
            *[jax.ShapeDtypeStruct((rows, width), bf16) for rows in split_frames(frames_here)],
        ],
        in_specs=[pl.BlockSpec(memory_space=pl.ANY)] * 3,
        out_specs=[vmem] * 3,
        scratch_shapes=[
            pltpu.VMEM((steps, frames_here, hidden_width // steps), bf16),
            pltpu.VMEM((steps, frames_here, hidden_width // steps), bf16),
            pltpu.VMEM((steps, hidden_width // steps, width), bf16),
            pltpu.SemaphoreType.DMA((3 * steps,)),
        ],
        compiler_params=pltpu.CompilerParams(vmem_limit_bytes=53 * 2**20),
        name="hidden_and_first_products",
    )(gate, up, down)


def share_kernel(partner, counts, hidden_ref, down_ref, *refs):
    outs = refs[: len(counts)]
    held, sems = refs[len(counts) :]
    steps, each, width = held.shape
    start = pl.multiple_of(jnp.bitwise_xor(lax.axis_index("book"), partner) * width, width)
    copies = []
    for step in range(steps):
        rows = pl.ds(step * each, each)
        copies.append(
            pltpu.make_async_copy(
                down_ref.at[rows, pl.ds(start, width)], held.at[step], sems.at[step]
            )
        )
        copies[-1].start()
    total = 0.0
    for step in range(steps):
        copies[step].wait()
        total = total + jnp.dot(
            hidden_ref[:, pl.ds(step * each, each)], held[step], preferred_element_type=f32
        )
    row = 0
    for ref, count in zip(outs, counts):
        ref[...] = total[row : row + count].astype(ref.dtype)
        row += count


def share_products(hidden, down, width, partner):
    frames_here, hidden_width = hidden.shape
    steps = max(hidden_width // 512, 1)
    vmem = pl.BlockSpec(memory_space=pltpu.VMEM)
    counts = [frames_here]
    held_as = bf16 if partner % 2 else f32
    return pl.pallas_call(
        functools.partial(share_kernel, partner, counts),
        out_shape=[jax.ShapeDtypeStruct((rows, width), held_as) for rows in counts],
        in_specs=[vmem, pl.BlockSpec(memory_space=pl.ANY)],
        out_specs=[vmem] * len(counts),
        scratch_shapes=[
            pltpu.VMEM((steps, hidden_width // steps, width), bf16),
            pltpu.SemaphoreType.DMA((steps,)),
        ],
        compiler_params=pltpu.CompilerParams(vmem_limit_bytes=53 * 2**20),
        name="share_products",
    )(hidden, down)


def total_kernel(starts, *refs):
    terms = refs[: len(starts)]
    whole_ref, two_ref, total = refs[len(starts) :]
    total[...] = terms[0][...].astype(f32)
    for start, ref in zip(starts[1:], terms[1:]):
        rows = pl.ds(start, ref.shape[0])
        total[rows, :] += ref[...].astype(f32)
    whole_ref[...] = total[...].astype(bf16)
    at = total.shape[0] - two_ref.shape[0]
    two_ref[...] = total[pl.ds(at, two_ref.shape[0]), :].astype(bf16)


def total_up(terms):
    frames_here, width = terms[0][1].shape
    vmem = pl.BlockSpec(memory_space=pltpu.VMEM)
    return pl.pallas_call(
        functools.partial(total_kernel, [start for start, _ in terms]),
        out_shape=[
            jax.ShapeDtypeStruct((frames_here, width), bf16),
            jax.ShapeDtypeStruct((split_frames(frames_here)[1], width), bf16),
        ],
        in_specs=[vmem] * len(terms),
        out_specs=[vmem] * 2,
        scratch_shapes=[pltpu.VMEM((frames_here, width), f32)],
        compiler_params=pltpu.CompilerParams(vmem_limit_bytes=16 * 2**20),
        name="total_of_sums",
    )(*[value for _, value in terms])


def pack_kernel(proj_ref, table_ref, qkv_ref, packed_ref, sems):
    proj_rows, depth = proj_ref.shape
    table_rows = table_ref.shape[0]
    qkv_rows, wide = qkv_ref.shape
    half, extra = qkv_rows // 2, wide - depth
    at_qkv = proj_rows + table_rows
    at_extra = at_qkv + qkv_rows
    moves = [
        (proj_ref, packed_ref.at[pl.ds(0, proj_rows)]),
        (table_ref, packed_ref.at[pl.ds(proj_rows, table_rows)]),
        (qkv_ref.at[:, pl.ds(0, depth)], packed_ref.at[pl.ds(at_qkv, qkv_rows)]),
    ]
    for side in range(2):
        moves.append(
            (
                qkv_ref.at[pl.ds(side * half, half), pl.ds(depth, extra)],
                packed_ref.at[pl.ds(at_extra, half), pl.ds(side * extra, extra)],
            )
        )
    copies = [
        pltpu.make_async_copy(source, target, sems.at[number])
        for number, (source, target) in enumerate(moves)
    ]
    for made in copies:
        made.start()
    for made in copies:
        made.wait()


def pack(proj, table, qkv):
    depth = proj.shape[1]
    rows = proj.shape[0] + table.shape[0] + qkv.shape[0] + qkv.shape[0] // 2
    return pl.pallas_call(
        pack_kernel,
        out_shape=jax.ShapeDtypeStruct((rows, depth), bf16),
        in_specs=[pl.BlockSpec(memory_space=pl.ANY)] * 3,
        out_specs=pl.BlockSpec(memory_space=pltpu.VMEM),
        scratch_shapes=[pltpu.SemaphoreType.DMA((5,))],
        compiler_params=pltpu.CompilerParams(vmem_limit_bytes=4 * 2**20),
        name="pack_weight_rows",
    )(proj, table, qkv)


def cut_kernel(cut, upper_from, lower_from, upper_ref, lower_ref, sems):
    upper = pltpu.make_async_copy(upper_from.at[pl.ds(0, cut)], upper_ref, sems.at[0])
    lower = pltpu.make_async_copy(
        lower_from.at[pl.ds(cut, lower_ref.shape[0])], lower_ref, sems.at[1]
    )
    upper.start()
    lower.start()
    upper.wait()
    lower.wait()


def cut_rows(upper_from, lower_from, cut):
    rows, depth = upper_from.shape
    return pl.pallas_call(
        functools.partial(cut_kernel, cut),
        out_shape=[
            jax.ShapeDtypeStruct((cut, depth), bf16),
            jax.ShapeDtypeStruct((rows - cut, depth), bf16),
        ],
        in_specs=[pl.BlockSpec(memory_space=pl.ANY)] * 2,
        out_specs=[pl.BlockSpec(memory_space=pltpu.VMEM)] * 2,
        scratch_shapes=[pltpu.SemaphoreType.DMA((2,))],
        name="cut_rows",
    )(upper_from, lower_from)


def is_late(m):
    return (m % 2 == 1) & (m != 1)


def hold_blocks(blocks, here, gain_ref, held, square_ref):
    for m, pieces in blocks.items():
        book = jnp.bitwise_xor(here, m)
        width = held.shape[2]
        columns = pl.ds(pl.multiple_of(book * width, width), width)
        gain = gain_ref[:, columns].astype(f32)
        row = 0
        for ref in pieces:
            rows = pl.ds(row, ref.shape[0])
            row += ref.shape[0]
            part = ref[...].astype(f32)
            square_ref[rows, :] += jnp.sum(part * part, axis=-1, keepdims=True)
            held[book, rows, :] = (part * gain).astype(bf16)


def with_refs(counts, refs):
    blocks, at = {}, 0
    for m, count in counts:
        blocks[m] = refs[at : at + count]
        at += count
    return blocks, refs[at:]


def early_kernel(books, counts, pieces, sizes, tokens_ref, gain_ref, *refs):
    blocks, refs = with_refs(counts, refs)
    parts = refs[: len(pieces)]
    projected_ref, square_ref, looked_ref, held, proj, table, sems = refs[len(pieces) :]
    proj_rows, table_rows, _ = sizes
    here, group = lax.axis_index("book"), lax.axis_index("frames")
    per_book = held.shape[2] // proj_rows

    table_copies, proj_copies = [], []
    for number, ((n, first), ref) in enumerate(zip(pieces, parts)):
        if first + ref.shape[0] > proj_rows:
            g = jnp.bitwise_xor(group, n)
            start = pl.multiple_of(g * table_rows, table_rows)
            made = pltpu.make_async_copy(
                ref.at[pl.ds(proj_rows - first, table_rows)],
                table.at[pl.ds(start, table_rows)],
                sems.at[number],
            )
            made.start()
            table_copies.append(made)
    for number, ((n, first), ref) in enumerate(zip(pieces, parts)):
        count = min(ref.shape[0], proj_rows - first)
        made = pltpu.make_async_copy(
            ref.at[pl.ds(0, count)],
            proj.at[pl.ds(n * proj_rows + first, count)],
            sems.at[len(pieces) + number],
        )
        made.start()
        proj_copies.append(made)

    square_ref[...] = jnp.zeros_like(square_ref)
    hold_blocks(blocks, here, gain_ref, held, square_ref)
    codes = lax.broadcasted_iota(jnp.int32, (table.shape[0], tokens_ref.shape[1]), 0)
    matches = (tokens_ref[...] == codes).astype(f32).astype(bf16)
    for made in table_copies:
        made.wait()
    looked = lax.dot_general(
        matches, table[...], (((0,), (0,)), ((), ())), preferred_element_type=f32
    )
    looked_ref[...] = looked.astype(bf16)
    projected_ref[...] = jnp.zeros_like(projected_ref)
    for (n, first), made, ref in zip(pieces, proj_copies, parts):
        count = min(ref.shape[0], proj_rows - first)
        owner = jnp.bitwise_xor(group, n)
        book = owner // per_book
        start = pl.multiple_of((owner % per_book) * proj_rows + first, 128)
        made.wait()

        @pl.when(jnp.logical_not(is_late(jnp.bitwise_xor(here, book))))
        def _():
            projected_ref[...] += jnp.dot(
                held[book, :, pl.ds(start, count)],
                proj[pl.ds(n * proj_rows + first, count), :],
                preferred_element_type=f32,
            )


def project_early(tokens, gain, blocks, early, pieces, parts, sizes):
    books = len(blocks)
    frames_here = sum(piece.shape[0] for piece in blocks[0])
    width = blocks[0][0].shape[1]
    counts = [(m, len(blocks[m])) for m in early]
    given = [piece for m in early for piece in blocks[m]]
    depth = parts[0].shape[1]
    proj_rows, table_rows, _ = sizes
    groups = books * width // proj_rows
    vmem = pl.BlockSpec(memory_space=pltpu.VMEM)
    return pl.pallas_call(
        functools.partial(early_kernel, books, counts, pieces, sizes),
        out_shape=[
            jax.ShapeDtypeStruct((frames_here, depth), f32),
            jax.ShapeDtypeStruct((frames_here, 1), f32),
            jax.ShapeDtypeStruct((frames_here, depth), bf16),
        ],
        in_specs=[vmem] * (2 + len(given))
        + [pl.BlockSpec(memory_space=pl.ANY)] * len(parts),
        out_specs=[vmem] * 3,
        scratch_shapes=[
            pltpu.VMEM((books, frames_here, width), bf16),
            pltpu.VMEM((books * width, depth), bf16),
            pltpu.VMEM((groups * table_rows, depth), bf16),
            pltpu.SemaphoreType.DMA((2 * len(pieces),)),
        ],
        compiler_params=pltpu.CompilerParams(vmem_limit_bytes=50 * 2**20),
        name="early_products_and_lookup",
    )(tokens, gain, *given, *parts)


def late_kernel(books, counts, pieces, sizes, gain_ref, *refs):
    blocks, refs = with_refs(counts, refs)
    early_ref, square_ref, looked_ref, depth_gain_ref = refs[:4]
    parts = refs[4 : len(pieces) + 4]
    refs = refs[len(pieces) + 4 :]
    outs = refs[:books]
    held, proj, qkv, packed, squares, sems = refs[books:]
    proj_rows, table_rows, qkv_rows = sizes
    here, group = lax.axis_index("book"), lax.axis_index("frames")
    frames_here, width = held.shape[1:]
    per_book = width // proj_rows
    half = qkv_rows // 2
    depth = proj.shape[2]
    extra = qkv.shape[1] - depth

    proj_copies = []
    for number, ((n, first), ref) in enumerate(zip(pieces, parts)):
        count = min(ref.shape[0], proj_rows - first)
        owner = jnp.bitwise_xor(group, n)
        m = jnp.bitwise_xor(here, owner // per_book)
        start = pl.multiple_of((owner % per_book) * proj_rows + first, 128)
        slot = jnp.maximum(m // 2 - 1, 0)
        made = pltpu.make_async_copy(
            ref.at[pl.ds(0, count)], proj.at[slot, pl.ds(start, count)], sems.at[number]
        )
        pl.when(is_late(m))(made.start)
        proj_copies.append((is_late(m), made))
    qkv_copies = []

    def copy(source, target):
        made = pltpu.make_async_copy(source, target, sems.at[len(pieces) + len(qkv_copies)])
        made.start()
        qkv_copies.append(made)

    for (n, first), ref in zip(pieces, parts):
        if first + ref.shape[0] > proj_rows:
            g = jnp.bitwise_xor(group, n)
            at_qkv = proj_rows - first + table_rows
            start = pl.multiple_of(g * qkv_rows, qkv_rows)
            copy(
                ref.at[pl.ds(at_qkv, qkv_rows)], qkv.at[pl.ds(start, qkv_rows), pl.ds(0, depth)]
            )
            for side in range(2):
                start = pl.multiple_of(g * qkv_rows + side * half, half)
                copy(
                    ref.at[pl.ds(at_qkv + qkv_rows, half), pl.ds(side * extra, extra)],
                    qkv.at[pl.ds(start, half), pl.ds(depth, extra)],
                )

    squares[...] = square_ref[...]
    hold_blocks(blocks, here, gain_ref, held, squares)
    square = squares[...]
    projected = early_ref[...]
    for late_here, made in proj_copies:
        pl.when(late_here)(made.wait)
    for slot, (m, _) in enumerate(counts):
        projected = projected + jnp.dot(
            held[jnp.bitwise_xor(here, m)], proj[slot], preferred_element_type=f32
        )
    projected = projected * lax.rsqrt(square / (books * width) + 1e-05)
    depth_in = (projected + looked_ref[...].astype(f32)).astype(bf16).astype(f32)
    moment = jnp.mean(depth_in * depth_in, axis=-1, keepdims=True)
    depth_normed = depth_in * lax.rsqrt(moment + 1e-05) * depth_gain_ref[...].astype(f32)
    for made in qkv_copies:
        made.wait()
    packed[...] = jnp.dot(
        depth_normed.astype(bf16), qkv[...], preferred_element_type=f32
    ).astype(bf16)
    rows = frames_here // books
    for m in range(books):
        start = pl.multiple_of(jnp.bitwise_xor(here, m) * rows, rows)
        outs[m][...] = packed[pl.ds(start, rows), :]


def project_late(
    gain, blocks, late, projected, square, looked, depth_gain, pieces, parts, sizes, wide
):
    books = len(blocks)
    frames_here = sum(piece.shape[0] for piece in blocks[0])
    width = blocks[0][0].shape[1]
    counts = [(m, len(blocks[m])) for m in late]
    given = [piece for m in late for piece in blocks[m]]
    depth = projected.shape[1]
    proj_rows, _, qkv_rows = sizes
    groups = books * width // proj_rows
    vmem = pl.BlockSpec(memory_space=pltpu.VMEM)
    return pl.pallas_call(
        functools.partial(late_kernel, books, counts, pieces, sizes),
        out_shape=[jax.ShapeDtypeStruct((frames_here // books, wide), bf16)] * books,
        in_specs=[vmem] * (len(given) + 5)
        + [pl.BlockSpec(memory_space=pl.ANY)] * len(parts),
        out_specs=[vmem] * books,
        scratch_shapes=[
            pltpu.VMEM((books, frames_here, width), bf16),
            pltpu.VMEM((len(late), width, depth), bf16),
            pltpu.VMEM((groups * qkv_rows, wide), bf16),
            pltpu.VMEM((frames_here, wide), bf16),
            pltpu.VMEM((frames_here, 1), f32),
            pltpu.SemaphoreType.DMA((len(pieces) + 3 * groups,)),
        ],
        compiler_params=pltpu.CompilerParams(vmem_limit_bytes=50 * 2**20),
        name="late_products_and_qkv",
    )(
        gain,
        *given,
        projected,
        square,
        looked,
        depth_gain,
        *parts,
    )


def attend_kernel(books, *refs):
    arrived = refs[:books]
    out_ref, inner = refs[books:]
    place = lax.axis_index("book")
    rows, wide = arrived[0].shape
    width = wide // 3
    for m in range(books):
        inner[jnp.bitwise_xor(place, m)] = arrived[m][...]
    head_of_row = lax.broadcasted_iota(jnp.int32, (width, width), 0) // HD
    head_of_column = lax.broadcasted_iota(jnp.int32, (width, width), 1) // HD
    same_head = (head_of_row == head_of_column).astype(f32).astype(bf16)
    keys_all = [inner[j, :, width : 2 * width].astype(f32) for j in range(books)]
    values_all = [inner[j, :, 2 * width :].astype(f32) for j in range(books)]
    contexts = []
    for k in range(books):
        query = inner[k, :, :width].astype(f32) * HD ** (-0.5)
        products = jnp.concatenate([query * keys_all[j] for j in range(k + 1)], axis=0)
        high = products.astype(bf16)
        low = (products - high.astype(f32)).astype(bf16)
        scores = jnp.dot(high, same_head, preferred_element_type=f32) + jnp.dot(
            low, same_head, preferred_element_type=f32
        )
        scores = [scores[j * rows : (j + 1) * rows] for j in range(k + 1)]
        peak = functools.reduce(jnp.maximum, scores)
        expo = [jnp.exp(score - peak) for score in scores]
        total = functools.reduce(jnp.add, expo)
        context = 0.0
        for j in range(k + 1):
            probability = (expo[j] / total).astype(bf16).astype(f32)
            context = context + probability * values_all[j]
        contexts.append(context)
    out_ref[...] = jnp.stack(contexts, axis=1).astype(bf16)


def attend(arrived):
    books = len(arrived)
    rows, wide = arrived[0].shape
    vmem = pl.BlockSpec(memory_space=pltpu.VMEM)
    return pl.pallas_call(
        functools.partial(attend_kernel, books),
        out_shape=jax.ShapeDtypeStruct((rows, books, wide // 3), bf16),
        in_specs=[vmem] * books,
        out_specs=vmem,
        scratch_shapes=[pltpu.VMEM((books, rows, wide), bf16)],
        compiler_params=pltpu.CompilerParams(vmem_limit_bytes=16 * 2**20),
        name="attend_books",
    )(*arrived)


def swap(value, axis, distance):
    return lax.ppermute(value, axis, [(i, i ^ distance) for i in range(lax.axis_size(axis))])


def after(value, *others):
    return lax.optimization_barrier((value, *others))[0]


def bits_of(number):
    return [1 << place for place in range(number.bit_length()) if number >> place & 1]


def per_device(
    gate_pre,
    up_pre,
    down_weight,
    residual,
    out_gain,
    in_proj,
    embedding,
    token_ids,
    depth_gain,
    qkv_weight,
):
    books = lax.axis_size("book")
    groups = lax.axis_size("frames")
    here = lax.axis_index("book").astype(jnp.int32)
    width = residual.shape[1]
    proj_rows = in_proj.shape[1]
    gain = out_gain[None]

    hidden, *first = first_products(gate_pre, up_pre, down_weight, width)

    def share(m, *others):
        factor = after(hidden, *others) if others else hidden
        return share_products(factor, down_weight, width, m)

    rows = pack(*after((in_proj[0], embedding[0], qkv_weight[0]), *first))
    parts = {0: [(0, rows)]}
    near = [n for n in range(2, groups, 2) if len(bits_of(n)) == 1]
    for n in near:
        parts[n] = [(0, swap(rows, "frames", n))]

    sums = {books - 1: first}
    parts[1] = [(0, swap(rows, "frames", 1))]
    sums[books - 2] = lax.optimization_barrier(share(books - 2, rows))
    for n in range(books - 3, 0, -1):
        sums[n] = lax.optimization_barrier(share(n, parts[1][0][1]))
    near_came = swap(first[0], "book", 1)
    far_came = swap(first[1], "book", books - 1)
    del sums[books - 1]
    one = first[0].shape[0]
    sums[0] = lax.optimization_barrier(share(0, near_came))
    terms = {m: [(0, sums[m][0])] for m in range(0, books, 2)}
    terms[0] += [(0, residual), (one, far_came)]
    terms[books - 2].append((0, near_came))
    for m in range(books - 3, 0, -2):
        came = swap(after(sums[m][0], near_came, far_came), "book", 1)
        terms[m ^ 1].append((0, came))
    distance = 2
    while distance < books:
        for m in range(books - distance, 0, -2 * distance):
            came = swap(total_up(terms.pop(m))[0], "book", distance)
            terms[m ^ distance].append((0, came))
        distance *= 2
    own, own_two = total_up(terms[0])

    arrived = after([parts[n][0][1] for n in near], own)
    for n, value in zip(near, arrived):
        parts[n] = [(0, value)]
    cut = rows.shape[0] // 2 // 128 * 128
    for n in range(2, groups, 2):
        sides = bits_of(n)
        if n in near:
            continue
        if len(sides) == 2 and 0 < cut < proj_rows:
            upper, lower = cut_rows(parts[n ^ sides[0]][0][1], parts[n ^ sides[1]][0][1], cut)
            upper = swap(upper, "frames", sides[0])
            lower = swap(lower, "frames", sides[1])
            parts[n] = [(0, upper), (cut, lower)]
        else:
            parts[n] = [(0, swap(rows, "frames", n))]
    for n in near:
        parts[n + 1] = [(0, swap(parts[n][0][1], "frames", 1))]

    near_there = [parts[n + 1][0][1] for n in near]
    blocks = {0: own}
    distance = books // 2
    while distance > 1:
        for m in sorted(blocks):
            blocks[m ^ distance] = swap(blocks[m], "book", distance)
        distance //= 2
    blocks = {m: [block] for m, block in blocks.items()}
    blocks[1] = [swap(after(own, *near_there), "book", 1)]
    for n in range(2, groups, 2):
        if n not in near:
            parts[n + 1] = [
                (first, swap(after(value, *blocks[books // 2], *blocks[1]), "frames", 1))
                for first, value in parts[n]
            ]
    for m in range(2, books, 2):
        blocks[m + 1] = [
            swap(after(blocks[m][0][:one], *blocks[1]), "book", 1),
            swap(after(own_two, *blocks[m]), "book", m + 1),
        ]

    pieces = [(n, first) for n in range(groups) for first, _ in parts[n]]
    arrived = [value for n in range(groups) for _, value in parts[n]]
    sizes = proj_rows, embedding.shape[1], qkv_weight.shape[1]
    early = [m for m in range(books) if not is_late(m)]
    late = [m for m in range(books) if is_late(m)]
    projected, square, looked = project_early(
        token_ids.reshape(1, -1), gain, blocks, early, pieces, arrived, sizes
    )
    packed = project_late(
        gain,
        blocks,
        late,
        projected,
        square,
        looked,
        depth_gain,
        pieces,
        arrived,
        sizes,
        qkv_weight.shape[2],
    )
    far = {m: swap(packed[m], "book", m) for m in range(books - 1, 0, -1)}
    return attend([packed[0]] + [far[m] for m in range(1, books)])


def solution(mesh):
    in_specs = (
        P("frames", "book"),
        P("frames", "book"),
        P("book", None),
        P("frames", "book"),
        P(),
        P("book", "frames", None),
        P("book", "frames", None),
        P("frames", "book"),
        P("book", None),
        P("book", "frames", None),
    )
    out_specs = P(("frames", "book"), None, None)
    return jax.shard_map(
        per_device, mesh=mesh, in_specs=in_specs, out_specs=out_specs, check_vma=False
    )
```

```python
import functools

import jax
import jax.numpy as jnp
from jax import lax
from jax.experimental import pallas as pl
from jax.experimental.pallas import tpu as pltpu
from jax.sharding import PartitionSpec as P

H = 8
HD = 64
f32, bf16 = jnp.float32, jnp.bfloat16


def first_kernel(gate_ref, up_ref, down_ref, hidden_ref, first_ref, gates, ups, held, sems):
    steps, each, width = held.shape
    books = down_ref.shape[1] // width
    start = pl.multiple_of(jnp.bitwise_xor(lax.axis_index("book"), books - 1) * width, width)
    copies = []
    for step in range(steps):
        rows = pl.ds(step * each, each)
        moves = [
            (gate_ref.at[:, rows], gates.at[step]),
            (up_ref.at[:, rows], ups.at[step]),
            (down_ref.at[rows, pl.ds(start, width)], held.at[step]),
        ]
        for kind, (source, target) in enumerate(moves):
            copies.append(pltpu.make_async_copy(source, target, sems.at[3 * step + kind]))
            copies[-1].start()
    total = 0.0
    for step in range(steps):
        copies[3 * step].wait()
        copies[3 * step + 1].wait()
        gate = gates[step].astype(f32)
        hidden = gate / (1.0 + jnp.exp(-gate)) * ups[step].astype(f32)
        hidden = hidden.astype(bf16)
        hidden_ref[:, pl.ds(step * each, each)] = hidden
        copies[3 * step + 2].wait()
        total = total + jnp.dot(hidden, held[step], preferred_element_type=f32)
    first_ref[...] = total.astype(bf16)


def first_products(gate, up, down, width):
    frames_here, hidden_width = gate.shape
    steps = max(hidden_width // 256, 1)
    vmem = pl.BlockSpec(memory_space=pltpu.VMEM)
    return pl.pallas_call(
        first_kernel,
        out_shape=[
            jax.ShapeDtypeStruct((frames_here, hidden_width), bf16),
            jax.ShapeDtypeStruct((frames_here, width), bf16),
        ],
        in_specs=[pl.BlockSpec(memory_space=pl.ANY)] * 3,
        out_specs=[vmem] * 2,
        scratch_shapes=[
            pltpu.VMEM((steps, frames_here, hidden_width // steps), bf16),
            pltpu.VMEM((steps, frames_here, hidden_width // steps), bf16),
            pltpu.VMEM((steps, hidden_width // steps, width), bf16),
            pltpu.SemaphoreType.DMA((3 * steps,)),
        ],
        compiler_params=pltpu.CompilerParams(vmem_limit_bytes=53 * 2**20),
        name="hidden_and_first_products",
    )(gate, up, down)


def share_kernel(partner, hidden_ref, down_ref, out_ref, held, sems):
    steps, each, width = held.shape
    start = pl.multiple_of(jnp.bitwise_xor(lax.axis_index("book"), partner) * width, width)
    copies = []
    for step in range(steps):
        rows = pl.ds(step * each, each)
        copies.append(
            pltpu.make_async_copy(
                down_ref.at[rows, pl.ds(start, width)], held.at[step], sems.at[step]
            )
        )
        copies[-1].start()
    total = 0.0
    for step in range(steps):
        copies[step].wait()
        total = total + jnp.dot(
            hidden_ref[:, pl.ds(step * each, each)], held[step], preferred_element_type=f32
        )
    out_ref[...] = total


def share_products(hidden, down, width, partner):
    frames_here, hidden_width = hidden.shape
    steps = max(hidden_width // 512, 1)
    vmem = pl.BlockSpec(memory_space=pltpu.VMEM)
    return pl.pallas_call(
        functools.partial(share_kernel, partner),
        out_shape=jax.ShapeDtypeStruct((frames_here, width), f32),
        in_specs=[vmem, pl.BlockSpec(memory_space=pl.ANY)],
        out_specs=vmem,
        scratch_shapes=[
            pltpu.VMEM((steps, hidden_width // steps, width), bf16),
            pltpu.SemaphoreType.DMA((steps,)),
        ],
        compiler_params=pltpu.CompilerParams(vmem_limit_bytes=53 * 2**20),
        name="share_products",
    )(hidden, down)


def pack_kernel(proj_ref, table_ref, qkv_ref, packed_ref, sems):
    proj_rows, depth = proj_ref.shape
    table_rows = table_ref.shape[0]
    qkv_rows, wide = qkv_ref.shape
    half, extra = qkv_rows // 2, wide - depth
    at_qkv = proj_rows + table_rows
    at_extra = at_qkv + qkv_rows
    moves = [
        (proj_ref, packed_ref.at[pl.ds(0, proj_rows)]),
        (table_ref, packed_ref.at[pl.ds(proj_rows, table_rows)]),
        (qkv_ref.at[:, pl.ds(0, depth)], packed_ref.at[pl.ds(at_qkv, qkv_rows)]),
    ]
    for side in range(2):
        moves.append(
            (
                qkv_ref.at[pl.ds(side * half, half), pl.ds(depth, extra)],
                packed_ref.at[pl.ds(at_extra, half), pl.ds(side * extra, extra)],
            )
        )
    copies = [
        pltpu.make_async_copy(source, target, sems.at[number])
        for number, (source, target) in enumerate(moves)
    ]
    for made in copies:
        made.start()
    for made in copies:
        made.wait()


def pack(proj, table, qkv):
    depth = proj.shape[1]
    rows = proj.shape[0] + table.shape[0] + qkv.shape[0] + qkv.shape[0] // 2
    return pl.pallas_call(
        pack_kernel,
        out_shape=jax.ShapeDtypeStruct((rows, depth), bf16),
        in_specs=[pl.BlockSpec(memory_space=pl.ANY)] * 3,
        out_specs=pl.BlockSpec(memory_space=pltpu.VMEM),
        scratch_shapes=[pltpu.SemaphoreType.DMA((5,))],
        compiler_params=pltpu.CompilerParams(vmem_limit_bytes=4 * 2**20),
        name="pack_weight_rows",
    )(proj, table, qkv)


def cut_kernel(cut, upper_from, lower_from, upper_ref, lower_ref, sems):
    upper = pltpu.make_async_copy(upper_from.at[pl.ds(0, cut)], upper_ref, sems.at[0])
    lower = pltpu.make_async_copy(
        lower_from.at[pl.ds(cut, lower_ref.shape[0])], lower_ref, sems.at[1]
    )
    upper.start()
    lower.start()
    upper.wait()
    lower.wait()


def cut_rows(upper_from, lower_from, cut):
    rows, depth = upper_from.shape
    return pl.pallas_call(
        functools.partial(cut_kernel, cut),
        out_shape=[
            jax.ShapeDtypeStruct((cut, depth), bf16),
            jax.ShapeDtypeStruct((rows - cut, depth), bf16),
        ],
        in_specs=[pl.BlockSpec(memory_space=pl.ANY)] * 2,
        out_specs=[pl.BlockSpec(memory_space=pltpu.VMEM)] * 2,
        scratch_shapes=[pltpu.SemaphoreType.DMA((2,))],
        name="cut_rows",
    )(upper_from, lower_from)


def is_late(m):
    return (m % 2 == 1) & (m != 1)


def hold_blocks(blocks, here, gain_ref, held):
    square = 0.0
    for m, ref in blocks.items():
        book = jnp.bitwise_xor(here, m)
        part = ref[...].astype(f32)
        square = square + jnp.sum(part * part, axis=-1, keepdims=True)
        width = part.shape[1]
        columns = pl.ds(pl.multiple_of(book * width, width), width)
        held[book] = (part * gain_ref[:, columns].astype(f32)).astype(bf16)
    return square


def early_kernel(books, early, pieces, sizes, tokens_ref, gain_ref, *refs):
    blocks = dict(zip(early, refs))
    parts = refs[len(early) : len(early) + len(pieces)]
    outs = refs[len(early) + len(pieces) :]
    projected_ref, square_ref, later_ref, looked_ref, qkv_ref, held, proj, table, sems = outs
    proj_rows, table_rows, qkv_rows = sizes
    here, group = lax.axis_index("book"), lax.axis_index("frames")
    width = held.shape[2]
    per_book = width // proj_rows
    half = qkv_rows // 2
    depth = table.shape[1]
    extra = qkv_ref.shape[1] - depth

    started = []

    def copy(source, target):
        made = pltpu.make_async_copy(source, target, sems.at[len(started)])
        made.start()
        started.append(made)
        return made

    table_copies, proj_copies, qkv_copies = [], [], []
    for (n, first), ref in zip(pieces, parts):
        if first + ref.shape[0] > proj_rows:
            g = jnp.bitwise_xor(group, n)
            start = pl.multiple_of(g * table_rows, table_rows)
            table_copies.append(
                copy(
                    ref.at[pl.ds(proj_rows - first, table_rows)], table.at[pl.ds(start, table_rows)]
                )
            )
    for (n, first), ref in zip(pieces, parts):
        count = min(ref.shape[0], proj_rows - first)
        proj_copies.append(
            copy(ref.at[pl.ds(0, count)], proj.at[pl.ds(n * proj_rows + first, count)])
        )
    for (n, first), ref in zip(pieces, parts):
        if first + ref.shape[0] > proj_rows:
            g = jnp.bitwise_xor(group, n)
            at_qkv = proj_rows - first + table_rows
            at_extra = at_qkv + qkv_rows
            start = pl.multiple_of(g * qkv_rows, qkv_rows)
            qkv_copies.append(
                copy(
                    ref.at[pl.ds(at_qkv, qkv_rows)],
                    qkv_ref.at[pl.ds(start, qkv_rows), pl.ds(0, depth)],
                )
            )
            for side in range(2):
                start = pl.multiple_of(g * qkv_rows + side * half, half)
                qkv_copies.append(
                    copy(
                        ref.at[pl.ds(at_extra, half), pl.ds(side * extra, extra)],
                        qkv_ref.at[pl.ds(start, half), pl.ds(depth, extra)],
                    )
                )

    square_ref[...] = hold_blocks(blocks, here, gain_ref, held)
    codes = lax.broadcasted_iota(jnp.int32, (table.shape[0], tokens_ref.shape[1]), 0)
    matches = (tokens_ref[...] == codes).astype(f32).astype(bf16)
    for made in table_copies:
        made.wait()
    looked = lax.dot_general(
        matches, table[...], (((0,), (0,)), ((), ())), preferred_element_type=f32
    )
    looked_ref[...] = looked.astype(bf16)
    projected_ref[...] = jnp.zeros_like(projected_ref)
    for (n, first), made, ref in zip(pieces, proj_copies, parts):
        count = min(ref.shape[0], proj_rows - first)
        rows = pl.ds(n * proj_rows + first, count)
        owner = jnp.bitwise_xor(group, n)
        book = owner // per_book
        start = pl.multiple_of((owner % per_book) * proj_rows + first, 128)
        late = is_late(jnp.bitwise_xor(here, book))
        made.wait()

        @pl.when(jnp.logical_not(late))
        def _():
            projected_ref[...] += jnp.dot(
                held[book, :, pl.ds(start, count)], proj[rows, :], preferred_element_type=f32
            )

        @pl.when(late)
        def _():
            slot = jnp.bitwise_xor(here, book) // 2 - 1
            later_ref[slot, pl.ds(start, count), :] = proj[rows, :]

    for made in qkv_copies:
        made.wait()


def project_early(tokens, gain, blocks, early, pieces, parts, sizes, wide):
    books = len(blocks)
    frames_here, width = blocks[0].shape
    depth = parts[0].shape[1]
    proj_rows, table_rows, qkv_rows = sizes
    groups = books * width // proj_rows
    vmem = pl.BlockSpec(memory_space=pltpu.VMEM)
    return pl.pallas_call(
        functools.partial(early_kernel, books, early, pieces, sizes),
        out_shape=[
            jax.ShapeDtypeStruct((frames_here, depth), f32),
            jax.ShapeDtypeStruct((frames_here, 1), f32),
            jax.ShapeDtypeStruct((books - len(early), width, depth), bf16),
            jax.ShapeDtypeStruct((frames_here, depth), bf16),
            jax.ShapeDtypeStruct((groups * qkv_rows, wide), bf16),
        ],
        in_specs=[vmem] * (2 + len(early))
        + [pl.BlockSpec(memory_space=pl.ANY)] * len(parts),
        out_specs=[vmem] * 5,
        scratch_shapes=[
            pltpu.VMEM((books, frames_here, width), bf16),
            pltpu.VMEM((books * width, depth), bf16),
            pltpu.VMEM((groups * table_rows, depth), bf16),
            pltpu.SemaphoreType.DMA((len(pieces) + 4 * groups,)),
        ],
        compiler_params=pltpu.CompilerParams(vmem_limit_bytes=45 * 2**20),
        name="early_products_and_lookup",
    )(tokens, gain, *[blocks[m] for m in early], *parts)


def late_kernel(books, late, gain_ref, *refs):
    blocks = dict(zip(late, refs))
    later_from, early_ref, square_ref, looked_ref, depth_gain_ref, qkv_from = refs[
        len(late) : len(late) + 6
    ]
    refs = refs[len(late) + 6 :]
    outs = refs[:books]
    held, packed, later_ref, qkv_ref, sems = refs[books:]
    later_copy = pltpu.make_async_copy(later_from, later_ref, sems.at[0])
    later_copy.start()
    qkv_copy = pltpu.make_async_copy(qkv_from, qkv_ref, sems.at[1])
    qkv_copy.start()
    here = lax.axis_index("book")
    frames_here, width = held.shape[1:]
    square = square_ref[...] + hold_blocks(blocks, here, gain_ref, held)
    projected = early_ref[...]
    later_copy.wait()
    for slot, m in enumerate(late):
        projected = projected + jnp.dot(
            held[jnp.bitwise_xor(here, m)], later_ref[slot], preferred_element_type=f32
        )
    projected = projected * lax.rsqrt(square / (books * width) + 1e-05)
    depth_in = (projected + looked_ref[...].astype(f32)).astype(bf16).astype(f32)
    moment = jnp.mean(depth_in * depth_in, axis=-1, keepdims=True)
    depth_normed = (depth_in * lax.rsqrt(moment + 1e-05) * depth_gain_ref[...].astype(f32)).astype(bf16)
    qkv_copy.wait()
    packed[...] = jnp.dot(depth_normed, qkv_ref[...], preferred_element_type=f32).astype(bf16)
    rows = frames_here // books
    for m in range(books):
        start = pl.multiple_of(jnp.bitwise_xor(here, m) * rows, rows)
        outs[m][...] = packed[pl.ds(start, rows), :]


def project_late(gain, blocks, late, later, projected, square, looked, depth_gain, qkv):
    books = len(blocks)
    frames_here, width = blocks[0].shape
    wide = qkv.shape[1]
    vmem = pl.BlockSpec(memory_space=pltpu.VMEM)
    return pl.pallas_call(
        functools.partial(late_kernel, books, late),
        out_shape=[jax.ShapeDtypeStruct((frames_here // books, wide), bf16)] * books,
        in_specs=[vmem] * (len(late) + 1)
        + [pl.BlockSpec(memory_space=pl.ANY)]
        + [vmem] * 4
        + [pl.BlockSpec(memory_space=pl.ANY)],
        out_specs=[vmem] * books,
        scratch_shapes=[
            pltpu.VMEM((books, frames_here, width), bf16),
            pltpu.VMEM((frames_here, wide), bf16),
            pltpu.VMEM(later.shape, bf16),
            pltpu.VMEM(qkv.shape, bf16),
            pltpu.SemaphoreType.DMA((2,)),
        ],
        compiler_params=pltpu.CompilerParams(vmem_limit_bytes=50 * 2**20),
        name="late_products_and_qkv",
    )(
        gain,
        *[blocks[m] for m in late],
        later,
        projected,
        square,
        looked,
        depth_gain,
        qkv,
    )


def attend_kernel(books, *refs):
    arrived = refs[:books]
    out_ref, inner = refs[books:]
    place = lax.axis_index("book")
    rows, wide = arrived[0].shape
    width = wide // 3
    for m in range(books):
        inner[jnp.bitwise_xor(place, m)] = arrived[m][...]
    head_of_row = lax.broadcasted_iota(jnp.int32, (width, width), 0) // HD
    head_of_column = lax.broadcasted_iota(jnp.int32, (width, width), 1) // HD
    same_head = (head_of_row == head_of_column).astype(f32).astype(bf16)
    keys_all = [inner[j, :, width : 2 * width].astype(f32) for j in range(books)]
    values_all = [inner[j, :, 2 * width :].astype(f32) for j in range(books)]
    contexts = []
    for k in range(books):
        query = inner[k, :, :width].astype(f32) * HD ** (-0.5)
        products = jnp.concatenate([query * keys_all[j] for j in range(k + 1)], axis=0)
        high = products.astype(bf16)
        low = (products - high.astype(f32)).astype(bf16)
        scores = jnp.dot(high, same_head, preferred_element_type=f32) + jnp.dot(
            low, same_head, preferred_element_type=f32
        )
        scores = [scores[j * rows : (j + 1) * rows] for j in range(k + 1)]
        peak = functools.reduce(jnp.maximum, scores)
        expo = [jnp.exp(score - peak) for score in scores]
        total = functools.reduce(jnp.add, expo)
        context = 0.0
        for j in range(k + 1):
            probability = (expo[j] / total).astype(bf16).astype(f32)
            context = context + probability * values_all[j]
        contexts.append(context)
    out_ref[...] = jnp.stack(contexts, axis=1).astype(bf16)


def attend(arrived):
    books = len(arrived)
    rows, wide = arrived[0].shape
    vmem = pl.BlockSpec(memory_space=pltpu.VMEM)
    return pl.pallas_call(
        functools.partial(attend_kernel, books),
        out_shape=jax.ShapeDtypeStruct((rows, books, wide // 3), bf16),
        in_specs=[vmem] * books,
        out_specs=vmem,
        scratch_shapes=[pltpu.VMEM((books, rows, wide), bf16)],
        compiler_params=pltpu.CompilerParams(vmem_limit_bytes=16 * 2**20),
        name="attend_books",
    )(*arrived)


def swap(value, axis, distance):
    return lax.ppermute(value, axis, [(i, i ^ distance) for i in range(lax.axis_size(axis))])


def after(value, *others):
    return lax.optimization_barrier((value, *others))[0]


def bits_of(number):
    return [1 << place for place in range(number.bit_length()) if number >> place & 1]


def per_device(
    gate_pre,
    up_pre,
    down_weight,
    residual,
    out_gain,
    in_proj,
    embedding,
    token_ids,
    depth_gain,
    qkv_weight,
):
    books = lax.axis_size("book")
    groups = lax.axis_size("frames")
    here = lax.axis_index("book").astype(jnp.int32)
    width = residual.shape[1]
    proj_rows = in_proj.shape[1]
    gain = out_gain[None]

    hidden, first = first_products(gate_pre, up_pre, down_weight, width)

    def share(m, *others):
        factor = after(hidden, *others) if others else hidden
        if m == 0:
            block = lax.dynamic_slice_in_dim(
                down_weight, lax.axis_index("book") * width, width, 1
            )
            return jnp.dot(factor, block, preferred_element_type=f32)
        return share_products(factor, down_weight, width, m)

    rows = pack(*after((in_proj[0], embedding[0], qkv_weight[0]), first))
    parts = {0: [(0, rows)]}
    near = [n for n in range(2, groups, 2) if len(bits_of(n)) == 1]
    for n in near:
        parts[n] = [(0, swap(rows, "frames", n))]

    sums = {books - 1: first}
    parts[1] = [(0, swap(rows, "frames", 1))]
    sums[books - 2] = lax.optimization_barrier(share(books - 2, rows))
    for n in range(books - 3, 0, -1):
        sums[n] = lax.optimization_barrier(share(n, rows))
    distance = 1
    while distance < books:
        came = None
        for m in range(books - distance, 0, -2 * distance):
            going = sums.pop(m).astype(bf16)
            if came is not None:
                going = after(going, came, sums[m + distance])
            came = swap(going, "book", distance)
            if m == books - 1:
                came = after(came, *[sums[n] for n in range(1, books - 1)])
            sums[m ^ distance] = sums[m ^ distance] + came.astype(f32)
            if m == books - 1:
                sums[0] = lax.optimization_barrier(share(0, came, parts[1][0][1]))
                sums[0] = sums[0] + residual.astype(f32)
        distance *= 2

    blocks = {0: sums[0].astype(bf16)}

    arrived = after([parts[n][0][1] for n in near], blocks[0])
    for n, value in zip(near, arrived):
        parts[n] = [(0, value)]
    cut = rows.shape[0] // 2 // 128 * 128
    for n in range(2, groups, 2):
        sides = bits_of(n)
        if n in near:
            continue
        if len(sides) == 2 and 0 < cut < proj_rows:
            upper, lower = cut_rows(parts[n ^ sides[0]][0][1], parts[n ^ sides[1]][0][1], cut)
            upper = swap(upper, "frames", sides[0])
            lower = swap(lower, "frames", sides[1])
            parts[n] = [(0, upper), (cut, lower)]
        else:
            parts[n] = [(0, swap(rows, "frames", n))]
    for n in range(2, groups, 2):
        parts[n + 1] = [(first, swap(value, "frames", 1)) for first, value in parts[n]]

    near_there = [parts[n + 1][0][1] for n in near]
    distance = books // 2
    while distance:
        for m in sorted(blocks):
            going = blocks[m]
            if m:
                going = after(going, blocks[distance])
            elif distance == 1:
                going = after(going, *near_there)
            blocks[m ^ distance] = swap(going, "book", distance)
        distance //= 2

    pieces = [(n, first) for n in range(groups) for first, _ in parts[n]]
    arrived = [value for n in range(groups) for _, value in parts[n]]
    sizes = proj_rows, embedding.shape[1], qkv_weight.shape[1]
    early = [m for m in range(books) if not is_late(m)]
    late = [m for m in range(books) if is_late(m)]
    projected, square, later, looked, qkv = project_early(
        token_ids.reshape(1, -1), gain, blocks, early, pieces, arrived, sizes, qkv_weight.shape[2]
    )
    packed = project_late(
        gain, blocks, late, later, projected, square, looked, depth_gain, qkv
    )
    far = {m: swap(packed[m], "book", m) for m in range(books - 1, 0, -1)}
    return attend([packed[0]] + [far[m] for m in range(1, books)])


def solution(mesh):
    in_specs = (
        P("frames", "book"),
        P("frames", "book"),
        P("book", None),
        P("frames", "book"),
        P(),
        P("book", "frames", None),
        P("book", "frames", None),
        P("frames", "book"),
        P("book", None),
        P("book", "frames", None),
    )
    out_specs = P(("frames", "book"), None, None)
    return jax.shard_map(
        per_device, mesh=mesh, in_specs=in_specs, out_specs=out_specs, check_vma=False
    )
```

```python
import functools

import jax
import jax.numpy as jnp
from jax import lax
from jax.experimental import pallas as pl
from jax.experimental.pallas import tpu as pltpu
from jax.sharding import PartitionSpec as P

H = 8
HD = 64
f32, bf16 = jnp.float32, jnp.bfloat16


def first_kernel(gate_ref, up_ref, down_ref, hidden_ref, first_ref, gates, ups, held, sems):
    steps, each, width = held.shape
    books = down_ref.shape[1] // width
    start = pl.multiple_of(jnp.bitwise_xor(lax.axis_index("book"), books - 1) * width, width)
    copies = []
    for step in range(steps):
        rows = pl.ds(step * each, each)
        moves = [
            (gate_ref.at[:, rows], gates.at[step]),
            (up_ref.at[:, rows], ups.at[step]),
            (down_ref.at[rows, pl.ds(start, width)], held.at[step]),
        ]
        for kind, (source, target) in enumerate(moves):
            copies.append(pltpu.make_async_copy(source, target, sems.at[3 * step + kind]))
            copies[-1].start()
    total = 0.0
    for step in range(steps):
        copies[3 * step].wait()
        copies[3 * step + 1].wait()
        gate = gates[step].astype(f32)
        hidden = gate / (1.0 + jnp.exp(-gate)) * ups[step].astype(f32)
        hidden = hidden.astype(bf16)
        hidden_ref[:, pl.ds(step * each, each)] = hidden
        copies[3 * step + 2].wait()
        total = total + jnp.dot(hidden, held[step], preferred_element_type=f32)
    first_ref[...] = total.astype(bf16)


def first_products(gate, up, down, width):
    frames_here, hidden_width = gate.shape
    steps = max(hidden_width // 512, 1)
    vmem = pl.BlockSpec(memory_space=pltpu.VMEM)
    return pl.pallas_call(
        first_kernel,
        out_shape=[
            jax.ShapeDtypeStruct((frames_here, hidden_width), bf16),
            jax.ShapeDtypeStruct((frames_here, width), bf16),
        ],
        in_specs=[pl.BlockSpec(memory_space=pl.ANY)] * 3,
        out_specs=[vmem] * 2,
        scratch_shapes=[
            pltpu.VMEM((steps, frames_here, hidden_width // steps), bf16),
            pltpu.VMEM((steps, frames_here, hidden_width // steps), bf16),
            pltpu.VMEM((steps, hidden_width // steps, width), bf16),
            pltpu.SemaphoreType.DMA((3 * steps,)),
        ],
        compiler_params=pltpu.CompilerParams(vmem_limit_bytes=53 * 2**20),
        name="hidden_and_first_products",
    )(gate, up, down)


def share_kernel(partner, hidden_ref, down_ref, out_ref, held, sems):
    steps, each, width = held.shape
    start = pl.multiple_of(jnp.bitwise_xor(lax.axis_index("book"), partner) * width, width)
    copies = []
    for step in range(steps):
        rows = pl.ds(step * each, each)
        copies.append(
            pltpu.make_async_copy(
                down_ref.at[rows, pl.ds(start, width)], held.at[step], sems.at[step]
            )
        )
        copies[-1].start()
    total = 0.0
    for step in range(steps):
        copies[step].wait()
        total = total + jnp.dot(
            hidden_ref[:, pl.ds(step * each, each)], held[step], preferred_element_type=f32
        )
    out_ref[...] = total


def share_products(hidden, down, width, partner):
    frames_here, hidden_width = hidden.shape
    steps = max(hidden_width // 512, 1)
    vmem = pl.BlockSpec(memory_space=pltpu.VMEM)
    return pl.pallas_call(
        functools.partial(share_kernel, partner),
        out_shape=jax.ShapeDtypeStruct((frames_here, width), f32),
        in_specs=[vmem, pl.BlockSpec(memory_space=pl.ANY)],
        out_specs=vmem,
        scratch_shapes=[
            pltpu.VMEM((steps, hidden_width // steps, width), bf16),
            pltpu.SemaphoreType.DMA((steps,)),
        ],
        compiler_params=pltpu.CompilerParams(vmem_limit_bytes=53 * 2**20),
        name="share_products",
    )(hidden, down)


def pack_kernel(proj_ref, table_ref, qkv_ref, packed_ref, sems):
    proj_rows, depth = proj_ref.shape
    table_rows = table_ref.shape[0]
    qkv_rows, wide = qkv_ref.shape
    half, extra = qkv_rows // 2, wide - depth
    at_qkv = proj_rows + table_rows
    at_extra = at_qkv + qkv_rows
    moves = [
        (proj_ref, packed_ref.at[pl.ds(0, proj_rows)]),
        (table_ref, packed_ref.at[pl.ds(proj_rows, table_rows)]),
        (qkv_ref.at[:, pl.ds(0, depth)], packed_ref.at[pl.ds(at_qkv, qkv_rows)]),
    ]
    for side in range(2):
        moves.append(
            (
                qkv_ref.at[pl.ds(side * half, half), pl.ds(depth, extra)],
                packed_ref.at[pl.ds(at_extra, half), pl.ds(side * extra, extra)],
            )
        )
    copies = [
        pltpu.make_async_copy(source, target, sems.at[number])
        for number, (source, target) in enumerate(moves)
    ]
    for made in copies:
        made.start()
    for made in copies:
        made.wait()


def pack(proj, table, qkv):
    depth = proj.shape[1]
    rows = proj.shape[0] + table.shape[0] + qkv.shape[0] + qkv.shape[0] // 2
    return pl.pallas_call(
        pack_kernel,
        out_shape=jax.ShapeDtypeStruct((rows, depth), bf16),
        in_specs=[pl.BlockSpec(memory_space=pl.ANY)] * 3,
        out_specs=pl.BlockSpec(memory_space=pltpu.VMEM),
        scratch_shapes=[pltpu.SemaphoreType.DMA((5,))],
        compiler_params=pltpu.CompilerParams(vmem_limit_bytes=4 * 2**20),
        name="pack_weight_rows",
    )(proj, table, qkv)


def cut_kernel(cut, upper_from, lower_from, upper_ref, lower_ref, sems):
    upper = pltpu.make_async_copy(upper_from.at[pl.ds(0, cut)], upper_ref, sems.at[0])
    lower = pltpu.make_async_copy(
        lower_from.at[pl.ds(cut, lower_ref.shape[0])], lower_ref, sems.at[1]
    )
    upper.start()
    lower.start()
    upper.wait()
    lower.wait()


def cut_rows(upper_from, lower_from, cut):
    rows, depth = upper_from.shape
    return pl.pallas_call(
        functools.partial(cut_kernel, cut),
        out_shape=[
            jax.ShapeDtypeStruct((cut, depth), bf16),
            jax.ShapeDtypeStruct((rows - cut, depth), bf16),
        ],
        in_specs=[pl.BlockSpec(memory_space=pl.ANY)] * 2,
        out_specs=[pl.BlockSpec(memory_space=pltpu.VMEM)] * 2,
        scratch_shapes=[pltpu.SemaphoreType.DMA((2,))],
        name="cut_rows",
    )(upper_from, lower_from)


def is_late(m):
    return (m % 2 == 1) & (m != 1)


def hold_blocks(blocks, here, gain_ref, held):
    square = 0.0
    for m, ref in blocks.items():
        book = jnp.bitwise_xor(here, m)
        part = ref[...].astype(f32)
        square = square + jnp.sum(part * part, axis=-1, keepdims=True)
        width = part.shape[1]
        columns = pl.ds(pl.multiple_of(book * width, width), width)
        held[book] = (part * gain_ref[:, columns].astype(f32)).astype(bf16)
    return square


def early_kernel(books, early, pieces, sizes, tokens_ref, gain_ref, *refs):
    blocks = dict(zip(early, refs))
    parts = refs[len(early) : len(early) + len(pieces)]
    outs = refs[len(early) + len(pieces) :]
    projected_ref, square_ref, later_ref, looked_ref, qkv_ref, held, proj, table, sems = outs
    proj_rows, table_rows, qkv_rows = sizes
    here, group = lax.axis_index("book"), lax.axis_index("frames")
    width = held.shape[2]
    per_book = width // proj_rows
    half = qkv_rows // 2
    depth = table.shape[1]
    extra = qkv_ref.shape[1] - depth

    started = []

    def copy(source, target):
        made = pltpu.make_async_copy(source, target, sems.at[len(started)])
        made.start()
        started.append(made)
        return made

    table_copies, proj_copies, qkv_copies = [], [], []
    for (n, first), ref in zip(pieces, parts):
        if first + ref.shape[0] > proj_rows:
            g = jnp.bitwise_xor(group, n)
            start = pl.multiple_of(g * table_rows, table_rows)
            table_copies.append(
                copy(
                    ref.at[pl.ds(proj_rows - first, table_rows)], table.at[pl.ds(start, table_rows)]
                )
            )
    for (n, first), ref in zip(pieces, parts):
        count = min(ref.shape[0], proj_rows - first)
        proj_copies.append(
            copy(ref.at[pl.ds(0, count)], proj.at[pl.ds(n * proj_rows + first, count)])
        )
    for (n, first), ref in zip(pieces, parts):
        if first + ref.shape[0] > proj_rows:
            g = jnp.bitwise_xor(group, n)
            at_qkv = proj_rows - first + table_rows
            at_extra = at_qkv + qkv_rows
            start = pl.multiple_of(g * qkv_rows, qkv_rows)
            qkv_copies.append(
                copy(
                    ref.at[pl.ds(at_qkv, qkv_rows)],
                    qkv_ref.at[pl.ds(start, qkv_rows), pl.ds(0, depth)],
                )
            )
            for side in range(2):
                start = pl.multiple_of(g * qkv_rows + side * half, half)
                qkv_copies.append(
                    copy(
                        ref.at[pl.ds(at_extra, half), pl.ds(side * extra, extra)],
                        qkv_ref.at[pl.ds(start, half), pl.ds(depth, extra)],
                    )
                )

    square_ref[...] = hold_blocks(blocks, here, gain_ref, held)
    codes = lax.broadcasted_iota(jnp.int32, (table.shape[0], tokens_ref.shape[1]), 0)
    matches = (tokens_ref[...] == codes).astype(f32).astype(bf16)
    for made in table_copies:
        made.wait()
    looked = lax.dot_general(
        matches, table[...], (((0,), (0,)), ((), ())), preferred_element_type=f32
    )
    looked_ref[...] = looked.astype(bf16)
    projected_ref[...] = jnp.zeros_like(projected_ref)
    for (n, first), made, ref in zip(pieces, proj_copies, parts):
        count = min(ref.shape[0], proj_rows - first)
        rows = pl.ds(n * proj_rows + first, count)
        owner = jnp.bitwise_xor(group, n)
        book = owner // per_book
        start = pl.multiple_of((owner % per_book) * proj_rows + first, 128)
        late = is_late(jnp.bitwise_xor(here, book))
        made.wait()

        @pl.when(jnp.logical_not(late))
        def _():
            projected_ref[...] += jnp.dot(
                held[book, :, pl.ds(start, count)], proj[rows, :], preferred_element_type=f32
            )

        @pl.when(late)
        def _():
            slot = jnp.bitwise_xor(here, book) // 2 - 1
            later_ref[slot, pl.ds(start, count), :] = proj[rows, :]

    for made in qkv_copies:
        made.wait()


def project_early(tokens, gain, blocks, early, pieces, parts, sizes, wide):
    books = len(blocks)
    frames_here, width = blocks[0].shape
    depth = parts[0].shape[1]
    proj_rows, table_rows, qkv_rows = sizes
    groups = books * width // proj_rows
    vmem = pl.BlockSpec(memory_space=pltpu.VMEM)
    return pl.pallas_call(
        functools.partial(early_kernel, books, early, pieces, sizes),
        out_shape=[
            jax.ShapeDtypeStruct((frames_here, depth), f32),
            jax.ShapeDtypeStruct((frames_here, 1), f32),
            jax.ShapeDtypeStruct((books - len(early), width, depth), bf16),
            jax.ShapeDtypeStruct((frames_here, depth), bf16),
            jax.ShapeDtypeStruct((groups * qkv_rows, wide), bf16),
        ],
        in_specs=[vmem] * (2 + len(early))
        + [pl.BlockSpec(memory_space=pl.ANY)] * len(parts),
        out_specs=[vmem] * 5,
        scratch_shapes=[
            pltpu.VMEM((books, frames_here, width), bf16),
            pltpu.VMEM((books * width, depth), bf16),
            pltpu.VMEM((groups * table_rows, depth), bf16),
            pltpu.SemaphoreType.DMA((len(pieces) + 4 * groups,)),
        ],
        compiler_params=pltpu.CompilerParams(vmem_limit_bytes=45 * 2**20),
        name="early_products_and_lookup",
    )(tokens, gain, *[blocks[m] for m in early], *parts)


def late_kernel(books, late, gain_ref, *refs):
    blocks = dict(zip(late, refs))
    later_from, early_ref, square_ref, looked_ref, depth_gain_ref, qkv_from = refs[
        len(late) : len(late) + 6
    ]
    refs = refs[len(late) + 6 :]
    outs = refs[:books]
    held, packed, later_ref, qkv_ref, sems = refs[books:]
    later_copy = pltpu.make_async_copy(later_from, later_ref, sems.at[0])
    later_copy.start()
    qkv_copy = pltpu.make_async_copy(qkv_from, qkv_ref, sems.at[1])
    qkv_copy.start()
    here = lax.axis_index("book")
    frames_here, width = held.shape[1:]
    square = square_ref[...] + hold_blocks(blocks, here, gain_ref, held)
    projected = early_ref[...]
    later_copy.wait()
    for slot, m in enumerate(late):
        projected = projected + jnp.dot(
            held[jnp.bitwise_xor(here, m)], later_ref[slot], preferred_element_type=f32
        )
    projected = projected * lax.rsqrt(square / (books * width) + 1e-05)
    depth_in = (projected + looked_ref[...].astype(f32)).astype(bf16).astype(f32)
    moment = jnp.mean(depth_in * depth_in, axis=-1, keepdims=True)
    depth_normed = (depth_in * lax.rsqrt(moment + 1e-05) * depth_gain_ref[...].astype(f32)).astype(bf16)
    qkv_copy.wait()
    packed[...] = jnp.dot(depth_normed, qkv_ref[...], preferred_element_type=f32).astype(bf16)
    rows = frames_here // books
    for m in range(books):
        start = pl.multiple_of(jnp.bitwise_xor(here, m) * rows, rows)
        outs[m][...] = packed[pl.ds(start, rows), :]


def project_late(gain, blocks, late, later, projected, square, looked, depth_gain, qkv):
    books = len(blocks)
    frames_here, width = blocks[0].shape
    wide = qkv.shape[1]
    vmem = pl.BlockSpec(memory_space=pltpu.VMEM)
    return pl.pallas_call(
        functools.partial(late_kernel, books, late),
        out_shape=[jax.ShapeDtypeStruct((frames_here // books, wide), bf16)] * books,
        in_specs=[vmem] * (len(late) + 1)
        + [pl.BlockSpec(memory_space=pl.ANY)]
        + [vmem] * 4
        + [pl.BlockSpec(memory_space=pl.ANY)],
        out_specs=[vmem] * books,
        scratch_shapes=[
            pltpu.VMEM((books, frames_here, width), bf16),
            pltpu.VMEM((frames_here, wide), bf16),
            pltpu.VMEM(later.shape, bf16),
            pltpu.VMEM(qkv.shape, bf16),
            pltpu.SemaphoreType.DMA((2,)),
        ],
        compiler_params=pltpu.CompilerParams(vmem_limit_bytes=50 * 2**20),
        name="late_products_and_qkv",
    )(
        gain,
        *[blocks[m] for m in late],
        later,
        projected,
        square,
        looked,
        depth_gain,
        qkv,
    )


def attend_kernel(books, *refs):
    arrived = refs[:books]
    out_ref, inner = refs[books:]
    place = lax.axis_index("book")
    rows, wide = arrived[0].shape
    width = wide // 3
    for m in range(books):
        inner[jnp.bitwise_xor(place, m)] = arrived[m][...]
    head_of_row = lax.broadcasted_iota(jnp.int32, (width, width), 0) // HD
    head_of_column = lax.broadcasted_iota(jnp.int32, (width, width), 1) // HD
    same_head = (head_of_row == head_of_column).astype(f32).astype(bf16)
    keys_all = [inner[j, :, width : 2 * width].astype(f32) for j in range(books)]
    values_all = [inner[j, :, 2 * width :].astype(f32) for j in range(books)]
    contexts = []
    for k in range(books):
        query = inner[k, :, :width].astype(f32) * HD ** (-0.5)
        products = jnp.concatenate([query * keys_all[j] for j in range(k + 1)], axis=0)
        high = products.astype(bf16)
        low = (products - high.astype(f32)).astype(bf16)
        scores = jnp.dot(high, same_head, preferred_element_type=f32) + jnp.dot(
            low, same_head, preferred_element_type=f32
        )
        scores = [scores[j * rows : (j + 1) * rows] for j in range(k + 1)]
        peak = functools.reduce(jnp.maximum, scores)
        expo = [jnp.exp(score - peak) for score in scores]
        total = functools.reduce(jnp.add, expo)
        context = 0.0
        for j in range(k + 1):
            probability = (expo[j] / total).astype(bf16).astype(f32)
            context = context + probability * values_all[j]
        contexts.append(context)
    out_ref[...] = jnp.stack(contexts, axis=1).astype(bf16)


def attend(arrived):
    books = len(arrived)
    rows, wide = arrived[0].shape
    vmem = pl.BlockSpec(memory_space=pltpu.VMEM)
    return pl.pallas_call(
        functools.partial(attend_kernel, books),
        out_shape=jax.ShapeDtypeStruct((rows, books, wide // 3), bf16),
        in_specs=[vmem] * books,
        out_specs=vmem,
        scratch_shapes=[pltpu.VMEM((books, rows, wide), bf16)],
        compiler_params=pltpu.CompilerParams(vmem_limit_bytes=16 * 2**20),
        name="attend_books",
    )(*arrived)


def swap(value, axis, distance):
    return lax.ppermute(value, axis, [(i, i ^ distance) for i in range(lax.axis_size(axis))])


def after(value, *others):
    return lax.optimization_barrier((value, *others))[0]


def bits_of(number):
    return [1 << place for place in range(number.bit_length()) if number >> place & 1]


def per_device(
    gate_pre,
    up_pre,
    down_weight,
    residual,
    out_gain,
    in_proj,
    embedding,
    token_ids,
    depth_gain,
    qkv_weight,
):
    books = lax.axis_size("book")
    groups = lax.axis_size("frames")
    here = lax.axis_index("book").astype(jnp.int32)
    width = residual.shape[1]
    proj_rows = in_proj.shape[1]
    gain = out_gain[None]

    hidden, first = first_products(gate_pre, up_pre, down_weight, width)

    def share(m, *others):
        factor = after(hidden, *others) if others else hidden
        if m == 0:
            block = lax.dynamic_slice_in_dim(
                down_weight, lax.axis_index("book") * width, width, 1
            )
            return jnp.dot(factor, block, preferred_element_type=f32)
        return share_products(factor, down_weight, width, m)

    rows = pack(*after((in_proj[0], embedding[0], qkv_weight[0]), first))
    parts = {0: [(0, rows)]}
    near = [n for n in range(2, groups, 2) if len(bits_of(n)) == 1]
    for n in near:
        parts[n] = [(0, swap(rows, "frames", n))]

    sums = {books - 1: first}
    parts[1] = [(0, swap(rows, "frames", 1))]
    sums[books - 2] = lax.optimization_barrier(share(books - 2, rows))
    for n in range(books - 3, 0, -1):
        sums[n] = lax.optimization_barrier(share(n, rows))
    came = swap(sums.pop(books - 1).astype(bf16), "book", 1)
    came = after(came, *[sums[n] for n in range(1, books - 1)])
    onward = (sums.pop(books - 2) + came.astype(f32)).astype(bf16)
    far_came = swap(onward, "book", 2)
    last = lax.optimization_barrier(share(0, came, parts[1][0][1]))
    sums[0] = last + residual.astype(f32)
    for m in range(books - 3, 0, -2):
        near_came = swap(after(sums.pop(m).astype(bf16), onward, last), "book", 1)
        sums[m ^ 1] = sums[m ^ 1] + near_came.astype(f32)
    sums[(books - 2) ^ 2] = sums[(books - 2) ^ 2] + far_came.astype(f32)
    distance = 2
    while distance < books:
        for m in range(books - distance, 0, -2 * distance):
            if m in sums:
                came = swap(sums.pop(m).astype(bf16), "book", distance)
                sums[m ^ distance] = sums[m ^ distance] + came.astype(f32)
        distance *= 2

    blocks = {0: sums[0].astype(bf16)}

    arrived = after([parts[n][0][1] for n in near], blocks[0])
    for n, value in zip(near, arrived):
        parts[n] = [(0, value)]
    cut = rows.shape[0] // 2 // 128 * 128
    for n in range(2, groups, 2):
        sides = bits_of(n)
        if n in near:
            continue
        if len(sides) == 2 and 0 < cut < proj_rows:
            upper, lower = cut_rows(parts[n ^ sides[0]][0][1], parts[n ^ sides[1]][0][1], cut)
            upper = swap(upper, "frames", sides[0])
            lower = swap(lower, "frames", sides[1])
            parts[n] = [(0, upper), (cut, lower)]
        else:
            parts[n] = [(0, swap(rows, "frames", n))]
    for n in range(2, groups, 2):
        parts[n + 1] = [(first, swap(value, "frames", 1)) for first, value in parts[n]]

    near_there = [parts[n + 1][0][1] for n in near]
    distance = books // 2
    while distance:
        for m in sorted(blocks):
            going = blocks[m]
            if m:
                going = after(going, blocks[distance])
            elif distance == 1:
                going = after(going, *near_there)
            blocks[m ^ distance] = swap(going, "book", distance)
        distance //= 2

    pieces = [(n, first) for n in range(groups) for first, _ in parts[n]]
    arrived = [value for n in range(groups) for _, value in parts[n]]
    sizes = proj_rows, embedding.shape[1], qkv_weight.shape[1]
    early = [m for m in range(books) if not is_late(m)]
    late = [m for m in range(books) if is_late(m)]
    projected, square, later, looked, qkv = project_early(
        token_ids.reshape(1, -1), gain, blocks, early, pieces, arrived, sizes, qkv_weight.shape[2]
    )
    packed = project_late(
        gain, blocks, late, later, projected, square, looked, depth_gain, qkv
    )
    far = {m: swap(packed[m], "book", m) for m in range(books - 1, 0, -1)}
    return attend([packed[0]] + [far[m] for m in range(1, books)])


def solution(mesh):
    in_specs = (
        P("frames", "book"),
        P("frames", "book"),
        P("book", None),
        P("frames", "book"),
        P(),
        P("book", "frames", None),
        P("book", "frames", None),
        P("frames", "book"),
        P("book", None),
        P("book", "frames", None),
    )
    out_specs = P(("frames", "book"), None, None)
    return jax.shard_map(
        per_device, mesh=mesh, in_specs=in_specs, out_specs=out_specs, check_vma=False
    )
```

```python
import functools

import jax
import jax.numpy as jnp
from jax import lax
from jax.experimental import pallas as pl
from jax.experimental.pallas import tpu as pltpu
from jax.sharding import PartitionSpec as P

H = 8
HD = 64
f32, bf16 = jnp.float32, jnp.bfloat16


def first_kernel(gate_ref, up_ref, down_ref, hidden_ref, first_ref, gates, ups, held, sems):
    steps, each, width = held.shape
    books = down_ref.shape[1] // width
    start = pl.multiple_of(jnp.bitwise_xor(lax.axis_index("book"), books - 1) * width, width)
    copies = []
    for step in range(steps):
        rows = pl.ds(step * each, each)
        moves = [
            (gate_ref.at[:, rows], gates.at[step]),
            (up_ref.at[:, rows], ups.at[step]),
            (down_ref.at[rows, pl.ds(start, width)], held.at[step]),
        ]
        for kind, (source, target) in enumerate(moves):
            copies.append(pltpu.make_async_copy(source, target, sems.at[3 * step + kind]))
            copies[-1].start()
    total = 0.0
    for step in range(steps):
        copies[3 * step].wait()
        copies[3 * step + 1].wait()
        gate = gates[step].astype(f32)
        hidden = gate / (1.0 + jnp.exp(-gate)) * ups[step].astype(f32)
        hidden = hidden.astype(bf16)
        hidden_ref[:, pl.ds(step * each, each)] = hidden
        copies[3 * step + 2].wait()
        total = total + jnp.dot(hidden, held[step], preferred_element_type=f32)
    first_ref[...] = total.astype(bf16)


def first_products(gate, up, down, width):
    frames_here, hidden_width = gate.shape
    steps = max(hidden_width // 512, 1)
    vmem = pl.BlockSpec(memory_space=pltpu.VMEM)
    return pl.pallas_call(
        first_kernel,
        out_shape=[
            jax.ShapeDtypeStruct((frames_here, hidden_width), bf16),
            jax.ShapeDtypeStruct((frames_here, width), bf16),
        ],
        in_specs=[pl.BlockSpec(memory_space=pl.ANY)] * 3,
        out_specs=[vmem] * 2,
        scratch_shapes=[
            pltpu.VMEM((steps, frames_here, hidden_width // steps), bf16),
            pltpu.VMEM((steps, frames_here, hidden_width // steps), bf16),
            pltpu.VMEM((steps, hidden_width // steps, width), bf16),
            pltpu.SemaphoreType.DMA((3 * steps,)),
        ],
        compiler_params=pltpu.CompilerParams(vmem_limit_bytes=53 * 2**20),
        name="hidden_and_first_products",
    )(gate, up, down)


def share_kernel(partner, hidden_ref, down_ref, out_ref, held, sems):
    steps, each, width = held.shape
    start = pl.multiple_of(jnp.bitwise_xor(lax.axis_index("book"), partner) * width, width)
    copies = []
    for step in range(steps):
        rows = pl.ds(step * each, each)
        copies.append(
            pltpu.make_async_copy(
                down_ref.at[rows, pl.ds(start, width)], held.at[step], sems.at[step]
            )
        )
        copies[-1].start()
    total = 0.0
    for step in range(steps):
        copies[step].wait()
        total = total + jnp.dot(
            hidden_ref[:, pl.ds(step * each, each)], held[step], preferred_element_type=f32
        )
    out_ref[...] = total


def share_products(hidden, down, width, partner):
    frames_here, hidden_width = hidden.shape
    steps = max(hidden_width // 512, 1)
    vmem = pl.BlockSpec(memory_space=pltpu.VMEM)
    return pl.pallas_call(
        functools.partial(share_kernel, partner),
        out_shape=jax.ShapeDtypeStruct((frames_here, width), f32),
        in_specs=[vmem, pl.BlockSpec(memory_space=pl.ANY)],
        out_specs=vmem,
        scratch_shapes=[
            pltpu.VMEM((steps, hidden_width // steps, width), bf16),
            pltpu.SemaphoreType.DMA((steps,)),
        ],
        compiler_params=pltpu.CompilerParams(vmem_limit_bytes=53 * 2**20),
        name="share_products",
    )(hidden, down)


def pack_kernel(proj_ref, table_ref, qkv_ref, packed_ref, sems):
    proj_rows, depth = proj_ref.shape
    table_rows = table_ref.shape[0]
    qkv_rows, wide = qkv_ref.shape
    half, extra = qkv_rows // 2, wide - depth
    at_qkv = proj_rows + table_rows
    at_extra = at_qkv + qkv_rows
    moves = [
        (proj_ref, packed_ref.at[pl.ds(0, proj_rows)]),
        (table_ref, packed_ref.at[pl.ds(proj_rows, table_rows)]),
        (qkv_ref.at[:, pl.ds(0, depth)], packed_ref.at[pl.ds(at_qkv, qkv_rows)]),
    ]
    for side in range(2):
        moves.append(
            (
                qkv_ref.at[pl.ds(side * half, half), pl.ds(depth, extra)],
                packed_ref.at[pl.ds(at_extra, half), pl.ds(side * extra, extra)],
            )
        )
    copies = [
        pltpu.make_async_copy(source, target, sems.at[number])
        for number, (source, target) in enumerate(moves)
    ]
    for made in copies:
        made.start()
    for made in copies:
        made.wait()


def pack(proj, table, qkv):
    depth = proj.shape[1]
    rows = proj.shape[0] + table.shape[0] + qkv.shape[0] + qkv.shape[0] // 2
    return pl.pallas_call(
        pack_kernel,
        out_shape=jax.ShapeDtypeStruct((rows, depth), bf16),
        in_specs=[pl.BlockSpec(memory_space=pl.ANY)] * 3,
        out_specs=pl.BlockSpec(memory_space=pltpu.VMEM),
        scratch_shapes=[pltpu.SemaphoreType.DMA((5,))],
        compiler_params=pltpu.CompilerParams(vmem_limit_bytes=4 * 2**20),
        name="pack_weight_rows",
    )(proj, table, qkv)


def cut_kernel(cut, upper_from, lower_from, upper_ref, lower_ref, sems):
    upper = pltpu.make_async_copy(upper_from.at[pl.ds(0, cut)], upper_ref, sems.at[0])
    lower = pltpu.make_async_copy(
        lower_from.at[pl.ds(cut, lower_ref.shape[0])], lower_ref, sems.at[1]
    )
    upper.start()
    lower.start()
    upper.wait()
    lower.wait()


def cut_rows(upper_from, lower_from, cut):
    rows, depth = upper_from.shape
    return pl.pallas_call(
        functools.partial(cut_kernel, cut),
        out_shape=[
            jax.ShapeDtypeStruct((cut, depth), bf16),
            jax.ShapeDtypeStruct((rows - cut, depth), bf16),
        ],
        in_specs=[pl.BlockSpec(memory_space=pl.ANY)] * 2,
        out_specs=[pl.BlockSpec(memory_space=pltpu.VMEM)] * 2,
        scratch_shapes=[pltpu.SemaphoreType.DMA((2,))],
        name="cut_rows",
    )(upper_from, lower_from)


def is_late(m):
    return (m % 2 == 1) & (m != 1)


def hold_blocks(blocks, here, gain_ref, held):
    square = 0.0
    for m, ref in blocks.items():
        book = jnp.bitwise_xor(here, m)
        part = ref[...].astype(f32)
        square = square + jnp.sum(part * part, axis=-1, keepdims=True)
        width = part.shape[1]
        columns = pl.ds(pl.multiple_of(book * width, width), width)
        held[book] = (part * gain_ref[:, columns].astype(f32)).astype(bf16)
    return square


def early_kernel(books, early, pieces, sizes, tokens_ref, gain_ref, *refs):
    blocks = dict(zip(early, refs))
    parts = refs[len(early) : len(early) + len(pieces)]
    outs = refs[len(early) + len(pieces) :]
    projected_ref, square_ref, later_ref, looked_ref, qkv_ref, held, proj, table, sems = outs
    proj_rows, table_rows, qkv_rows = sizes
    here, group = lax.axis_index("book"), lax.axis_index("frames")
    width = held.shape[2]
    per_book = width // proj_rows
    half = qkv_rows // 2
    depth = table.shape[1]
    extra = qkv_ref.shape[1] - depth

    started = []

    def copy(source, target):
        made = pltpu.make_async_copy(source, target, sems.at[len(started)])
        made.start()
        started.append(made)
        return made

    table_copies, proj_copies, qkv_copies = [], [], []
    for (n, first), ref in zip(pieces, parts):
        if first + ref.shape[0] > proj_rows:
            g = jnp.bitwise_xor(group, n)
            start = pl.multiple_of(g * table_rows, table_rows)
            table_copies.append(
                copy(
                    ref.at[pl.ds(proj_rows - first, table_rows)], table.at[pl.ds(start, table_rows)]
                )
            )
    for (n, first), ref in zip(pieces, parts):
        count = min(ref.shape[0], proj_rows - first)
        proj_copies.append(
            copy(ref.at[pl.ds(0, count)], proj.at[pl.ds(n * proj_rows + first, count)])
        )
    for (n, first), ref in zip(pieces, parts):
        if first + ref.shape[0] > proj_rows:
            g = jnp.bitwise_xor(group, n)
            at_qkv = proj_rows - first + table_rows
            at_extra = at_qkv + qkv_rows
            start = pl.multiple_of(g * qkv_rows, qkv_rows)
            qkv_copies.append(
                copy(
                    ref.at[pl.ds(at_qkv, qkv_rows)],
                    qkv_ref.at[pl.ds(start, qkv_rows), pl.ds(0, depth)],
                )
            )
            for side in range(2):
                start = pl.multiple_of(g * qkv_rows + side * half, half)
                qkv_copies.append(
                    copy(
                        ref.at[pl.ds(at_extra, half), pl.ds(side * extra, extra)],
                        qkv_ref.at[pl.ds(start, half), pl.ds(depth, extra)],
                    )
                )

    square_ref[...] = hold_blocks(blocks, here, gain_ref, held)
    codes = lax.broadcasted_iota(jnp.int32, (table.shape[0], tokens_ref.shape[1]), 0)
    matches = (tokens_ref[...] == codes).astype(f32).astype(bf16)
    for made in table_copies:
        made.wait()
    looked = lax.dot_general(
        matches, table[...], (((0,), (0,)), ((), ())), preferred_element_type=f32
    )
    looked_ref[...] = looked.astype(bf16)
    projected_ref[...] = jnp.zeros_like(projected_ref)
    for (n, first), made, ref in zip(pieces, proj_copies, parts):
        count = min(ref.shape[0], proj_rows - first)
        rows = pl.ds(n * proj_rows + first, count)
        owner = jnp.bitwise_xor(group, n)
        book = owner // per_book
        start = pl.multiple_of((owner % per_book) * proj_rows + first, 128)
        late = is_late(jnp.bitwise_xor(here, book))
        made.wait()

        @pl.when(jnp.logical_not(late))
        def _():
            projected_ref[...] += jnp.dot(
                held[book, :, pl.ds(start, count)], proj[rows, :], preferred_element_type=f32
            )

        @pl.when(late)
        def _():
            slot = jnp.bitwise_xor(here, book) // 2 - 1
            later_ref[slot, pl.ds(start, count), :] = proj[rows, :]

    for made in qkv_copies:
        made.wait()


def project_early(tokens, gain, blocks, early, pieces, parts, sizes, wide):
    books = len(blocks)
    frames_here, width = blocks[0].shape
    depth = parts[0].shape[1]
    proj_rows, table_rows, qkv_rows = sizes
    groups = books * width // proj_rows
    vmem = pl.BlockSpec(memory_space=pltpu.VMEM)
    return pl.pallas_call(
        functools.partial(early_kernel, books, early, pieces, sizes),
        out_shape=[
            jax.ShapeDtypeStruct((frames_here, depth), f32),
            jax.ShapeDtypeStruct((frames_here, 1), f32),
            jax.ShapeDtypeStruct((books - len(early), width, depth), bf16),
            jax.ShapeDtypeStruct((frames_here, depth), bf16),
            jax.ShapeDtypeStruct((groups * qkv_rows, wide), bf16),
        ],
        in_specs=[vmem] * (2 + len(early))
        + [pl.BlockSpec(memory_space=pl.ANY)] * len(parts),
        out_specs=[vmem] * 5,
        scratch_shapes=[
            pltpu.VMEM((books, frames_here, width), bf16),
            pltpu.VMEM((books * width, depth), bf16),
            pltpu.VMEM((groups * table_rows, depth), bf16),
            pltpu.SemaphoreType.DMA((len(pieces) + 4 * groups,)),
        ],
        compiler_params=pltpu.CompilerParams(vmem_limit_bytes=45 * 2**20),
        name="early_products_and_lookup",
    )(tokens, gain, *[blocks[m] for m in early], *parts)


def late_kernel(books, late, gain_ref, *refs):
    blocks = dict(zip(late, refs))
    later_from, early_ref, square_ref, looked_ref, depth_gain_ref, qkv_from = refs[
        len(late) : len(late) + 6
    ]
    refs = refs[len(late) + 6 :]
    outs = refs[:books]
    held, packed, later_ref, qkv_ref, sems = refs[books:]
    later_copy = pltpu.make_async_copy(later_from, later_ref, sems.at[0])
    later_copy.start()
    qkv_copy = pltpu.make_async_copy(qkv_from, qkv_ref, sems.at[1])
    qkv_copy.start()
    here = lax.axis_index("book")
    frames_here, width = held.shape[1:]
    square = square_ref[...] + hold_blocks(blocks, here, gain_ref, held)
    projected = early_ref[...]
    later_copy.wait()
    for slot, m in enumerate(late):
        projected = projected + jnp.dot(
            held[jnp.bitwise_xor(here, m)], later_ref[slot], preferred_element_type=f32
        )
    projected = projected * lax.rsqrt(square / (books * width) + 1e-05)
    depth_in = (projected + looked_ref[...].astype(f32)).astype(bf16).astype(f32)
    moment = jnp.mean(depth_in * depth_in, axis=-1, keepdims=True)
    depth_normed = (depth_in * lax.rsqrt(moment + 1e-05) * depth_gain_ref[...].astype(f32)).astype(bf16)
    qkv_copy.wait()
    packed[...] = jnp.dot(depth_normed, qkv_ref[...], preferred_element_type=f32).astype(bf16)
    rows = frames_here // books
    for m in range(books):
        start = pl.multiple_of(jnp.bitwise_xor(here, m) * rows, rows)
        outs[m][...] = packed[pl.ds(start, rows), :]


def project_late(gain, blocks, late, later, projected, square, looked, depth_gain, qkv):
    books = len(blocks)
    frames_here, width = blocks[0].shape
    wide = qkv.shape[1]
    vmem = pl.BlockSpec(memory_space=pltpu.VMEM)
    return pl.pallas_call(
        functools.partial(late_kernel, books, late),
        out_shape=[jax.ShapeDtypeStruct((frames_here // books, wide), bf16)] * books,
        in_specs=[vmem] * (len(late) + 1)
        + [pl.BlockSpec(memory_space=pl.ANY)]
        + [vmem] * 4
        + [pl.BlockSpec(memory_space=pl.ANY)],
        out_specs=[vmem] * books,
        scratch_shapes=[
            pltpu.VMEM((books, frames_here, width), bf16),
            pltpu.VMEM((frames_here, wide), bf16),
            pltpu.VMEM(later.shape, bf16),
            pltpu.VMEM(qkv.shape, bf16),
            pltpu.SemaphoreType.DMA((2,)),
        ],
        compiler_params=pltpu.CompilerParams(vmem_limit_bytes=50 * 2**20),
        name="late_products_and_qkv",
    )(
        gain,
        *[blocks[m] for m in late],
        later,
        projected,
        square,
        looked,
        depth_gain,
        qkv,
    )


def attend_kernel(books, *refs):
    arrived = refs[:books]
    out_ref, inner = refs[books:]
    place = lax.axis_index("book")
    rows, wide = arrived[0].shape
    width = wide // 3
    for m in range(books):
        inner[jnp.bitwise_xor(place, m)] = arrived[m][...]
    head_of_row = lax.broadcasted_iota(jnp.int32, (width, width), 0) // HD
    head_of_column = lax.broadcasted_iota(jnp.int32, (width, width), 1) // HD
    same_head = (head_of_row == head_of_column).astype(f32).astype(bf16)
    keys_all = [inner[j, :, width : 2 * width].astype(f32) for j in range(books)]
    values_all = [inner[j, :, 2 * width :].astype(f32) for j in range(books)]
    contexts = []
    for k in range(books):
        query = inner[k, :, :width].astype(f32) * HD ** (-0.5)
        products = jnp.concatenate([query * keys_all[j] for j in range(k + 1)], axis=0)
        high = products.astype(bf16)
        low = (products - high.astype(f32)).astype(bf16)
        scores = jnp.dot(high, same_head, preferred_element_type=f32) + jnp.dot(
            low, same_head, preferred_element_type=f32
        )
        scores = [scores[j * rows : (j + 1) * rows] for j in range(k + 1)]
        peak = functools.reduce(jnp.maximum, scores)
        expo = [jnp.exp(score - peak) for score in scores]
        total = functools.reduce(jnp.add, expo)
        context = 0.0
        for j in range(k + 1):
            probability = (expo[j] / total).astype(bf16).astype(f32)
            context = context + probability * values_all[j]
        contexts.append(context)
    out_ref[...] = jnp.stack(contexts, axis=1).astype(bf16)


def attend(arrived):
    books = len(arrived)
    rows, wide = arrived[0].shape
    vmem = pl.BlockSpec(memory_space=pltpu.VMEM)
    return pl.pallas_call(
        functools.partial(attend_kernel, books),
        out_shape=jax.ShapeDtypeStruct((rows, books, wide // 3), bf16),
        in_specs=[vmem] * books,
        out_specs=vmem,
        scratch_shapes=[pltpu.VMEM((books, rows, wide), bf16)],
        compiler_params=pltpu.CompilerParams(vmem_limit_bytes=16 * 2**20),
        name="attend_books",
    )(*arrived)


def swap(value, axis, distance):
    return lax.ppermute(value, axis, [(i, i ^ distance) for i in range(lax.axis_size(axis))])


def after(value, *others):
    return lax.optimization_barrier((value, *others))[0]


def bits_of(number):
    return [1 << place for place in range(number.bit_length()) if number >> place & 1]


def per_device(
    gate_pre,
    up_pre,
    down_weight,
    residual,
    out_gain,
    in_proj,
    embedding,
    token_ids,
    depth_gain,
    qkv_weight,
):
    books = lax.axis_size("book")
    groups = lax.axis_size("frames")
    here = lax.axis_index("book").astype(jnp.int32)
    width = residual.shape[1]
    proj_rows = in_proj.shape[1]
    gain = out_gain[None]

    hidden, first = first_products(gate_pre, up_pre, down_weight, width)

    def share(m, *others):
        factor = after(hidden, *others) if others else hidden
        if m == 0:
            total = 0.0
            each = factor.shape[1] // 4
            for step in range(4):
                block = lax.dynamic_slice(
                    down_weight, (step * each, lax.axis_index("book") * width), (each, width)
                )
                part = lax.slice_in_dim(factor, step * each, (step + 1) * each, axis=1)
                total = total + jnp.dot(part, block, preferred_element_type=f32)
                total = lax.optimization_barrier(total)
            return total
        return share_products(factor, down_weight, width, m)

    rows = pack(*after((in_proj[0], embedding[0], qkv_weight[0]), first))
    parts = {0: [(0, rows)]}
    near = [n for n in range(2, groups, 2) if len(bits_of(n)) == 1]
    for n in near:
        parts[n] = [(0, swap(rows, "frames", n))]

    sums = {books - 1: first}
    parts[1] = [(0, swap(rows, "frames", 1))]
    sums[books - 2] = lax.optimization_barrier(share(books - 2, rows))
    for n in range(books - 3, 0, -1):
        sums[n] = lax.optimization_barrier(share(n, rows))
    came = swap(sums.pop(books - 1).astype(bf16), "book", 1)
    came = after(came, *[sums[n] for n in range(1, books - 1)])
    onward = (sums.pop(books - 2) + came.astype(f32)).astype(bf16)
    far_came = swap(onward, "book", 2)
    last = lax.optimization_barrier(share(0, came, parts[1][0][1]))
    sums[0] = last + residual.astype(f32)
    for m in range(books - 3, 0, -2):
        near_came = swap(after(sums.pop(m).astype(bf16), onward), "book", 1)
        sums[m ^ 1] = sums[m ^ 1] + near_came.astype(f32)
    sums[(books - 2) ^ 2] = sums[(books - 2) ^ 2] + far_came.astype(f32)
    distance = 2
    while distance < books:
        for m in range(books - distance, 0, -2 * distance):
            if m in sums:
                came = swap(sums.pop(m).astype(bf16), "book", distance)
                sums[m ^ distance] = sums[m ^ distance] + came.astype(f32)
        distance *= 2

    blocks = {0: sums[0].astype(bf16)}

    arrived = after([parts[n][0][1] for n in near], blocks[0])
    for n, value in zip(near, arrived):
        parts[n] = [(0, value)]
    cut = rows.shape[0] // 2 // 128 * 128
    for n in range(2, groups, 2):
        sides = bits_of(n)
        if n in near:
            continue
        if len(sides) == 2 and 0 < cut < proj_rows:
            upper, lower = cut_rows(parts[n ^ sides[0]][0][1], parts[n ^ sides[1]][0][1], cut)
            upper = swap(upper, "frames", sides[0])
            lower = swap(lower, "frames", sides[1])
            parts[n] = [(0, upper), (cut, lower)]
        else:
            parts[n] = [(0, swap(rows, "frames", n))]
    for n in range(2, groups, 2):
        parts[n + 1] = [(first, swap(value, "frames", 1)) for first, value in parts[n]]

    near_there = [parts[n + 1][0][1] for n in near]
    distance = books // 2
    while distance:
        for m in sorted(blocks):
            going = blocks[m]
            if m:
                going = after(going, blocks[distance])
            elif distance == 1:
                going = after(going, *near_there)
            blocks[m ^ distance] = swap(going, "book", distance)
        distance //= 2

    pieces = [(n, first) for n in range(groups) for first, _ in parts[n]]
    arrived = [value for n in range(groups) for _, value in parts[n]]
    sizes = proj_rows, embedding.shape[1], qkv_weight.shape[1]
    early = [m for m in range(books) if not is_late(m)]
    late = [m for m in range(books) if is_late(m)]
    projected, square, later, looked, qkv = project_early(
        token_ids.reshape(1, -1), gain, blocks, early, pieces, arrived, sizes, qkv_weight.shape[2]
    )
    packed = project_late(
        gain, blocks, late, later, projected, square, looked, depth_gain, qkv
    )
    far = {m: swap(packed[m], "book", m) for m in range(books - 1, 0, -1)}
    return attend([packed[0]] + [far[m] for m in range(1, books)])


def solution(mesh):
    in_specs = (
        P("frames", "book"),
        P("frames", "book"),
        P("book", None),
        P("frames", "book"),
        P(),
        P("book", "frames", None),
        P("book", "frames", None),
        P("frames", "book"),
        P("book", None),
        P("book", "frames", None),
    )
    out_specs = P(("frames", "book"), None, None)
    return jax.shard_map(
        per_device, mesh=mesh, in_specs=in_specs, out_specs=out_specs, check_vma=False
    )
```

```python
import functools

import jax
import jax.numpy as jnp
from jax import lax
from jax.experimental import pallas as pl
from jax.experimental.pallas import tpu as pltpu
from jax.sharding import PartitionSpec as P

H = 8
HD = 64
f32, bf16 = jnp.float32, jnp.bfloat16


def first_kernel(gate_ref, up_ref, down_ref, hidden_ref, first_ref, gates, ups, held, sems):
    steps, each, width = held.shape
    books = down_ref.shape[1] // width
    start = pl.multiple_of(jnp.bitwise_xor(lax.axis_index("book"), books - 1) * width, width)
    copies = []
    for step in range(steps):
        rows = pl.ds(step * each, each)
        moves = [
            (gate_ref.at[:, rows], gates.at[step]),
            (up_ref.at[:, rows], ups.at[step]),
            (down_ref.at[rows, pl.ds(start, width)], held.at[step]),
        ]
        for kind, (source, target) in enumerate(moves):
            copies.append(pltpu.make_async_copy(source, target, sems.at[3 * step + kind]))
            copies[-1].start()
    total = 0.0
    for step in range(steps):
        copies[3 * step].wait()
        copies[3 * step + 1].wait()
        gate = gates[step].astype(f32)
        hidden = gate / (1.0 + jnp.exp(-gate)) * ups[step].astype(f32)
        hidden = hidden.astype(bf16)
        hidden_ref[:, pl.ds(step * each, each)] = hidden
        copies[3 * step + 2].wait()
        total = total + jnp.dot(hidden, held[step], preferred_element_type=f32)
    first_ref[...] = total.astype(bf16)


def first_products(gate, up, down, width):
    frames_here, hidden_width = gate.shape
    steps = max(hidden_width // 512, 1)
    vmem = pl.BlockSpec(memory_space=pltpu.VMEM)
    return pl.pallas_call(
        first_kernel,
        out_shape=[
            jax.ShapeDtypeStruct((frames_here, hidden_width), bf16),
            jax.ShapeDtypeStruct((frames_here, width), bf16),
        ],
        in_specs=[pl.BlockSpec(memory_space=pl.ANY)] * 3,
        out_specs=[vmem] * 2,
        scratch_shapes=[
            pltpu.VMEM((steps, frames_here, hidden_width // steps), bf16),
            pltpu.VMEM((steps, frames_here, hidden_width // steps), bf16),
            pltpu.VMEM((steps, hidden_width // steps, width), bf16),
            pltpu.SemaphoreType.DMA((3 * steps,)),
        ],
        compiler_params=pltpu.CompilerParams(vmem_limit_bytes=53 * 2**20),
        name="hidden_and_first_products",
    )(gate, up, down)


def share_kernel(partner, hidden_ref, down_ref, out_ref, held, sems):
    steps, each, width = held.shape
    start = pl.multiple_of(jnp.bitwise_xor(lax.axis_index("book"), partner) * width, width)
    copies = []
    for step in range(steps):
        rows = pl.ds(step * each, each)
        copies.append(
            pltpu.make_async_copy(
                down_ref.at[rows, pl.ds(start, width)], held.at[step], sems.at[step]
            )
        )
        copies[-1].start()
    total = 0.0
    for step in range(steps):
        copies[step].wait()
        total = total + jnp.dot(
            hidden_ref[:, pl.ds(step * each, each)], held[step], preferred_element_type=f32
        )
    out_ref[...] = total.astype(out_ref.dtype)


def share_products(hidden, down, width, partner):
    frames_here, hidden_width = hidden.shape
    steps = max(hidden_width // 512, 1)
    vmem = pl.BlockSpec(memory_space=pltpu.VMEM)
    return pl.pallas_call(
        functools.partial(share_kernel, partner),
        out_shape=jax.ShapeDtypeStruct((frames_here, width), bf16 if partner % 2 else f32),
        in_specs=[vmem, pl.BlockSpec(memory_space=pl.ANY)],
        out_specs=vmem,
        scratch_shapes=[
            pltpu.VMEM((steps, hidden_width // steps, width), bf16),
            pltpu.SemaphoreType.DMA((steps,)),
        ],
        compiler_params=pltpu.CompilerParams(vmem_limit_bytes=53 * 2**20),
        name="share_products",
    )(hidden, down)


def pack_kernel(proj_ref, table_ref, qkv_ref, packed_ref, sems):
    proj_rows, depth = proj_ref.shape
    table_rows = table_ref.shape[0]
    qkv_rows, wide = qkv_ref.shape
    half, extra = qkv_rows // 2, wide - depth
    at_qkv = proj_rows + table_rows
    at_extra = at_qkv + qkv_rows
    moves = [
        (proj_ref, packed_ref.at[pl.ds(0, proj_rows)]),
        (table_ref, packed_ref.at[pl.ds(proj_rows, table_rows)]),
        (qkv_ref.at[:, pl.ds(0, depth)], packed_ref.at[pl.ds(at_qkv, qkv_rows)]),
    ]
    for side in range(2):
        moves.append(
            (
                qkv_ref.at[pl.ds(side * half, half), pl.ds(depth, extra)],
                packed_ref.at[pl.ds(at_extra, half), pl.ds(side * extra, extra)],
            )
        )
    copies = [
        pltpu.make_async_copy(source, target, sems.at[number])
        for number, (source, target) in enumerate(moves)
    ]
    for made in copies:
        made.start()
    for made in copies:
        made.wait()


def pack(proj, table, qkv):
    depth = proj.shape[1]
    rows = proj.shape[0] + table.shape[0] + qkv.shape[0] + qkv.shape[0] // 2
    return pl.pallas_call(
        pack_kernel,
        out_shape=jax.ShapeDtypeStruct((rows, depth), bf16),
        in_specs=[pl.BlockSpec(memory_space=pl.ANY)] * 3,
        out_specs=pl.BlockSpec(memory_space=pltpu.VMEM),
        scratch_shapes=[pltpu.SemaphoreType.DMA((5,))],
        compiler_params=pltpu.CompilerParams(vmem_limit_bytes=4 * 2**20),
        name="pack_weight_rows",
    )(proj, table, qkv)


def cut_kernel(cut, upper_from, lower_from, upper_ref, lower_ref, sems):
    upper = pltpu.make_async_copy(upper_from.at[pl.ds(0, cut)], upper_ref, sems.at[0])
    lower = pltpu.make_async_copy(
        lower_from.at[pl.ds(cut, lower_ref.shape[0])], lower_ref, sems.at[1]
    )
    upper.start()
    lower.start()
    upper.wait()
    lower.wait()


def cut_rows(upper_from, lower_from, cut):
    rows, depth = upper_from.shape
    return pl.pallas_call(
        functools.partial(cut_kernel, cut),
        out_shape=[
            jax.ShapeDtypeStruct((cut, depth), bf16),
            jax.ShapeDtypeStruct((rows - cut, depth), bf16),
        ],
        in_specs=[pl.BlockSpec(memory_space=pl.ANY)] * 2,
        out_specs=[pl.BlockSpec(memory_space=pltpu.VMEM)] * 2,
        scratch_shapes=[pltpu.SemaphoreType.DMA((2,))],
        name="cut_rows",
    )(upper_from, lower_from)


def is_late(m):
    return (m % 2 == 1) & (m != 1)


def hold_blocks(blocks, here, gain_ref, held):
    square = 0.0
    for m, ref in blocks.items():
        book = jnp.bitwise_xor(here, m)
        part = ref[...].astype(f32)
        square = square + jnp.sum(part * part, axis=-1, keepdims=True)
        width = part.shape[1]
        columns = pl.ds(pl.multiple_of(book * width, width), width)
        held[book] = (part * gain_ref[:, columns].astype(f32)).astype(bf16)
    return square


def early_kernel(books, early, pieces, sizes, tokens_ref, gain_ref, *refs):
    blocks = dict(zip(early, refs))
    parts = refs[len(early) : len(early) + len(pieces)]
    outs = refs[len(early) + len(pieces) :]
    projected_ref, square_ref, later_ref, looked_ref, qkv_ref, held, proj, table, sems = outs
    proj_rows, table_rows, qkv_rows = sizes
    here, group = lax.axis_index("book"), lax.axis_index("frames")
    width = held.shape[2]
    per_book = width // proj_rows
    half = qkv_rows // 2
    depth = table.shape[1]
    extra = qkv_ref.shape[1] - depth

    started = []

    def copy(source, target):
        made = pltpu.make_async_copy(source, target, sems.at[len(started)])
        made.start()
        started.append(made)
        return made

    table_copies, proj_copies, qkv_copies = [], [], []
    for (n, first), ref in zip(pieces, parts):
        if first + ref.shape[0] > proj_rows:
            g = jnp.bitwise_xor(group, n)
            start = pl.multiple_of(g * table_rows, table_rows)
            table_copies.append(
                copy(
                    ref.at[pl.ds(proj_rows - first, table_rows)], table.at[pl.ds(start, table_rows)]
                )
            )
    for (n, first), ref in zip(pieces, parts):
        count = min(ref.shape[0], proj_rows - first)
        proj_copies.append(
            copy(ref.at[pl.ds(0, count)], proj.at[pl.ds(n * proj_rows + first, count)])
        )
    for (n, first), ref in zip(pieces, parts):
        if first + ref.shape[0] > proj_rows:
            g = jnp.bitwise_xor(group, n)
            at_qkv = proj_rows - first + table_rows
            at_extra = at_qkv + qkv_rows
            start = pl.multiple_of(g * qkv_rows, qkv_rows)
            qkv_copies.append(
                copy(
                    ref.at[pl.ds(at_qkv, qkv_rows)],
                    qkv_ref.at[pl.ds(start, qkv_rows), pl.ds(0, depth)],
                )
            )
            for side in range(2):
                start = pl.multiple_of(g * qkv_rows + side * half, half)
                qkv_copies.append(
                    copy(
                        ref.at[pl.ds(at_extra, half), pl.ds(side * extra, extra)],
                        qkv_ref.at[pl.ds(start, half), pl.ds(depth, extra)],
                    )
                )

    square_ref[...] = hold_blocks(blocks, here, gain_ref, held)
    codes = lax.broadcasted_iota(jnp.int32, (table.shape[0], tokens_ref.shape[1]), 0)
    matches = (tokens_ref[...] == codes).astype(f32).astype(bf16)
    for made in table_copies:
        made.wait()
    looked = lax.dot_general(
        matches, table[...], (((0,), (0,)), ((), ())), preferred_element_type=f32
    )
    looked_ref[...] = looked.astype(bf16)
    projected_ref[...] = jnp.zeros_like(projected_ref)
    for (n, first), made, ref in zip(pieces, proj_copies, parts):
        count = min(ref.shape[0], proj_rows - first)
        rows = pl.ds(n * proj_rows + first, count)
        owner = jnp.bitwise_xor(group, n)
        book = owner // per_book
        start = pl.multiple_of((owner % per_book) * proj_rows + first, 128)
        late = is_late(jnp.bitwise_xor(here, book))
        made.wait()

        @pl.when(jnp.logical_not(late))
        def _():
            projected_ref[...] += jnp.dot(
                held[book, :, pl.ds(start, count)], proj[rows, :], preferred_element_type=f32
            )

        @pl.when(late)
        def _():
            slot = jnp.bitwise_xor(here, book) // 2 - 1
            later_ref[slot, pl.ds(start, count), :] = proj[rows, :]

    for made in qkv_copies:
        made.wait()


def project_early(tokens, gain, blocks, early, pieces, parts, sizes, wide):
    books = len(blocks)
    frames_here, width = blocks[0].shape
    depth = parts[0].shape[1]
    proj_rows, table_rows, qkv_rows = sizes
    groups = books * width // proj_rows
    vmem = pl.BlockSpec(memory_space=pltpu.VMEM)
    return pl.pallas_call(
        functools.partial(early_kernel, books, early, pieces, sizes),
        out_shape=[
            jax.ShapeDtypeStruct((frames_here, depth), f32),
            jax.ShapeDtypeStruct((frames_here, 1), f32),
            jax.ShapeDtypeStruct((books - len(early), width, depth), bf16),
            jax.ShapeDtypeStruct((frames_here, depth), bf16),
            jax.ShapeDtypeStruct((groups * qkv_rows, wide), bf16),
        ],
        in_specs=[vmem] * (2 + len(early))
        + [pl.BlockSpec(memory_space=pl.ANY)] * len(parts),
        out_specs=[vmem] * 5,
        scratch_shapes=[
            pltpu.VMEM((books, frames_here, width), bf16),
            pltpu.VMEM((books * width, depth), bf16),
            pltpu.VMEM((groups * table_rows, depth), bf16),
            pltpu.SemaphoreType.DMA((len(pieces) + 4 * groups,)),
        ],
        compiler_params=pltpu.CompilerParams(vmem_limit_bytes=45 * 2**20),
        name="early_products_and_lookup",
    )(tokens, gain, *[blocks[m] for m in early], *parts)


def late_kernel(books, late, gain_ref, *refs):
    blocks = dict(zip(late, refs))
    later_from, early_ref, square_ref, looked_ref, depth_gain_ref, qkv_from = refs[
        len(late) : len(late) + 6
    ]
    refs = refs[len(late) + 6 :]
    outs = refs[:books]
    held, packed, later_ref, qkv_ref, sems = refs[books:]
    later_copy = pltpu.make_async_copy(later_from, later_ref, sems.at[0])
    later_copy.start()
    qkv_copy = pltpu.make_async_copy(qkv_from, qkv_ref, sems.at[1])
    qkv_copy.start()
    here = lax.axis_index("book")
    frames_here, width = held.shape[1:]
    square = square_ref[...] + hold_blocks(blocks, here, gain_ref, held)
    projected = early_ref[...]
    later_copy.wait()
    for slot, m in enumerate(late):
        projected = projected + jnp.dot(
            held[jnp.bitwise_xor(here, m)], later_ref[slot], preferred_element_type=f32
        )
    projected = projected * lax.rsqrt(square / (books * width) + 1e-05)
    depth_in = (projected + looked_ref[...].astype(f32)).astype(bf16).astype(f32)
    moment = jnp.mean(depth_in * depth_in, axis=-1, keepdims=True)
    depth_normed = (depth_in * lax.rsqrt(moment + 1e-05) * depth_gain_ref[...].astype(f32)).astype(bf16)
    qkv_copy.wait()
    packed[...] = jnp.dot(depth_normed, qkv_ref[...], preferred_element_type=f32).astype(bf16)
    rows = frames_here // books
    for m in range(books):
        start = pl.multiple_of(jnp.bitwise_xor(here, m) * rows, rows)
        outs[m][...] = packed[pl.ds(start, rows), :]


def project_late(gain, blocks, late, later, projected, square, looked, depth_gain, qkv):
    books = len(blocks)
    frames_here, width = blocks[0].shape
    wide = qkv.shape[1]
    vmem = pl.BlockSpec(memory_space=pltpu.VMEM)
    return pl.pallas_call(
        functools.partial(late_kernel, books, late),
        out_shape=[jax.ShapeDtypeStruct((frames_here // books, wide), bf16)] * books,
        in_specs=[vmem] * (len(late) + 1)
        + [pl.BlockSpec(memory_space=pl.ANY)]
        + [vmem] * 4
        + [pl.BlockSpec(memory_space=pl.ANY)],
        out_specs=[vmem] * books,
        scratch_shapes=[
            pltpu.VMEM((books, frames_here, width), bf16),
            pltpu.VMEM((frames_here, wide), bf16),
            pltpu.VMEM(later.shape, bf16),
            pltpu.VMEM(qkv.shape, bf16),
            pltpu.SemaphoreType.DMA((2,)),
        ],
        compiler_params=pltpu.CompilerParams(vmem_limit_bytes=50 * 2**20),
        name="late_products_and_qkv",
    )(
        gain,
        *[blocks[m] for m in late],
        later,
        projected,
        square,
        looked,
        depth_gain,
        qkv,
    )


def attend_kernel(books, *refs):
    arrived = refs[:books]
    out_ref, inner = refs[books:]
    place = lax.axis_index("book")
    rows, wide = arrived[0].shape
    width = wide // 3
    for m in range(books):
        inner[jnp.bitwise_xor(place, m)] = arrived[m][...]
    head_of_row = lax.broadcasted_iota(jnp.int32, (width, width), 0) // HD
    head_of_column = lax.broadcasted_iota(jnp.int32, (width, width), 1) // HD
    same_head = (head_of_row == head_of_column).astype(f32).astype(bf16)
    keys_all = [inner[j, :, width : 2 * width].astype(f32) for j in range(books)]
    values_all = [inner[j, :, 2 * width :].astype(f32) for j in range(books)]
    contexts = []
    for k in range(books):
        query = inner[k, :, :width].astype(f32) * HD ** (-0.5)
        products = jnp.concatenate([query * keys_all[j] for j in range(k + 1)], axis=0)
        high = products.astype(bf16)
        low = (products - high.astype(f32)).astype(bf16)
        scores = jnp.dot(high, same_head, preferred_element_type=f32) + jnp.dot(
            low, same_head, preferred_element_type=f32
        )
        scores = [scores[j * rows : (j + 1) * rows] for j in range(k + 1)]
        peak = functools.reduce(jnp.maximum, scores)
        expo = [jnp.exp(score - peak) for score in scores]
        total = functools.reduce(jnp.add, expo)
        context = 0.0
        for j in range(k + 1):
            probability = (expo[j] / total).astype(bf16).astype(f32)
            context = context + probability * values_all[j]
        contexts.append(context)
    out_ref[...] = jnp.stack(contexts, axis=1).astype(bf16)


def attend(arrived):
    books = len(arrived)
    rows, wide = arrived[0].shape
    vmem = pl.BlockSpec(memory_space=pltpu.VMEM)
    return pl.pallas_call(
        functools.partial(attend_kernel, books),
        out_shape=jax.ShapeDtypeStruct((rows, books, wide // 3), bf16),
        in_specs=[vmem] * books,
        out_specs=vmem,
        scratch_shapes=[pltpu.VMEM((books, rows, wide), bf16)],
        compiler_params=pltpu.CompilerParams(vmem_limit_bytes=16 * 2**20),
        name="attend_books",
    )(*arrived)


def swap(value, axis, distance):
    return lax.ppermute(value, axis, [(i, i ^ distance) for i in range(lax.axis_size(axis))])


def after(value, *others):
    return lax.optimization_barrier((value, *others))[0]


def bits_of(number):
    return [1 << place for place in range(number.bit_length()) if number >> place & 1]


def per_device(
    gate_pre,
    up_pre,
    down_weight,
    residual,
    out_gain,
    in_proj,
    embedding,
    token_ids,
    depth_gain,
    qkv_weight,
):
    books = lax.axis_size("book")
    groups = lax.axis_size("frames")
    here = lax.axis_index("book").astype(jnp.int32)
    width = residual.shape[1]
    proj_rows = in_proj.shape[1]
    gain = out_gain[None]

    hidden, first = first_products(gate_pre, up_pre, down_weight, width)

    def share(m, *others):
        factor = after(hidden, *others) if others else hidden
        if m == 0:
            total = 0.0
            each = factor.shape[1] // 4
            for step in range(4):
                block = lax.dynamic_slice(
                    down_weight, (step * each, lax.axis_index("book") * width), (each, width)
                )
                part = lax.slice_in_dim(factor, step * each, (step + 1) * each, axis=1)
                total = total + jnp.dot(part, block, preferred_element_type=f32)
                total = lax.optimization_barrier(total)
            return total
        return share_products(factor, down_weight, width, m)

    rows = pack(*after((in_proj[0], embedding[0], qkv_weight[0]), first))
    parts = {0: [(0, rows)]}
    near = [n for n in range(2, groups, 2) if len(bits_of(n)) == 1]
    for n in near:
        parts[n] = [(0, swap(rows, "frames", n))]

    sums = {books - 1: first}
    parts[1] = [(0, swap(rows, "frames", 1))]
    sums[books - 2] = lax.optimization_barrier(share(books - 2, rows))
    for n in range(books - 3, 0, -1):
        sums[n] = lax.optimization_barrier(share(n, rows))
    came = swap(sums.pop(books - 1).astype(bf16), "book", 1)
    came = after(came, *[sums[n] for n in range(1, books - 1)])
    onward = (sums.pop(books - 2) + came.astype(f32)).astype(bf16)
    far_came = swap(onward, "book", 2)
    last = lax.optimization_barrier(share(0, came, parts[1][0][1]))
    sums[0] = last + residual.astype(f32)
    for m in range(books - 3, 0, -2):
        near_came = swap(after(sums.pop(m).astype(bf16), onward), "book", 1)
        sums[m ^ 1] = sums[m ^ 1] + near_came.astype(f32)
    sums[(books - 2) ^ 2] = sums[(books - 2) ^ 2] + far_came.astype(f32)
    distance = 2
    while distance < books:
        for m in range(books - distance, 0, -2 * distance):
            if m in sums:
                came = swap(sums.pop(m).astype(bf16), "book", distance)
                sums[m ^ distance] = sums[m ^ distance] + came.astype(f32)
        distance *= 2

    blocks = {0: sums[0].astype(bf16)}

    arrived = after([parts[n][0][1] for n in near], blocks[0])
    for n, value in zip(near, arrived):
        parts[n] = [(0, value)]
    cut = rows.shape[0] // 2 // 128 * 128
    for n in range(2, groups, 2):
        sides = bits_of(n)
        if n in near:
            continue
        if len(sides) == 2 and 0 < cut < proj_rows:
            upper, lower = cut_rows(parts[n ^ sides[0]][0][1], parts[n ^ sides[1]][0][1], cut)
            upper = swap(upper, "frames", sides[0])
            lower = swap(lower, "frames", sides[1])
            parts[n] = [(0, upper), (cut, lower)]
        else:
            parts[n] = [(0, swap(rows, "frames", n))]
    for n in range(2, groups, 2):
        parts[n + 1] = [(first, swap(value, "frames", 1)) for first, value in parts[n]]

    near_there = [parts[n + 1][0][1] for n in near]
    distance = books // 2
    while distance:
        for m in sorted(blocks):
            going = blocks[m]
            if m:
                going = after(going, blocks[distance])
            elif distance == 1:
                going = after(going, *near_there)
            blocks[m ^ distance] = swap(going, "book", distance)
        distance //= 2

    pieces = [(n, first) for n in range(groups) for first, _ in parts[n]]
    arrived = [value for n in range(groups) for _, value in parts[n]]
    sizes = proj_rows, embedding.shape[1], qkv_weight.shape[1]
    early = [m for m in range(books) if not is_late(m)]
    late = [m for m in range(books) if is_late(m)]
    projected, square, later, looked, qkv = project_early(
        token_ids.reshape(1, -1), gain, blocks, early, pieces, arrived, sizes, qkv_weight.shape[2]
    )
    packed = project_late(
        gain, blocks, late, later, projected, square, looked, depth_gain, qkv
    )
    far = {m: swap(packed[m], "book", m) for m in range(books - 1, 0, -1)}
    return attend([packed[0]] + [far[m] for m in range(1, books)])


def solution(mesh):
    in_specs = (
        P("frames", "book"),
        P("frames", "book"),
        P("book", None),
        P("frames", "book"),
        P(),
        P("book", "frames", None),
        P("book", "frames", None),
        P("frames", "book"),
        P("book", None),
        P("book", "frames", None),
    )
    out_specs = P(("frames", "book"), None, None)
    return jax.shard_map(
        per_device, mesh=mesh, in_specs=in_specs, out_specs=out_specs, check_vma=False
    )
```

```python
import functools

import jax
import jax.numpy as jnp
from jax import lax
from jax.experimental import pallas as pl
from jax.experimental.pallas import tpu as pltpu
from jax.sharding import PartitionSpec as P

H = 8
HD = 64
f32, bf16 = jnp.float32, jnp.bfloat16


def first_kernel(gate_ref, up_ref, down_ref, hidden_ref, first_ref, gates, ups, held, sems):
    steps, each, width = held.shape
    books = down_ref.shape[1] // width
    start = pl.multiple_of(jnp.bitwise_xor(lax.axis_index("book"), books - 1) * width, width)
    copies = []
    for step in range(steps):
        rows = pl.ds(step * each, each)
        moves = [
            (gate_ref.at[:, rows], gates.at[step]),
            (up_ref.at[:, rows], ups.at[step]),
            (down_ref.at[rows, pl.ds(start, width)], held.at[step]),
        ]
        for kind, (source, target) in enumerate(moves):
            copies.append(pltpu.make_async_copy(source, target, sems.at[3 * step + kind]))
            copies[-1].start()
    total = 0.0
    for step in range(steps):
        copies[3 * step].wait()
        copies[3 * step + 1].wait()
        gate = gates[step].astype(f32)
        hidden = gate / (1.0 + jnp.exp(-gate)) * ups[step].astype(f32)
        hidden = hidden.astype(bf16)
        hidden_ref[:, pl.ds(step * each, each)] = hidden
        copies[3 * step + 2].wait()
        total = total + jnp.dot(hidden, held[step], preferred_element_type=f32)
    first_ref[...] = total.astype(bf16)


def first_products(gate, up, down, width):
    frames_here, hidden_width = gate.shape
    steps = max(hidden_width // 512, 1)
    vmem = pl.BlockSpec(memory_space=pltpu.VMEM)
    return pl.pallas_call(
        first_kernel,
        out_shape=[
            jax.ShapeDtypeStruct((frames_here, hidden_width), bf16),
            jax.ShapeDtypeStruct((frames_here, width), bf16),
        ],
        in_specs=[pl.BlockSpec(memory_space=pl.ANY)] * 3,
        out_specs=[vmem] * 2,
        scratch_shapes=[
            pltpu.VMEM((steps, frames_here, hidden_width // steps), bf16),
            pltpu.VMEM((steps, frames_here, hidden_width // steps), bf16),
            pltpu.VMEM((steps, hidden_width // steps, width), bf16),
            pltpu.SemaphoreType.DMA((3 * steps,)),
        ],
        compiler_params=pltpu.CompilerParams(vmem_limit_bytes=53 * 2**20),
        name="hidden_and_first_products",
    )(gate, up, down)


def share_kernel(partner, hidden_ref, down_ref, out_ref, held, sems):
    steps, each, width = held.shape
    start = pl.multiple_of(jnp.bitwise_xor(lax.axis_index("book"), partner) * width, width)
    copies = []
    for step in range(steps):
        rows = pl.ds(step * each, each)
        copies.append(
            pltpu.make_async_copy(
                down_ref.at[rows, pl.ds(start, width)], held.at[step], sems.at[step]
            )
        )
        copies[-1].start()
    total = 0.0
    for step in range(steps):
        copies[step].wait()
        total = total + jnp.dot(
            hidden_ref[:, pl.ds(step * each, each)], held[step], preferred_element_type=f32
        )
    out_ref[...] = total.astype(out_ref.dtype)


def share_products(hidden, down, width, partner):
    frames_here, hidden_width = hidden.shape
    steps = max(hidden_width // 512, 1)
    vmem = pl.BlockSpec(memory_space=pltpu.VMEM)
    return pl.pallas_call(
        functools.partial(share_kernel, partner),
        out_shape=jax.ShapeDtypeStruct((frames_here, width), bf16 if partner % 2 else f32),
        in_specs=[vmem, pl.BlockSpec(memory_space=pl.ANY)],
        out_specs=vmem,
        scratch_shapes=[
            pltpu.VMEM((steps, hidden_width // steps, width), bf16),
            pltpu.SemaphoreType.DMA((steps,)),
        ],
        compiler_params=pltpu.CompilerParams(vmem_limit_bytes=53 * 2**20),
        name="share_products",
    )(hidden, down)


def pack_kernel(proj_ref, table_ref, qkv_ref, packed_ref, sems):
    proj_rows, depth = proj_ref.shape
    table_rows = table_ref.shape[0]
    qkv_rows, wide = qkv_ref.shape
    half, extra = qkv_rows // 2, wide - depth
    at_qkv = proj_rows + table_rows
    at_extra = at_qkv + qkv_rows
    moves = [
        (proj_ref, packed_ref.at[pl.ds(0, proj_rows)]),
        (table_ref, packed_ref.at[pl.ds(proj_rows, table_rows)]),
        (qkv_ref.at[:, pl.ds(0, depth)], packed_ref.at[pl.ds(at_qkv, qkv_rows)]),
    ]
    for side in range(2):
        moves.append(
            (
                qkv_ref.at[pl.ds(side * half, half), pl.ds(depth, extra)],
                packed_ref.at[pl.ds(at_extra, half), pl.ds(side * extra, extra)],
            )
        )
    copies = [
        pltpu.make_async_copy(source, target, sems.at[number])
        for number, (source, target) in enumerate(moves)
    ]
    for made in copies:
        made.start()
    for made in copies:
        made.wait()


def pack(proj, table, qkv):
    depth = proj.shape[1]
    rows = proj.shape[0] + table.shape[0] + qkv.shape[0] + qkv.shape[0] // 2
    return pl.pallas_call(
        pack_kernel,
        out_shape=jax.ShapeDtypeStruct((rows, depth), bf16),
        in_specs=[pl.BlockSpec(memory_space=pl.ANY)] * 3,
        out_specs=pl.BlockSpec(memory_space=pltpu.VMEM),
        scratch_shapes=[pltpu.SemaphoreType.DMA((5,))],
        compiler_params=pltpu.CompilerParams(vmem_limit_bytes=4 * 2**20),
        name="pack_weight_rows",
    )(proj, table, qkv)


def is_late(m):
    return (m % 2 == 1) & (m != 1)


def hold_blocks(blocks, here, gain_ref, held):
    square = 0.0
    for m, ref in blocks.items():
        book = jnp.bitwise_xor(here, m)
        part = ref[...].astype(f32)
        square = square + jnp.sum(part * part, axis=-1, keepdims=True)
        width = part.shape[1]
        columns = pl.ds(pl.multiple_of(book * width, width), width)
        held[book] = (part * gain_ref[:, columns].astype(f32)).astype(bf16)
    return square


def early_kernel(books, early, pieces, sizes, tokens_ref, gain_ref, *refs):
    blocks = dict(zip(early, refs))
    parts = refs[len(early) : len(early) + len(pieces)]
    outs = refs[len(early) + len(pieces) :]
    projected_ref, square_ref, later_ref, looked_ref, qkv_ref, held, proj, table, sems = outs
    proj_rows, table_rows, qkv_rows = sizes
    here, group = lax.axis_index("book"), lax.axis_index("frames")
    width = held.shape[2]
    per_book = width // proj_rows
    half = qkv_rows // 2
    depth = table.shape[1]
    extra = qkv_ref.shape[1] - depth

    started = []

    def copy(source, target):
        made = pltpu.make_async_copy(source, target, sems.at[len(started)])
        made.start()
        started.append(made)
        return made

    table_copies, proj_copies, qkv_copies = [], [], []
    for (n, first), ref in zip(pieces, parts):
        if first + ref.shape[0] > proj_rows:
            g = jnp.bitwise_xor(group, n)
            start = pl.multiple_of(g * table_rows, table_rows)
            table_copies.append(
                copy(
                    ref.at[pl.ds(proj_rows - first, table_rows)], table.at[pl.ds(start, table_rows)]
                )
            )
    for (n, first), ref in zip(pieces, parts):
        count = min(ref.shape[0], proj_rows - first)
        proj_copies.append(
            copy(ref.at[pl.ds(0, count)], proj.at[pl.ds(n * proj_rows + first, count)])
        )
    for (n, first), ref in zip(pieces, parts):
        if first + ref.shape[0] > proj_rows:
            g = jnp.bitwise_xor(group, n)
            at_qkv = proj_rows - first + table_rows
            at_extra = at_qkv + qkv_rows
            start = pl.multiple_of(g * qkv_rows, qkv_rows)
            qkv_copies.append(
                copy(
                    ref.at[pl.ds(at_qkv, qkv_rows)],
                    qkv_ref.at[pl.ds(start, qkv_rows), pl.ds(0, depth)],
                )
            )
            for side in range(2):
                start = pl.multiple_of(g * qkv_rows + side * half, half)
                qkv_copies.append(
                    copy(
                        ref.at[pl.ds(at_extra, half), pl.ds(side * extra, extra)],
                        qkv_ref.at[pl.ds(start, half), pl.ds(depth, extra)],
                    )
                )

    square_ref[...] = hold_blocks(blocks, here, gain_ref, held)
    codes = lax.broadcasted_iota(jnp.int32, (table.shape[0], tokens_ref.shape[1]), 0)
    matches = (tokens_ref[...] == codes).astype(f32).astype(bf16)
    for made in table_copies:
        made.wait()
    looked = lax.dot_general(
        matches, table[...], (((0,), (0,)), ((), ())), preferred_element_type=f32
    )
    looked_ref[...] = looked.astype(bf16)
    projected_ref[...] = jnp.zeros_like(projected_ref)
    for (n, first), made, ref in zip(pieces, proj_copies, parts):
        count = min(ref.shape[0], proj_rows - first)
        rows = pl.ds(n * proj_rows + first, count)
        owner = jnp.bitwise_xor(group, n)
        book = owner // per_book
        start = pl.multiple_of((owner % per_book) * proj_rows + first, 128)
        late = is_late(jnp.bitwise_xor(here, book))
        made.wait()

        @pl.when(jnp.logical_not(late))
        def _():
            projected_ref[...] += jnp.dot(
                held[book, :, pl.ds(start, count)], proj[rows, :], preferred_element_type=f32
            )

        @pl.when(late)
        def _():
            slot = jnp.bitwise_xor(here, book) // 2 - 1
            later_ref[slot, pl.ds(start, count), :] = proj[rows, :]

    for made in qkv_copies:
        made.wait()


def project_early(tokens, gain, blocks, early, pieces, parts, sizes, wide):
    books = len(blocks)
    frames_here, width = blocks[0].shape
    depth = parts[0].shape[1]
    proj_rows, table_rows, qkv_rows = sizes
    groups = books * width // proj_rows
    vmem = pl.BlockSpec(memory_space=pltpu.VMEM)
    return pl.pallas_call(
        functools.partial(early_kernel, books, early, pieces, sizes),
        out_shape=[
            jax.ShapeDtypeStruct((frames_here, depth), f32),
            jax.ShapeDtypeStruct((frames_here, 1), f32),
            jax.ShapeDtypeStruct((books - len(early), width, depth), bf16),
            jax.ShapeDtypeStruct((frames_here, depth), bf16),
            jax.ShapeDtypeStruct((groups * qkv_rows, wide), bf16),
        ],
        in_specs=[vmem] * (2 + len(early))
        + [pl.BlockSpec(memory_space=pl.ANY)] * len(parts),
        out_specs=[vmem] * 5,
        scratch_shapes=[
            pltpu.VMEM((books, frames_here, width), bf16),
            pltpu.VMEM((books * width, depth), bf16),
            pltpu.VMEM((groups * table_rows, depth), bf16),
            pltpu.SemaphoreType.DMA((len(pieces) + 4 * groups,)),
        ],
        compiler_params=pltpu.CompilerParams(vmem_limit_bytes=45 * 2**20),
        name="early_products_and_lookup",
    )(tokens, gain, *[blocks[m] for m in early], *parts)


def late_kernel(books, late, gain_ref, *refs):
    blocks = dict(zip(late, refs))
    later_from, early_ref, square_ref, looked_ref, depth_gain_ref, qkv_from = refs[
        len(late) : len(late) + 6
    ]
    refs = refs[len(late) + 6 :]
    outs = refs[:books]
    held, packed, later_ref, qkv_ref, sems = refs[books:]
    later_copy = pltpu.make_async_copy(later_from, later_ref, sems.at[0])
    later_copy.start()
    qkv_copy = pltpu.make_async_copy(qkv_from, qkv_ref, sems.at[1])
    qkv_copy.start()
    here = lax.axis_index("book")
    frames_here, width = held.shape[1:]
    square = square_ref[...] + hold_blocks(blocks, here, gain_ref, held)
    projected = early_ref[...]
    later_copy.wait()
    for slot, m in enumerate(late):
        projected = projected + jnp.dot(
            held[jnp.bitwise_xor(here, m)], later_ref[slot], preferred_element_type=f32
        )
    projected = projected * lax.rsqrt(square / (books * width) + 1e-05)
    depth_in = (projected + looked_ref[...].astype(f32)).astype(bf16).astype(f32)
    moment = jnp.mean(depth_in * depth_in, axis=-1, keepdims=True)
    depth_normed = (depth_in * lax.rsqrt(moment + 1e-05) * depth_gain_ref[...].astype(f32)).astype(bf16)
    qkv_copy.wait()
    packed[...] = jnp.dot(depth_normed, qkv_ref[...], preferred_element_type=f32).astype(bf16)
    rows = frames_here // books
    for m in range(books):
        start = pl.multiple_of(jnp.bitwise_xor(here, m) * rows, rows)
        outs[m][...] = packed[pl.ds(start, rows), :]


def project_late(gain, blocks, late, later, projected, square, looked, depth_gain, qkv):
    books = len(blocks)
    frames_here, width = blocks[0].shape
    wide = qkv.shape[1]
    vmem = pl.BlockSpec(memory_space=pltpu.VMEM)
    return pl.pallas_call(
        functools.partial(late_kernel, books, late),
        out_shape=[jax.ShapeDtypeStruct((frames_here // books, wide), bf16)] * books,
        in_specs=[vmem] * (len(late) + 1)
        + [pl.BlockSpec(memory_space=pl.ANY)]
        + [vmem] * 4
        + [pl.BlockSpec(memory_space=pl.ANY)],
        out_specs=[vmem] * books,
        scratch_shapes=[
            pltpu.VMEM((books, frames_here, width), bf16),
            pltpu.VMEM((frames_here, wide), bf16),
            pltpu.VMEM(later.shape, bf16),
            pltpu.VMEM(qkv.shape, bf16),
            pltpu.SemaphoreType.DMA((2,)),
        ],
        compiler_params=pltpu.CompilerParams(vmem_limit_bytes=50 * 2**20),
        name="late_products_and_qkv",
    )(
        gain,
        *[blocks[m] for m in late],
        later,
        projected,
        square,
        looked,
        depth_gain,
        qkv,
    )


def attend_kernel(books, *refs):
    arrived = refs[:books]
    out_ref, inner = refs[books:]
    place = lax.axis_index("book")
    rows, wide = arrived[0].shape
    width = wide // 3
    for m in range(books):
        inner[jnp.bitwise_xor(place, m)] = arrived[m][...]
    head_of_row = lax.broadcasted_iota(jnp.int32, (width, width), 0) // HD
    head_of_column = lax.broadcasted_iota(jnp.int32, (width, width), 1) // HD
    same_head = (head_of_row == head_of_column).astype(f32).astype(bf16)
    keys_all = [inner[j, :, width : 2 * width].astype(f32) for j in range(books)]
    values_all = [inner[j, :, 2 * width :].astype(f32) for j in range(books)]
    contexts = []
    for k in range(books):
        query = inner[k, :, :width].astype(f32) * HD ** (-0.5)
        products = jnp.concatenate([query * keys_all[j] for j in range(k + 1)], axis=0)
        high = products.astype(bf16)
        low = (products - high.astype(f32)).astype(bf16)
        scores = jnp.dot(high, same_head, preferred_element_type=f32) + jnp.dot(
            low, same_head, preferred_element_type=f32
        )
        scores = [scores[j * rows : (j + 1) * rows] for j in range(k + 1)]
        peak = functools.reduce(jnp.maximum, scores)
        expo = [jnp.exp(score - peak) for score in scores]
        total = functools.reduce(jnp.add, expo)
        context = 0.0
        for j in range(k + 1):
            probability = (expo[j] / total).astype(bf16).astype(f32)
            context = context + probability * values_all[j]
        contexts.append(context)
    out_ref[...] = jnp.stack(contexts, axis=1).astype(bf16)


def attend(arrived):
    books = len(arrived)
    rows, wide = arrived[0].shape
    vmem = pl.BlockSpec(memory_space=pltpu.VMEM)
    return pl.pallas_call(
        functools.partial(attend_kernel, books),
        out_shape=jax.ShapeDtypeStruct((rows, books, wide // 3), bf16),
        in_specs=[vmem] * books,
        out_specs=vmem,
        scratch_shapes=[pltpu.VMEM((books, rows, wide), bf16)],
        compiler_params=pltpu.CompilerParams(vmem_limit_bytes=16 * 2**20),
        name="attend_books",
    )(*arrived)


def swap(value, axis, distance):
    return lax.ppermute(value, axis, [(i, i ^ distance) for i in range(lax.axis_size(axis))])


def after(value, *others):
    return lax.optimization_barrier((value, *others))[0]


def bits_of(number):
    return [1 << place for place in range(number.bit_length()) if number >> place & 1]


def per_device(
    gate_pre,
    up_pre,
    down_weight,
    residual,
    out_gain,
    in_proj,
    embedding,
    token_ids,
    depth_gain,
    qkv_weight,
):
    books = lax.axis_size("book")
    groups = lax.axis_size("frames")
    here = lax.axis_index("book").astype(jnp.int32)
    width = residual.shape[1]
    proj_rows = in_proj.shape[1]
    gain = out_gain[None]

    hidden, first = first_products(gate_pre, up_pre, down_weight, width)

    def share(m, *others):
        factor = after(hidden, *others) if others else hidden
        if m == 0:
            total = 0.0
            each = factor.shape[1] // 4
            for step in range(4):
                block = lax.dynamic_slice(
                    down_weight, (step * each, lax.axis_index("book") * width), (each, width)
                )
                part = lax.slice_in_dim(factor, step * each, (step + 1) * each, axis=1)
                total = total + jnp.dot(part, block, preferred_element_type=f32)
                total = lax.optimization_barrier(total)
            return total
        return share_products(factor, down_weight, width, m)

    rows = pack(*after((in_proj[0], embedding[0], qkv_weight[0]), first))
    parts = {0: [(0, rows)]}
    near = [n for n in range(2, groups, 2) if len(bits_of(n)) == 1]
    for n in near:
        parts[n] = [(0, swap(rows, "frames", n))]

    sums = {books - 1: first}
    parts[1] = [(0, swap(rows, "frames", 1))]
    sums[books - 2] = lax.optimization_barrier(share(books - 2, rows))
    for n in range(books - 3, 0, -1):
        sums[n] = lax.optimization_barrier(share(n, rows))
    came = swap(sums.pop(books - 1).astype(bf16), "book", 1)
    came = after(came, *[sums[n] for n in range(1, books - 1)])
    onward = (sums.pop(books - 2) + came.astype(f32)).astype(bf16)
    far_came = swap(onward, "book", 2)
    last = lax.optimization_barrier(share(0, came, parts[1][0][1]))
    sums[0] = last + residual.astype(f32)
    for m in range(books - 3, 0, -2):
        near_came = swap(after(sums.pop(m).astype(bf16), onward), "book", 1)
        sums[m ^ 1] = sums[m ^ 1] + near_came.astype(f32)
    sums[(books - 2) ^ 2] = sums[(books - 2) ^ 2] + far_came.astype(f32)
    distance = 2
    while distance < books:
        for m in range(books - distance, 0, -2 * distance):
            if m in sums:
                came = swap(sums.pop(m).astype(bf16), "book", distance)
                sums[m ^ distance] = sums[m ^ distance] + came.astype(f32)
        distance *= 2

    blocks = {0: sums[0].astype(bf16)}

    arrived = after([parts[n][0][1] for n in near], blocks[0])
    for n, value in zip(near, arrived):
        parts[n] = [(0, value)]
    cut = rows.shape[0] // 2 // 128 * 128
    for n in range(2, groups, 2):
        sides = bits_of(n)
        if n in near:
            continue
        if len(sides) == 2 and 0 < cut < proj_rows:
            upper = swap(parts[n ^ sides[0]][0][1][:cut], "frames", sides[0])
            lower = swap(parts[n ^ sides[1]][0][1][cut:], "frames", sides[1])
            parts[n] = [(0, upper), (cut, lower)]
        else:
            parts[n] = [(0, swap(rows, "frames", n))]
    for n in range(2, groups, 2):
        parts[n + 1] = [(first, swap(value, "frames", 1)) for first, value in parts[n]]

    near_there = [parts[n + 1][0][1] for n in near]
    distance = books // 2
    while distance:
        for m in sorted(blocks):
            going = blocks[m]
            if m:
                going = after(going, blocks[distance])
            elif distance == 1:
                going = after(going, *near_there)
            blocks[m ^ distance] = swap(going, "book", distance)
        distance //= 2

    pieces = [(n, first) for n in range(groups) for first, _ in parts[n]]
    arrived = [value for n in range(groups) for _, value in parts[n]]
    sizes = proj_rows, embedding.shape[1], qkv_weight.shape[1]
    early = [m for m in range(books) if not is_late(m)]
    late = [m for m in range(books) if is_late(m)]
    projected, square, later, looked, qkv = project_early(
        token_ids.reshape(1, -1), gain, blocks, early, pieces, arrived, sizes, qkv_weight.shape[2]
    )
    packed = project_late(
        gain, blocks, late, later, projected, square, looked, depth_gain, qkv
    )
    far = {m: swap(packed[m], "book", m) for m in range(books - 1, 0, -1)}
    return attend([packed[0]] + [far[m] for m in range(1, books)])


def solution(mesh):
    in_specs = (
        P("frames", "book"),
        P("frames", "book"),
        P("book", None),
        P("frames", "book"),
        P(),
        P("book", "frames", None),
        P("book", "frames", None),
        P("frames", "book"),
        P("book", None),
        P("book", "frames", None),
    )
    out_specs = P(("frames", "book"), None, None)
    return jax.shard_map(
        per_device, mesh=mesh, in_specs=in_specs, out_specs=out_specs, check_vma=False
    )
```

```python
import functools

import jax
import jax.numpy as jnp
from jax import lax
from jax.experimental import pallas as pl
from jax.experimental.pallas import tpu as pltpu
from jax.sharding import PartitionSpec as P

H = 8
HD = 64
f32, bf16 = jnp.float32, jnp.bfloat16


def first_kernel(gate_ref, up_ref, down_ref, hidden_ref, first_ref, gates, ups, held, sems):
    steps, each, width = held.shape
    books = down_ref.shape[1] // width
    start = pl.multiple_of(jnp.bitwise_xor(lax.axis_index("book"), books - 1) * width, width)
    copies = []
    for step in range(steps):
        rows = pl.ds(step * each, each)
        moves = [
            (gate_ref.at[:, rows], gates.at[step]),
            (up_ref.at[:, rows], ups.at[step]),
            (down_ref.at[rows, pl.ds(start, width)], held.at[step]),
        ]
        for kind, (source, target) in enumerate(moves):
            copies.append(pltpu.make_async_copy(source, target, sems.at[3 * step + kind]))
            copies[-1].start()
    total = 0.0
    for step in range(steps):
        copies[3 * step].wait()
        copies[3 * step + 1].wait()
        gate = gates[step].astype(f32)
        hidden = gate / (1.0 + jnp.exp(-gate)) * ups[step].astype(f32)
        hidden = hidden.astype(bf16)
        hidden_ref[:, pl.ds(step * each, each)] = hidden
        copies[3 * step + 2].wait()
        total = total + jnp.dot(hidden, held[step], preferred_element_type=f32)
    first_ref[...] = total.astype(bf16)


def first_products(gate, up, down, width):
    frames_here, hidden_width = gate.shape
    steps = max(hidden_width // 512, 1)
    vmem = pl.BlockSpec(memory_space=pltpu.VMEM)
    return pl.pallas_call(
        first_kernel,
        out_shape=[
            jax.ShapeDtypeStruct((frames_here, hidden_width), bf16),
            jax.ShapeDtypeStruct((frames_here, width), bf16),
        ],
        in_specs=[pl.BlockSpec(memory_space=pl.ANY)] * 3,
        out_specs=[vmem] * 2,
        scratch_shapes=[
            pltpu.VMEM((steps, frames_here, hidden_width // steps), bf16),
            pltpu.VMEM((steps, frames_here, hidden_width // steps), bf16),
            pltpu.VMEM((steps, hidden_width // steps, width), bf16),
            pltpu.SemaphoreType.DMA((3 * steps,)),
        ],
        compiler_params=pltpu.CompilerParams(vmem_limit_bytes=53 * 2**20),
        name="hidden_and_first_products",
    )(gate, up, down)


def share_kernel(partner, hidden_ref, down_ref, out_ref, held, sems):
    steps, each, width = held.shape
    start = pl.multiple_of(jnp.bitwise_xor(lax.axis_index("book"), partner) * width, width)
    copies = []
    for step in range(steps):
        rows = pl.ds(step * each, each)
        copies.append(
            pltpu.make_async_copy(
                down_ref.at[rows, pl.ds(start, width)], held.at[step], sems.at[step]
            )
        )
        copies[-1].start()
    total = 0.0
    for step in range(steps):
        copies[step].wait()
        total = total + jnp.dot(
            hidden_ref[:, pl.ds(step * each, each)], held[step], preferred_element_type=f32
        )
    out_ref[...] = total.astype(out_ref.dtype)


def share_products(hidden, down, width, partner):
    frames_here, hidden_width = hidden.shape
    steps = max(hidden_width // 512, 1)
    vmem = pl.BlockSpec(memory_space=pltpu.VMEM)
    return pl.pallas_call(
        functools.partial(share_kernel, partner),
        out_shape=jax.ShapeDtypeStruct((frames_here, width), bf16 if partner % 2 else f32),
        in_specs=[vmem, pl.BlockSpec(memory_space=pl.ANY)],
        out_specs=vmem,
        scratch_shapes=[
            pltpu.VMEM((steps, hidden_width // steps, width), bf16),
            pltpu.SemaphoreType.DMA((steps,)),
        ],
        compiler_params=pltpu.CompilerParams(vmem_limit_bytes=53 * 2**20),
        name="share_products",
    )(hidden, down)


def pack_kernel(proj_ref, table_ref, qkv_ref, packed_ref, sems):
    proj_rows, depth = proj_ref.shape
    table_rows = table_ref.shape[0]
    qkv_rows, wide = qkv_ref.shape
    half, extra = qkv_rows // 2, wide - depth
    at_qkv = proj_rows + table_rows
    at_extra = at_qkv + qkv_rows
    moves = [
        (proj_ref, packed_ref.at[pl.ds(0, proj_rows)]),
        (table_ref, packed_ref.at[pl.ds(proj_rows, table_rows)]),
        (qkv_ref.at[:, pl.ds(0, depth)], packed_ref.at[pl.ds(at_qkv, qkv_rows)]),
    ]
    for side in range(2):
        moves.append(
            (
                qkv_ref.at[pl.ds(side * half, half), pl.ds(depth, extra)],
                packed_ref.at[pl.ds(at_extra, half), pl.ds(side * extra, extra)],
            )
        )
    copies = [
        pltpu.make_async_copy(source, target, sems.at[number])
        for number, (source, target) in enumerate(moves)
    ]
    for made in copies:
        made.start()
    for made in copies:
        made.wait()


def pack(proj, table, qkv):
    depth = proj.shape[1]
    rows = proj.shape[0] + table.shape[0] + qkv.shape[0] + qkv.shape[0] // 2
    return pl.pallas_call(
        pack_kernel,
        out_shape=jax.ShapeDtypeStruct((rows, depth), bf16),
        in_specs=[pl.BlockSpec(memory_space=pl.ANY)] * 3,
        out_specs=pl.BlockSpec(memory_space=pltpu.VMEM),
        scratch_shapes=[pltpu.SemaphoreType.DMA((5,))],
        compiler_params=pltpu.CompilerParams(vmem_limit_bytes=4 * 2**20),
        name="pack_weight_rows",
    )(proj, table, qkv)


def cut_kernel(cut, upper_from, lower_from, upper_ref, lower_ref, sems):
    upper = pltpu.make_async_copy(upper_from.at[pl.ds(0, cut)], upper_ref, sems.at[0])
    lower = pltpu.make_async_copy(
        lower_from.at[pl.ds(cut, lower_ref.shape[0])], lower_ref, sems.at[1]
    )
    upper.start()
    lower.start()
    upper.wait()
    lower.wait()


def cut_rows(upper_from, lower_from, cut):
    rows, depth = upper_from.shape
    return pl.pallas_call(
        functools.partial(cut_kernel, cut),
        out_shape=[
            jax.ShapeDtypeStruct((cut, depth), bf16),
            jax.ShapeDtypeStruct((rows - cut, depth), bf16),
        ],
        in_specs=[pl.BlockSpec(memory_space=pl.ANY)] * 2,
        out_specs=[pl.BlockSpec(memory_space=pltpu.VMEM)] * 2,
        scratch_shapes=[pltpu.SemaphoreType.DMA((2,))],
        name="cut_rows",
    )(upper_from, lower_from)


def is_late(m):
    return (m % 2 == 1) & (m != 1)


def hold_blocks(blocks, here, gain_ref, held):
    square = 0.0
    for m, ref in blocks.items():
        book = jnp.bitwise_xor(here, m)
        part = ref[...].astype(f32)
        square = square + jnp.sum(part * part, axis=-1, keepdims=True)
        width = part.shape[1]
        columns = pl.ds(pl.multiple_of(book * width, width), width)
        held[book] = (part * gain_ref[:, columns].astype(f32)).astype(bf16)
    return square


def early_kernel(books, early, pieces, sizes, tokens_ref, gain_ref, *refs):
    blocks = dict(zip(early, refs))
    parts = refs[len(early) : len(early) + len(pieces)]
    outs = refs[len(early) + len(pieces) :]
    projected_ref, square_ref, later_ref, looked_ref, qkv_ref, held, proj, table, sems = outs
    proj_rows, table_rows, qkv_rows = sizes
    here, group = lax.axis_index("book"), lax.axis_index("frames")
    width = held.shape[2]
    per_book = width // proj_rows
    half = qkv_rows // 2
    depth = table.shape[1]
    extra = qkv_ref.shape[1] - depth

    started = []

    def copy(source, target):
        made = pltpu.make_async_copy(source, target, sems.at[len(started)])
        made.start()
        started.append(made)
        return made

    table_copies, proj_copies, qkv_copies = [], [], []
    for (n, first), ref in zip(pieces, parts):
        if first + ref.shape[0] > proj_rows:
            g = jnp.bitwise_xor(group, n)
            start = pl.multiple_of(g * table_rows, table_rows)
            table_copies.append(
                copy(
                    ref.at[pl.ds(proj_rows - first, table_rows)], table.at[pl.ds(start, table_rows)]
                )
            )
    for (n, first), ref in zip(pieces, parts):
        count = min(ref.shape[0], proj_rows - first)
        proj_copies.append(
            copy(ref.at[pl.ds(0, count)], proj.at[pl.ds(n * proj_rows + first, count)])
        )
    for (n, first), ref in zip(pieces, parts):
        if first + ref.shape[0] > proj_rows:
            g = jnp.bitwise_xor(group, n)
            at_qkv = proj_rows - first + table_rows
            at_extra = at_qkv + qkv_rows
            start = pl.multiple_of(g * qkv_rows, qkv_rows)
            qkv_copies.append(
                copy(
                    ref.at[pl.ds(at_qkv, qkv_rows)],
                    qkv_ref.at[pl.ds(start, qkv_rows), pl.ds(0, depth)],
                )
            )
            for side in range(2):
                start = pl.multiple_of(g * qkv_rows + side * half, half)
                qkv_copies.append(
                    copy(
                        ref.at[pl.ds(at_extra, half), pl.ds(side * extra, extra)],
                        qkv_ref.at[pl.ds(start, half), pl.ds(depth, extra)],
                    )
                )

    square_ref[...] = hold_blocks(blocks, here, gain_ref, held)
    codes = lax.broadcasted_iota(jnp.int32, (table.shape[0], tokens_ref.shape[1]), 0)
    matches = (tokens_ref[...] == codes).astype(f32).astype(bf16)
    for made in table_copies:
        made.wait()
    looked = lax.dot_general(
        matches, table[...], (((0,), (0,)), ((), ())), preferred_element_type=f32
    )
    looked_ref[...] = looked.astype(bf16)
    projected_ref[...] = jnp.zeros_like(projected_ref)
    for (n, first), made, ref in zip(pieces, proj_copies, parts):
        count = min(ref.shape[0], proj_rows - first)
        rows = pl.ds(n * proj_rows + first, count)
        owner = jnp.bitwise_xor(group, n)
        book = owner // per_book
        start = pl.multiple_of((owner % per_book) * proj_rows + first, 128)
        late = is_late(jnp.bitwise_xor(here, book))
        made.wait()

        @pl.when(jnp.logical_not(late))
        def _():
            projected_ref[...] += jnp.dot(
                held[book, :, pl.ds(start, count)], proj[rows, :], preferred_element_type=f32
            )

        @pl.when(late)
        def _():
            slot = jnp.bitwise_xor(here, book) // 2 - 1
            later_ref[slot, pl.ds(start, count), :] = proj[rows, :]

    for made in qkv_copies:
        made.wait()


def project_early(tokens, gain, blocks, early, pieces, parts, sizes, wide):
    books = len(blocks)
    frames_here, width = blocks[0].shape
    depth = parts[0].shape[1]
    proj_rows, table_rows, qkv_rows = sizes
    groups = books * width // proj_rows
    vmem = pl.BlockSpec(memory_space=pltpu.VMEM)
    return pl.pallas_call(
        functools.partial(early_kernel, books, early, pieces, sizes),
        out_shape=[
            jax.ShapeDtypeStruct((frames_here, depth), f32),
            jax.ShapeDtypeStruct((frames_here, 1), f32),
            jax.ShapeDtypeStruct((books - len(early), width, depth), bf16),
            jax.ShapeDtypeStruct((frames_here, depth), bf16),
            jax.ShapeDtypeStruct((groups * qkv_rows, wide), bf16),
        ],
        in_specs=[vmem] * (2 + len(early))
        + [pl.BlockSpec(memory_space=pl.ANY)] * len(parts),
        out_specs=[vmem] * 5,
        scratch_shapes=[
            pltpu.VMEM((books, frames_here, width), bf16),
            pltpu.VMEM((books * width, depth), bf16),
            pltpu.VMEM((groups * table_rows, depth), bf16),
            pltpu.SemaphoreType.DMA((len(pieces) + 4 * groups,)),
        ],
        compiler_params=pltpu.CompilerParams(vmem_limit_bytes=45 * 2**20),
        name="early_products_and_lookup",
    )(tokens, gain, *[blocks[m] for m in early], *parts)


def late_kernel(books, late, gain_ref, *refs):
    blocks = dict(zip(late, refs))
    later_from, early_ref, square_ref, looked_ref, depth_gain_ref, qkv_from = refs[
        len(late) : len(late) + 6
    ]
    refs = refs[len(late) + 6 :]
    outs = refs[:books]
    held, packed, later_ref, qkv_ref, sems = refs[books:]
    later_copy = pltpu.make_async_copy(later_from, later_ref, sems.at[0])
    later_copy.start()
    qkv_copy = pltpu.make_async_copy(qkv_from, qkv_ref, sems.at[1])
    qkv_copy.start()
    here = lax.axis_index("book")
    frames_here, width = held.shape[1:]
    square = square_ref[...] + hold_blocks(blocks, here, gain_ref, held)
    projected = early_ref[...]
    later_copy.wait()
    for slot, m in enumerate(late):
        projected = projected + jnp.dot(
            held[jnp.bitwise_xor(here, m)], later_ref[slot], preferred_element_type=f32
        )
    projected = projected * lax.rsqrt(square / (books * width) + 1e-05)
    depth_in = (projected + looked_ref[...].astype(f32)).astype(bf16).astype(f32)
    moment = jnp.mean(depth_in * depth_in, axis=-1, keepdims=True)
    depth_normed = (depth_in * lax.rsqrt(moment + 1e-05) * depth_gain_ref[...].astype(f32)).astype(bf16)
    qkv_copy.wait()
    packed[...] = jnp.dot(depth_normed, qkv_ref[...], preferred_element_type=f32).astype(bf16)
    rows = frames_here // books
    for m in range(books):
        start = pl.multiple_of(jnp.bitwise_xor(here, m) * rows, rows)
        outs[m][...] = packed[pl.ds(start, rows), :]


def project_late(gain, blocks, late, later, projected, square, looked, depth_gain, qkv):
    books = len(blocks)
    frames_here, width = blocks[0].shape
    wide = qkv.shape[1]
    vmem = pl.BlockSpec(memory_space=pltpu.VMEM)
    return pl.pallas_call(
        functools.partial(late_kernel, books, late),
        out_shape=[jax.ShapeDtypeStruct((frames_here // books, wide), bf16)] * books,
        in_specs=[vmem] * (len(late) + 1)
        + [pl.BlockSpec(memory_space=pl.ANY)]
        + [vmem] * 4
        + [pl.BlockSpec(memory_space=pl.ANY)],
        out_specs=[vmem] * books,
        scratch_shapes=[
            pltpu.VMEM((books, frames_here, width), bf16),
            pltpu.VMEM((frames_here, wide), bf16),
            pltpu.VMEM(later.shape, bf16),
            pltpu.VMEM(qkv.shape, bf16),
            pltpu.SemaphoreType.DMA((2,)),
        ],
        compiler_params=pltpu.CompilerParams(vmem_limit_bytes=50 * 2**20),
        name="late_products_and_qkv",
    )(
        gain,
        *[blocks[m] for m in late],
        later,
        projected,
        square,
        looked,
        depth_gain,
        qkv,
    )


def attend_kernel(books, *refs):
    arrived = refs[:books]
    out_ref, inner = refs[books:]
    place = lax.axis_index("book")
    rows, wide = arrived[0].shape
    width = wide // 3
    for m in range(books):
        inner[jnp.bitwise_xor(place, m)] = arrived[m][...]
    head_of_row = lax.broadcasted_iota(jnp.int32, (width, width), 0) // HD
    head_of_column = lax.broadcasted_iota(jnp.int32, (width, width), 1) // HD
    same_head = (head_of_row == head_of_column).astype(f32).astype(bf16)
    keys_all = [inner[j, :, width : 2 * width].astype(f32) for j in range(books)]
    values_all = [inner[j, :, 2 * width :].astype(f32) for j in range(books)]
    pairs = [(k, j) for k in range(books) for j in range(k + 1)]
    queries = [inner[k, :, :width].astype(f32) * HD ** (-0.5) for k in range(books)]
    products = jnp.concatenate([queries[k] * keys_all[j] for k, j in pairs], axis=0)
    high = products.astype(bf16)
    low = (products - high.astype(f32)).astype(bf16)
    both = jnp.dot(
        jnp.concatenate([high, low], axis=0), same_head, preferred_element_type=f32
    )
    every = both[: len(pairs) * rows] + both[len(pairs) * rows :]
    contexts = []
    for k in range(books):
        first = pairs.index((k, 0))
        scores = [every[(first + j) * rows : (first + j + 1) * rows] for j in range(k + 1)]
        peak = functools.reduce(jnp.maximum, scores)
        expo = [jnp.exp(score - peak) for score in scores]
        share = 1.0 / functools.reduce(jnp.add, expo)
        context = 0.0
        for j in range(k + 1):
            probability = (expo[j] * share).astype(bf16).astype(f32)
            context = context + probability * values_all[j]
        contexts.append(context)
    out_ref[...] = jnp.stack(contexts, axis=1).astype(bf16)


def attend(arrived):
    books = len(arrived)
    rows, wide = arrived[0].shape
    vmem = pl.BlockSpec(memory_space=pltpu.VMEM)
    return pl.pallas_call(
        functools.partial(attend_kernel, books),
        out_shape=jax.ShapeDtypeStruct((rows, books, wide // 3), bf16),
        in_specs=[vmem] * books,
        out_specs=vmem,
        scratch_shapes=[pltpu.VMEM((books, rows, wide), bf16)],
        compiler_params=pltpu.CompilerParams(vmem_limit_bytes=16 * 2**20),
        name="attend_books",
    )(*arrived)


def swap(value, axis, distance):
    return lax.ppermute(value, axis, [(i, i ^ distance) for i in range(lax.axis_size(axis))])


def after(value, *others):
    return lax.optimization_barrier((value, *others))[0]


def bits_of(number):
    return [1 << place for place in range(number.bit_length()) if number >> place & 1]


def per_device(
    gate_pre,
    up_pre,
    down_weight,
    residual,
    out_gain,
    in_proj,
    embedding,
    token_ids,
    depth_gain,
    qkv_weight,
):
    books = lax.axis_size("book")
    groups = lax.axis_size("frames")
    here = lax.axis_index("book").astype(jnp.int32)
    width = residual.shape[1]
    proj_rows = in_proj.shape[1]
    gain = out_gain[None]

    hidden, first = first_products(gate_pre, up_pre, down_weight, width)

    def share(m, *others):
        factor = after(hidden, *others) if others else hidden
        if m == 0:
            total = 0.0
            each = factor.shape[1] // 4
            for step in range(4):
                block = lax.dynamic_slice(
                    down_weight, (step * each, lax.axis_index("book") * width), (each, width)
                )
                part = lax.slice_in_dim(factor, step * each, (step + 1) * each, axis=1)
                total = total + jnp.dot(part, block, preferred_element_type=f32)
                total = lax.optimization_barrier(total)
            return total
        return share_products(factor, down_weight, width, m)

    rows = pack(*after((in_proj[0], embedding[0], qkv_weight[0]), first))
    parts = {0: [(0, rows)]}
    near = [n for n in range(2, groups, 2) if len(bits_of(n)) == 1]
    for n in near:
        parts[n] = [(0, swap(rows, "frames", n))]

    sums = {books - 1: first}
    parts[1] = [(0, swap(rows, "frames", 1))]
    sums[books - 2] = lax.optimization_barrier(share(books - 2, rows))
    for n in range(books - 3, 0, -1):
        sums[n] = lax.optimization_barrier(share(n, rows))
    came = swap(sums.pop(books - 1).astype(bf16), "book", 1)
    came = after(came, *[sums[n] for n in range(1, books - 1)])
    onward = (sums.pop(books - 2) + came.astype(f32)).astype(bf16)
    far_came = swap(onward, "book", 2)
    last = lax.optimization_barrier(share(0, came, parts[1][0][1]))
    sums[0] = last + residual.astype(f32)
    for m in range(books - 3, 0, -2):
        near_came = swap(after(sums.pop(m).astype(bf16), onward), "book", 1)
        sums[m ^ 1] = sums[m ^ 1] + near_came.astype(f32)
    sums[(books - 2) ^ 2] = sums[(books - 2) ^ 2] + far_came.astype(f32)
    distance = 2
    while distance < books:
        for m in range(books - distance, 0, -2 * distance):
            if m in sums:
                came = swap(sums.pop(m).astype(bf16), "book", distance)
                sums[m ^ distance] = sums[m ^ distance] + came.astype(f32)
        distance *= 2

    blocks = {0: sums[0].astype(bf16)}

    arrived = after([parts[n][0][1] for n in near], blocks[0])
    for n, value in zip(near, arrived):
        parts[n] = [(0, value)]
    cut = rows.shape[0] // 2 // 128 * 128
    for n in range(2, groups, 2):
        sides = bits_of(n)
        if n in near:
            continue
        if len(sides) == 2 and 0 < cut < proj_rows:
            upper, lower = cut_rows(parts[n ^ sides[0]][0][1], parts[n ^ sides[1]][0][1], cut)
            upper = swap(upper, "frames", sides[0])
            lower = swap(lower, "frames", sides[1])
            parts[n] = [(0, upper), (cut, lower)]
        else:
            parts[n] = [(0, swap(rows, "frames", n))]
    for n in range(2, groups, 2):
        parts[n + 1] = [(first, swap(value, "frames", 1)) for first, value in parts[n]]

    near_there = [parts[n + 1][0][1] for n in near]
    distance = books // 2
    while distance:
        for m in sorted(blocks):
            going = blocks[m]
            if m:
                going = after(going, blocks[distance])
            elif distance == 1:
                going = after(going, *near_there)
            blocks[m ^ distance] = swap(going, "book", distance)
        distance //= 2

    pieces = [(n, first) for n in range(groups) for first, _ in parts[n]]
    arrived = [value for n in range(groups) for _, value in parts[n]]
    sizes = proj_rows, embedding.shape[1], qkv_weight.shape[1]
    early = [m for m in range(books) if not is_late(m)]
    late = [m for m in range(books) if is_late(m)]
    projected, square, later, looked, qkv = project_early(
        token_ids.reshape(1, -1), gain, blocks, early, pieces, arrived, sizes, qkv_weight.shape[2]
    )
    packed = project_late(
        gain, blocks, late, later, projected, square, looked, depth_gain, qkv
    )
    far = {m: swap(packed[m], "book", m) for m in range(books - 1, 0, -1)}
    return attend([packed[0]] + [far[m] for m in range(1, books)])


def solution(mesh):
    in_specs = (
        P("frames", "book"),
        P("frames", "book"),
        P("book", None),
        P("frames", "book"),
        P(),
        P("book", "frames", None),
        P("book", "frames", None),
        P("frames", "book"),
        P("book", None),
        P("book", "frames", None),
    )
    out_specs = P(("frames", "book"), None, None)
    return jax.shard_map(
        per_device, mesh=mesh, in_specs=in_specs, out_specs=out_specs, check_vma=False
    )
```
